32 devices in a mesh: row: 4 (over y, core), col: 8 (over z, x).
Axes of the slice: x: 2, y: 2, z: 4, core: 2. Of those that a mesh axis runs over, the one named last changes fastest.
Arguments:
- features: bfloat16 [32768, 128], P('col', 'row'), may hold values from -6 to 6
- block_codes: int32 [4, 3072], P('row', 'col'), may hold values from 0 to 8191
- block_count: int32 [4, 8], P('row', 'col'), may hold values from 1 to 384, as said below
- block_values: bfloat16 [4, 3072, 4096], P('row', 'col'), may hold values from -0.119628906 to 0.119628906
- weight: bfloat16 [128, 256], replicated, may hold values from -0.5 to 0.5
- bias: float32 [256], replicated, may hold values from -3 to 3
Outputs:
- activated: bfloat16 [32768, 256], P(('row', 'col'))
The draws below stay inside these ranges and needn't reach their ends.
Inputs may be any that keep to these rules, and one draw needn't show every extreme that they name: `block_count`: every tile's count is at most 384; some tile holds exactly 384 in every draw; counts are skewed, the busiest tile about three times the mean. `block_codes`: A code c names local row block c // 64 and local column block c % 64.
All inputs are finite; a program needn't handle non-finite values.
Results may differ from the reference program's by a relative error of at most 0.0045.
Values may be sent and summed in bfloat16 or wider, within the bound.
No kernel may reach another device: no remote copies, remote signals or barrier semaphores. Data moves between devices by JAX's collectives and lax.ppermute only.
A program may use at most 128 MiB of HBM per device.

```python
import jax
import jax.numpy as jnp
from jax import lax

F = 128
H = 256
BLK = 64
MAXB = 384
TILE_RB = 128
TILE_CB = 64
NODES = 32768
N_ROW = 4
N_COL = 8


def draw_block_count(key, part):
    first_key, second_key = jax.random.split(jax.random.fold_in(key, 17))
    base = jax.random.randint(first_key, (N_ROW, N_COL), 1, MAXB + 1)
    skewed = jnp.maximum(base * base // MAXB, 1)
    chosen = jax.random.randint(second_key, (), 0, N_ROW * N_COL)
    flat = skewed.reshape(-1)
    flat = jnp.where(jnp.arange(N_ROW * N_COL) == chosen, MAXB, flat)
    return flat.reshape(N_ROW, N_COL).astype(jnp.int32)


def set_ends(array, key, smallest, top_value):
    longest = array.shape.index(max(array.shape))
    spots = []
    for shift in (0, 1):
        where = [jax.random.randint(jax.random.fold_in(key, axis), (), 0, length) for axis, length in enumerate(array.shape)]
        where[longest] = (where[longest] + shift) % array.shape[longest]
        spots.append(tuple(where))
    return array.at[spots[0]].set(smallest).at[spots[1]].set(top_value)


def steps_of(own_key, dims, shards, low, largest):
    gain = 1.0
    for dim, parts in shards:
        heights = jax.random.uniform(jax.random.fold_in(jax.random.fold_in(own_key, 6), dim), (parts,), jnp.float32, low / len(shards), largest / len(shards))
        gain = gain * jnp.repeat(jnp.exp(heights), dims[dim] // parts).reshape((-1,) + (1,) * (len(dims) - 1 - dim))
    return gain


def gaussian(rng, extent, deviation, most, shards=(), held_as=jnp.bfloat16):
    result = jax.random.normal(rng, extent, jnp.float32) * deviation
    if len(shards) > 0:
        result = steps_of(rng, extent, shards, -0.22, 0.18) * result
    return jnp.clip(result, min=-most, max=most).astype(held_as)


def setup_inputs(seed: int = 0) -> dict:
    key_list = jax.random.split(jax.random.key(seed), 7)
    return {
        "features": gaussian(key_list[0], (NODES, F), 1.0, 6.0, ((0, 8), (1, 4))),
        "block_codes": set_ends(jax.random.randint(key_list[1], (N_ROW, N_COL * MAXB), 0, TILE_RB * TILE_CB), jax.random.fold_in(key_list[1], 1), 0, (TILE_RB * TILE_CB) - 1).astype(jnp.int32),
        "block_count": draw_block_count(jax.random.fold_in(key_list[6], 71), 0),
        "block_values": gaussian(key_list[3], (N_ROW, N_COL * MAXB, BLK * BLK), 0.02, 0.119628906, ((0, 4), (1, 8))),
        "weight": gaussian(key_list[4], (F, H), F ** -0.5, 0.5),
        "bias": gaussian(key_list[5], (H,), 0.5, 3.0, (), jnp.float32),
    }


def tile_partial(tile_codes, tile_count, tile_values, column_slab):
    row_block = tile_codes // TILE_CB
    col_block = tile_codes % TILE_CB
    is_live = jnp.arange(MAXB, dtype=jnp.int32) < tile_count
    picked = column_slab[col_block].astype(jnp.float32)
    blocks = tile_values.reshape(MAXB, BLK, BLK).astype(jnp.float32)
    products = jnp.einsum("bij,bjf->bif", blocks, picked)
    products = jnp.where(is_live[:, None, None], products, jnp.zeros_like(products))
    return jax.ops.segment_sum(products, row_block, num_segments=TILE_RB)


def reference(features, block_codes, block_count, block_values, weight, bias):
    slabs = features.reshape(N_COL, TILE_CB, BLK, F)

    def grid_row(index_row):
        row_codes = block_codes[index_row]
        row_values = block_values[index_row]
        row_counts = block_count[index_row]

        def add_tile(total, index_col):
            first_slot = (index_col * MAXB).astype(jnp.int32)
            tile_codes = lax.dynamic_slice_in_dim(row_codes, first_slot, MAXB)
            tile_values = lax.dynamic_slice_in_dim(row_values, first_slot, MAXB, 0)
            return total + tile_partial(tile_codes, row_counts[index_col], tile_values, slabs[index_col]), None

        total, _ = lax.scan(add_tile, jnp.zeros((TILE_RB, BLK, F), jnp.float32), jnp.arange(N_COL, dtype=jnp.int32))
        return total

    sums = lax.map(grid_row, jnp.arange(N_ROW, dtype=jnp.int32))
    aggregated = sums.reshape(NODES, F).astype(jnp.bfloat16)
    hidden = jnp.dot(aggregated, weight, preferred_element_type=jnp.float32) + bias
    return jnp.maximum(hidden, 0.0).astype(jnp.bfloat16)
```

```python
import functools

import jax
import jax.numpy as jnp
from jax import lax
from jax.experimental import pallas as pl
from jax.experimental.pallas import tpu as pltpu
from jax.sharding import PartitionSpec as P

BLK = 64
PAIR = BLK // 2
LANES = 2 * BLK
GROUP = 16
UNROLL = 8


def relayout_kernel(values_ref, out_ref, scratch):
    for p in range(PAIR):
        scratch[p * GROUP : (p + 1) * GROUP, :] = values_ref[:, p * LANES : (p + 1) * LANES].astype(jnp.float32)
    for s in range(GROUP):
        rows = scratch[pl.ds(s, PAIR, stride=GROUP), :]
        out_ref[s * PAIR : (s + 1) * PAIR, :] = rows.astype(out_ref.dtype)


def relayout(values):
    slots = values.shape[0]
    return pl.pallas_call(
        relayout_kernel,
        grid=(slots // GROUP,),
        in_specs=[pl.BlockSpec((GROUP, BLK * BLK), lambda i: (i, 0))],
        out_specs=pl.BlockSpec((GROUP * PAIR, LANES), lambda i: (i, 0)),
        out_shape=jax.ShapeDtypeStruct((slots * PAIR, LANES), values.dtype),
        scratch_shapes=[pltpu.VMEM((GROUP * PAIR, LANES), jnp.float32)],
        cost_estimate=pl.CostEstimate(flops=0, bytes_accessed=4 * slots * BLK * BLK, transcendentals=0),
        name="relayout",
    )(values)


def product_kernel(count_ref, source_ref, target_ref, blocks_ref, ft_ref, keep_ref, send_ref, table, acc):
    lane = lax.broadcasted_iota(jnp.int32, (BLK, LANES), 1)
    low = lane < BLK

    def build(q, carry):
        x = ft_ref[:, pl.ds(pl.multiple_of(q * LANES, LANES), LANES)].astype(jnp.float32)
        both = jnp.concatenate([x, x], axis=0).T
        base = pl.multiple_of(q * 2 * LANES, 2 * LANES)
        zero = jnp.zeros((BLK, LANES), jnp.float32)
        for h in range(2):
            part = both[h * BLK : (h + 1) * BLK, :]
            full = jnp.concatenate([jnp.where(low, part, zero), jnp.where(low, zero, part)], axis=0)
            table[pl.ds(base + h * LANES, LANES), :] = full.astype(table.dtype)
        return carry

    lax.fori_loop(0, ft_ref.shape[1] // LANES, build, 0)
    acc[...] = jnp.zeros_like(acc)
    groups = (count_ref[0, 0] + (UNROLL - 1)) // UNROLL

    def step(g, carry):
        products = []
        for u in range(UNROLL):
            s = g * UNROLL + u
            block = blocks_ref[pl.ds(pl.multiple_of(s * PAIR, PAIR), PAIR), :]
            right = table[pl.ds(pl.multiple_of(source_ref[0, s], LANES), LANES), :]
            products.append(jnp.dot(block, right, preferred_element_type=jnp.float32))
        for u in range(UNROLL):
            rows = pl.ds(pl.multiple_of(target_ref[0, g * UNROLL + u], PAIR), PAIR)
            acc[rows, :] = acc[rows, :] + products[u]
        return carry

    lax.fori_loop(0, groups, step, 0)
    half = keep_ref.shape[0]
    keep_ref[...] = acc[:half, :]
    send_ref[...] = acc[half : 2 * half, :].astype(send_ref.dtype)


def product(count, source, target, blocks, ft, row_total):
    nodes = ft.shape[1]
    half = row_total // 2 * PAIR
    smem = pl.BlockSpec(memory_space=pltpu.SMEM)
    vmem = pl.BlockSpec(memory_space=pltpu.VMEM)
    return pl.pallas_call(
        product_kernel,
        in_specs=[smem, smem, smem, vmem, vmem],
        out_specs=(vmem, vmem),
        out_shape=(
            jax.ShapeDtypeStruct((half, LANES), jnp.float32),
            jax.ShapeDtypeStruct((half, LANES), jnp.bfloat16),
        ),
        scratch_shapes=[
            pltpu.VMEM((nodes * 2, LANES), jnp.bfloat16),
            pltpu.VMEM(((row_total + 1) * PAIR, LANES), jnp.float32),
        ],
        compiler_params=pltpu.CompilerParams(vmem_limit_bytes=32 * 1024 * 1024),
        cost_estimate=pl.CostEstimate(
            flops=2 * blocks.shape[0] * LANES * LANES, bytes_accessed=6 * 1024 * 1024, transcendentals=0
        ),
        name="product",
    )(count, source, target, blocks, ft)


def layer_kernel(keep0, got0, keep1, got1, even_ref, odd_ref, bias_ref, out_ref, left, right):
    first = (keep0[...] + got0[...].astype(jnp.float32)).astype(jnp.bfloat16)
    second = (keep1[...] + got1[...].astype(jnp.float32)).astype(jnp.bfloat16)
    both = jnp.concatenate([first, second], axis=1)
    rows = both.shape[0]
    for h, w_ref in enumerate((even_ref, odd_ref)):
        hidden = jnp.dot(both, w_ref[...], preferred_element_type=jnp.float32) + bias_ref[...]
        hidden = jnp.maximum(hidden, 0.0)
        left[pl.ds(h, rows, stride=2), :] = hidden[:, :LANES]
        right[pl.ds(h, rows, stride=2), :] = hidden[:, LANES:]
    out_ref[:, :LANES] = left[...].astype(out_ref.dtype)
    out_ref[:, LANES:] = right[...].astype(out_ref.dtype)


def layer(keep0, got0, keep1, got1, even, odd, bias):
    rows = keep0.shape[0]
    return pl.pallas_call(
        layer_kernel,
        out_shape=jax.ShapeDtypeStruct((2 * rows, even.shape[1]), jnp.bfloat16),
        scratch_shapes=[pltpu.VMEM((2 * rows, LANES), jnp.float32)] * 2,
        name="layer",
    )(keep0, got0, keep1, got1, even, odd, bias)


def bits_of(size):
    return range(size.bit_length() - 1)


def exchange(x, axis, size, bit):
    return lax.ppermute(x, axis, [(i, i ^ (1 << bit)) for i in range(size)])


def shards(n_row, n_col, features, block_codes, block_count, block_values, weight, bias):
    r, c = lax.axis_index("row"), lax.axis_index("col")
    top = n_row.bit_length() - 2
    low_bits, col_bits = list(range(top)), list(bits_of(n_col))

    def spread(piece):
        for bit in low_bits:
            piece = jnp.concatenate([piece, exchange(piece, "row", n_row, bit)], axis=0)
        return piece

    mine = features.T
    halves = [spread(mine), spread(exchange(mine, "row", n_row, top))]

    col_blocks = features.shape[0] // BLK
    row_total = col_blocks * n_col // n_row
    per = row_total // n_col
    slots = block_codes.shape[1]
    row_block, col_block = block_codes // col_blocks, block_codes % col_blocks
    owner = (row_block // per) ^ c
    live = lax.broadcasted_iota(jnp.int32, (1, slots), 1) < block_count
    source = col_block * LANES
    orders = [col_bits[1:] + col_bits[:1], col_bits]
    targets = []
    for order in orders:
        place = sum(((owner >> bit) & 1) << (len(order) - 1 - k) for k, bit in enumerate(order))
        targets.append(jnp.where(live, place * per + row_block % per, row_total) * PAIR)

    blocks = relayout(block_values[0])
    sums = [product(block_count, source, t, blocks, ft, row_total) for t, ft in zip(targets, halves)]

    for k in range(len(col_bits)):
        for i, order in enumerate(orders):
            keep, send = sums[i]
            got = exchange(send, "col", n_col, order[k])
            if k < len(col_bits) - 1:
                half = keep.shape[0] // 2
                total = keep + got.astype(jnp.float32)
                sums[i] = (total[:half], total[half:].astype(jnp.bfloat16))
            else:
                sums[i] = (keep, got)

    pieces = weight.reshape(n_row, -1, weight.shape[1])[jnp.arange(n_row) ^ r]
    pieces = pieces.reshape(2, BLK, weight.shape[1])
    zero = jnp.zeros_like(pieces)
    even = jnp.concatenate([pieces, zero], axis=1).reshape(2 * LANES, -1)
    odd = jnp.concatenate([zero, pieces], axis=1).reshape(2 * LANES, -1)
    return layer(*sums[0], *sums[1], even, odd, bias[None, :])


def solution(mesh):
    in_specs = (P("col", "row"), P("row", "col"), P("row", "col"), P("row", "col", None), P(), P())
    out_specs = P(("row", "col"), None)
    body = functools.partial(shards, mesh.shape["row"], mesh.shape["col"])
    return jax.shard_map(body, mesh=mesh, in_specs=in_specs, out_specs=out_specs, check_vma=False)
```

```python
import functools

import jax
import jax.numpy as jnp
from jax import lax
from jax.experimental import pallas as pl
from jax.experimental.pallas import tpu as pltpu
from jax.sharding import PartitionSpec as P

BLK = 64
PAIR = BLK // 2
LANES = 2 * BLK
GROUP = 16
STEPS = 4
UNROLL = 4
SMEM = pl.BlockSpec(memory_space=pltpu.SMEM)
VMEM = pl.BlockSpec(memory_space=pltpu.VMEM)


def relayout_kernel(values_ref, out_ref, scratch):
    def one(g, carry):
        slots = pl.ds(pl.multiple_of(g * GROUP, GROUP), GROUP)
        base = pl.multiple_of(g * (GROUP * PAIR), GROUP * PAIR)
        for p in range(PAIR):
            scratch[pl.ds(base + p * GROUP, GROUP), :] = values_ref[slots, p * LANES : (p + 1) * LANES].astype(jnp.float32)
        for s in range(GROUP):
            rows = scratch[pl.ds(base + s, PAIR, stride=GROUP), :]
            out_ref[pl.ds(base + s * PAIR, PAIR), :] = rows.astype(out_ref.dtype)
        return carry

    lax.fori_loop(0, values_ref.shape[0] // GROUP, one, 0, unroll=2)


def relayout(values):
    slots = values.shape[0]
    step = slots // STEPS
    return pl.pallas_call(
        relayout_kernel,
        grid=(STEPS,),
        in_specs=[pl.BlockSpec((step, BLK * BLK), lambda i: (i, 0))],
        out_specs=pl.BlockSpec((step * PAIR, LANES), lambda i: (i, 0)),
        out_shape=jax.ShapeDtypeStruct((slots * PAIR, LANES), values.dtype),
        scratch_shapes=[pltpu.VMEM((step * PAIR, LANES), jnp.float32)],
        cost_estimate=pl.CostEstimate(flops=0, bytes_accessed=4 * slots * BLK * BLK, transcendentals=0),
        compiler_params=pltpu.CompilerParams(vmem_limit_bytes=16 * 1024 * 1024),
        name="relayout",
    )(values)


def table_kernel(*refs):
    parts, table = refs[:-1], refs[-1]

    def build(q, carry):
        at = pl.ds(pl.multiple_of(q * LANES, LANES), LANES)
        x = jnp.concatenate([part[:, at].astype(jnp.float32) for part in parts], axis=0)
        table[at, :] = x.T.astype(table.dtype)
        return carry

    lax.fori_loop(0, table.shape[0] // LANES, build, 0, unroll=4)


def make_table(parts):
    nodes = parts[0].shape[1]
    return pl.pallas_call(
        table_kernel,
        in_specs=[VMEM] * len(parts),
        out_specs=VMEM,
        out_shape=jax.ShapeDtypeStruct((nodes, LANES), jnp.bfloat16),
        compiler_params=pltpu.CompilerParams(vmem_limit_bytes=8 * 1024 * 1024),
        name="table",
    )(*parts)


def product_kernel(trash, start_ref, end_ref, order_ref, source_ref, target_ref, blocks_ref, table_ref, *outs):
    acc = outs[-1]
    start, end = start_ref[0], end_ref[0]
    low = lax.broadcasted_iota(jnp.int32, (PAIR, LANES), 1) < BLK
    acc[...] = jnp.zeros_like(acc)

    def multiply(first):
        products = []
        for u in range(UNROLL):
            s = order_ref[first + u]
            block = blocks_ref[pl.ds(pl.multiple_of(s * PAIR, PAIR), PAIR), :]
            zero = jnp.zeros_like(block)
            left = jnp.concatenate([jnp.where(low, block, zero), jnp.where(low, zero, block)], axis=0)
            right = table_ref[pl.ds(pl.multiple_of(source_ref[s] * BLK, BLK), BLK), :]
            right = jnp.concatenate([right, right], axis=0)
            products.append(jnp.dot(left, right, preferred_element_type=jnp.float32))
        return tuple(products)

    def add(first, products):
        for u in range(UNROLL):
            place = jnp.where(first + u < end, target_ref[order_ref[first + u]], trash)
            rows = pl.ds(pl.multiple_of(place * BLK, BLK), BLK)
            acc[rows, :] = acc[rows, :] + products[u]

    def step(g, products):
        first = start + g * UNROLL
        later = multiply(first)
        add(first - UNROLL, products)
        return later

    groups = (end - start + (UNROLL - 1)) // UNROLL

    @pl.when(groups > 0)
    def _():
        last = lax.fori_loop(1, groups, step, multiply(start))
        add(start + (groups - 1) * UNROLL, last)

    if len(outs) > 1:
        outs[0][...] = acc[: trash * BLK, :].astype(outs[0].dtype)


def product(start, end, order, source, target, blocks, table, trash, sent):
    rows = (trash + 1) * BLK
    full = jax.ShapeDtypeStruct((rows, LANES), jnp.float32)
    out = jax.ShapeDtypeStruct((trash * BLK, LANES), jnp.bfloat16) if sent else full
    return pl.pallas_call(
        functools.partial(product_kernel, trash),
        in_specs=[SMEM] * 5 + [VMEM] * 2,
        out_specs=VMEM,
        out_shape=out,
        scratch_shapes=[pltpu.VMEM(full.shape, full.dtype)] if sent else [],
        compiler_params=pltpu.CompilerParams(vmem_limit_bytes=16 * 1024 * 1024),
        cost_estimate=pl.CostEstimate(flops=2 * rows * LANES * LANES * 3, bytes_accessed=1024 * 1024, transcendentals=0),
        name="product_send" if sent else "product_keep",
    )(start, end, order, source, target, blocks, table)


def add_kernel(keep_ref, got_ref, next_ref, send_ref):
    half = next_ref.shape[0]
    next_ref[...] = keep_ref[:half, :] + got_ref[:half, :].astype(jnp.float32)
    send_ref[...] = (keep_ref[half:, :] + got_ref[half:, :].astype(jnp.float32)).astype(send_ref.dtype)


def add_halves(keep, which, got):
    rows = got.shape[0]
    part = pl.BlockSpec((rows, LANES), lambda i: (which, 0))
    whole = lambda n: pl.BlockSpec((n, LANES), lambda i: (0, 0))
    return pl.pallas_call(
        add_kernel,
        grid=(1,),
        in_specs=[part, whole(rows)],
        out_specs=(whole(rows // 2), whole(rows // 2)),
        out_shape=(
            jax.ShapeDtypeStruct((rows // 2, LANES), jnp.float32),
            jax.ShapeDtypeStruct((rows // 2, LANES), jnp.bfloat16),
        ),
        compiler_params=pltpu.CompilerParams(vmem_limit_bytes=16 * 1024 * 1024),
        cost_estimate=pl.CostEstimate(flops=rows * LANES, bytes_accessed=rows * LANES * 6, transcendentals=0),
        name="add",
    )(keep, got)


def layer_kernel(keep0, got0, keep1, got1, weight_ref, bias_ref, out_ref, left, right):
    base = 0
    for keep, got in ((keep0, got0), (keep1, got1)):
        rows = got.shape[0]
        aggregated = (keep[...] + got[...].astype(jnp.float32)).astype(jnp.bfloat16)
        hidden = jnp.dot(aggregated, weight_ref[...], preferred_element_type=jnp.float32) + bias_ref[...]
        hidden = jnp.maximum(hidden, 0.0)
        for at in range(0, rows, PAIR):
            spot = pl.ds(base + at // BLK * BLK + at % BLK // PAIR, PAIR, stride=2)
            left[spot, :] = hidden[at : at + PAIR, :LANES]
            right[spot, :] = hidden[at : at + PAIR, LANES:]
        base += rows
    out_ref[:, :LANES] = left[...].astype(out_ref.dtype)
    out_ref[:, LANES:] = right[...].astype(out_ref.dtype)


def layer(keep0, got0, keep1, got1, weight, bias):
    rows = got0.shape[0] + got1.shape[0]
    return pl.pallas_call(
        layer_kernel,
        out_shape=jax.ShapeDtypeStruct((rows, weight.shape[1]), jnp.bfloat16),
        scratch_shapes=[pltpu.VMEM((rows, LANES), jnp.float32)] * 2,
        name="layer",
    )(keep0, got0, keep1, got1, weight, bias)


def exchange(x, axis, size, bit):
    return lax.ppermute(x, axis, [(i, i ^ (1 << bit)) for i in range(size)])


def shards(n_row, n_col, features, block_codes, block_count, block_values, weight, bias):
    r, c = lax.axis_index("row"), lax.axis_index("col")
    top = n_row.bit_length() - 2
    col_bits = list(range(n_col.bit_length() - 1))

    mine = features.T
    parts = [mine, exchange(mine, "row", n_row, top)]
    for bit in range(top):
        parts = [[p, exchange(p, "row", n_row, bit)] for p in parts]
        parts = [pair[k] for k in range(2) for pair in parts]
    index = [0, 1 << top]
    for bit in range(top):
        index = index + [i ^ (1 << bit) for i in index]

    col_blocks = features.shape[0] // BLK
    row_total = col_blocks * n_col // n_row
    per = row_total // n_col
    small, half = per // 2, row_total // 4
    slots = block_codes.shape[1]
    row_block, col_block = block_codes[0] // col_blocks, block_codes[0] % col_blocks
    owner, sub = (row_block // per) ^ c, row_block % per
    number = jnp.arange(slots, dtype=jnp.int32)
    live = number < block_count[0, 0]
    orders = [col_bits[1:] + col_bits[:1], col_bits]
    places = []
    for order in orders:
        places.append(sum(((owner >> bit) & 1) << (len(order) - 1 - k) for k, bit in enumerate(order)))
    chunk = sub // small
    place = jnp.where(chunk == 0, places[0], places[1]) * small + sub % small
    keep = place < half
    target = jnp.where(keep, chunk * half + place, place - half)
    part = jnp.where(live, jnp.where(keep, 2, chunk), 3)
    key = part * slots + number
    rank = jnp.sum((key[None, :] < key[:, None]).astype(jnp.int32), axis=1)
    order = jnp.sum(jnp.where(rank[None, :] == number[:, None], number[None, :], 0), axis=1)
    ends = [jnp.sum((part <= k).astype(jnp.int32)).reshape(1) for k in range(3)]
    starts = [jnp.zeros_like(ends[0])] + ends[:2]
    order = jnp.concatenate([order, jnp.zeros((UNROLL,), jnp.int32)])

    blocks = relayout(block_values[0])
    table = make_table(parts)
    mul = lambda k, trash, sent: product(starts[k], ends[k], order, col_block, target, blocks, table, trash, sent)
    sends = [mul(0, half, True), mul(1, half, True)]
    kept = mul(2, 2 * half, False)

    keeps = [(kept, 0), (kept, 1)]
    for k in range(len(col_bits)):
        for i in range(2):
            got = exchange(sends[i], "col", n_col, orders[i][k])
            if k < len(col_bits) - 1:
                total, sends[i] = add_halves(*keeps[i], got)
                keeps[i] = (total, 0)
            else:
                keeps[i], sends[i] = keeps[i][0], got

    pieces = weight.reshape(n_row, -1, weight.shape[1])[jnp.array(index) ^ r]
    return layer(keeps[0], sends[0], keeps[1], sends[1], pieces.reshape(weight.shape), bias[None, :])


def solution(mesh):
    in_specs = (P("col", "row"), P("row", "col"), P("row", "col"), P("row", "col", None), P(), P())
    out_specs = P(("row", "col"), None)
    body = functools.partial(shards, mesh.shape["row"], mesh.shape["col"])
    return jax.shard_map(body, mesh=mesh, in_specs=in_specs, out_specs=out_specs, check_vma=False)
```

```python
import functools

import jax
import jax.numpy as jnp
from jax import lax
from jax.experimental import pallas as pl
from jax.experimental.pallas import tpu as pltpu
from jax.sharding import PartitionSpec as P

BLK = 64
PAIR = BLK // 2
LANES = 2 * BLK
GROUP = 16
STEPS = 4
UNROLL = 4
SMEM = pl.BlockSpec(memory_space=pltpu.SMEM)
VMEM = pl.BlockSpec(memory_space=pltpu.VMEM)


def relayout_kernel(values_hbm, out_ref, held, scratch, arrived):
    step = values_hbm.shape[0] // STEPS
    copies = []
    for k in range(STEPS):
        rows = pl.ds(k * step, step)
        copies.append(pltpu.make_async_copy(values_hbm.at[rows], held.at[rows], arrived.at[k]))
        copies[k].start()

    def one(g, carry):
        slots = pl.ds(pl.multiple_of(g * GROUP, GROUP), GROUP)
        base = pl.multiple_of(g * (GROUP * PAIR), GROUP * PAIR)
        for p in range(PAIR):
            scratch[pl.ds(base + p * GROUP, GROUP), :] = held[slots, p * LANES : (p + 1) * LANES].astype(jnp.float32)
        for s in range(GROUP):
            rows = scratch[pl.ds(base + s, PAIR, stride=GROUP), :]
            out_ref[pl.ds(base + s * PAIR, PAIR), :] = rows.astype(out_ref.dtype)
        return carry

    groups = step // GROUP
    for k in range(STEPS):
        copies[k].wait()
        lax.fori_loop(k * groups, (k + 1) * groups, one, 0, unroll=2)


def relayout(values):
    slots = values.shape[0]
    return pl.pallas_call(
        relayout_kernel,
        in_specs=[pl.BlockSpec(memory_space=pltpu.HBM)],
        out_specs=VMEM,
        out_shape=jax.ShapeDtypeStruct((slots * PAIR, LANES), values.dtype),
        scratch_shapes=[
            pltpu.VMEM(values.shape, values.dtype),
            pltpu.VMEM((slots * PAIR, LANES), jnp.float32),
            pltpu.SemaphoreType.DMA((STEPS,)),
        ],
        cost_estimate=pl.CostEstimate(flops=0, bytes_accessed=4 * slots * BLK * BLK, transcendentals=0),
        compiler_params=pltpu.CompilerParams(vmem_limit_bytes=20 * 1024 * 1024),
        name="relayout",
    )(values)


def table_kernel(*refs):
    parts, table = refs[:-1], refs[-1]

    def build(q, carry):
        at = pl.ds(pl.multiple_of(q * LANES, LANES), LANES)
        x = jnp.concatenate([part[:, at].astype(jnp.float32) for part in parts], axis=0)
        table[at, :] = x.T.astype(table.dtype)
        return carry

    lax.fori_loop(0, table.shape[0] // LANES, build, 0, unroll=4)


def make_table(parts):
    nodes = parts[0].shape[1]
    return pl.pallas_call(
        table_kernel,
        in_specs=[VMEM] * len(parts),
        out_specs=VMEM,
        out_shape=jax.ShapeDtypeStruct((nodes, LANES), jnp.bfloat16),
        compiler_params=pltpu.CompilerParams(vmem_limit_bytes=8 * 1024 * 1024),
        name="table",
    )(*parts)


def product_kernel(trash, first_word, words_ref, blocks_ref, table_ref, *outs):
    acc = outs[-1]
    start, end = words_ref[first_word], words_ref[first_word + 1]
    acc[...] = jnp.zeros_like(acc)

    def multiply(first):
        products = []
        for u in range(UNROLL):
            word = words_ref[first + u]
            block = blocks_ref[pl.ds(pl.multiple_of((word >> 16) * PAIR, PAIR), PAIR), :]
            part = table_ref[pl.ds(pl.multiple_of(((word >> 8) & 255) * BLK, BLK), BLK), :]
            zero = jnp.zeros_like(part)
            right = jnp.concatenate([jnp.concatenate([part, zero], axis=1), jnp.concatenate([zero, part], axis=1)], axis=0)
            products.append(jnp.dot(block, right, preferred_element_type=jnp.float32))
        return tuple(products)

    def add(first, products):
        for u in range(UNROLL):
            place = jnp.where(first + u < end, words_ref[first + u] & 255, trash)
            rows = pl.ds(pl.multiple_of(place * PAIR, PAIR), PAIR)
            acc[rows, :] = acc[rows, :] + products[u]

    def step(g, products):
        first = start + g * UNROLL
        later = multiply(first)
        add(first - UNROLL, products)
        return later

    groups = (end - start + (UNROLL - 1)) // UNROLL

    @pl.when(groups > 0)
    def _():
        last = lax.fori_loop(1, groups, step, multiply(start))
        add(start + (groups - 1) * UNROLL, last)

    if len(outs) > 1:
        outs[0][...] = acc[: trash * PAIR, :].astype(outs[0].dtype)


def product(first_word, words, blocks, table, trash, sent):
    full = jax.ShapeDtypeStruct(((trash + 1) * PAIR, 2 * LANES), jnp.float32)
    out = jax.ShapeDtypeStruct((trash * PAIR, 2 * LANES), jnp.bfloat16) if sent else full
    return pl.pallas_call(
        functools.partial(product_kernel, trash, first_word),
        in_specs=[SMEM, VMEM, VMEM],
        out_specs=VMEM,
        out_shape=out,
        scratch_shapes=[pltpu.VMEM(full.shape, full.dtype)] if sent else [],
        compiler_params=pltpu.CompilerParams(vmem_limit_bytes=16 * 1024 * 1024),
        cost_estimate=pl.CostEstimate(flops=8 * trash * BLK * LANES * LANES, bytes_accessed=1024 * 1024, transcendentals=0),
        name="product_send" if sent else "product_keep",
    )(words, blocks, table)


def add_kernel(keep_ref, got_ref, next_ref, send_ref):
    half = next_ref.shape[0]
    next_ref[...] = keep_ref[:half, :] + got_ref[:half, :].astype(jnp.float32)
    send_ref[...] = (keep_ref[half:, :] + got_ref[half:, :].astype(jnp.float32)).astype(send_ref.dtype)


def add_halves(keep, which, got):
    rows, lanes = got.shape
    block = lambda n, i: pl.BlockSpec((n, lanes), lambda _: (i, 0))
    return pl.pallas_call(
        add_kernel,
        grid=(1,),
        in_specs=[block(rows, which), block(rows, 0)],
        out_specs=(block(rows // 2, 0), block(rows // 2, 0)),
        out_shape=(
            jax.ShapeDtypeStruct((rows // 2, lanes), jnp.float32),
            jax.ShapeDtypeStruct((rows // 2, lanes), jnp.bfloat16),
        ),
        compiler_params=pltpu.CompilerParams(vmem_limit_bytes=8 * 1024 * 1024),
        cost_estimate=pl.CostEstimate(flops=rows * lanes, bytes_accessed=rows * lanes * 6, transcendentals=0),
        name="add",
    )(keep, got)


def layer_kernel(keep0, got0, keep1, got1, weight_ref, bias_ref, out_ref, left, right):
    base = 0
    for keep, got in ((keep0, got0), (keep1, got1)):
        rows = got.shape[0]
        aggregated = (keep[...] + got[...].astype(jnp.float32)).astype(jnp.bfloat16)
        for h in range(2):
            part = aggregated[:, h * LANES : (h + 1) * LANES]
            hidden = jnp.dot(part, weight_ref[...], preferred_element_type=jnp.float32) + bias_ref[...]
            hidden = jnp.maximum(hidden, 0.0)
            left[pl.ds(base + h, rows, stride=2), :] = hidden[:, :LANES]
            right[pl.ds(base + h, rows, stride=2), :] = hidden[:, LANES:]
        base += 2 * rows
    out_ref[:, :LANES] = left[...].astype(out_ref.dtype)
    out_ref[:, LANES:] = right[...].astype(out_ref.dtype)


def layer(keep0, got0, keep1, got1, weight, bias):
    rows = 2 * (got0.shape[0] + got1.shape[0])
    return pl.pallas_call(
        layer_kernel,
        out_shape=jax.ShapeDtypeStruct((rows, weight.shape[1]), jnp.bfloat16),
        scratch_shapes=[pltpu.VMEM((rows, LANES), jnp.float32)] * 2,
        compiler_params=pltpu.CompilerParams(vmem_limit_bytes=8 * 1024 * 1024),
        name="layer",
    )(keep0, got0, keep1, got1, weight, bias)


def exchange(x, axis, size, bit):
    return lax.ppermute(x, axis, [(i, i ^ (1 << bit)) for i in range(size)])


def shards(n_row, n_col, features, block_codes, block_count, block_values, weight, bias):
    r, c = lax.axis_index("row"), lax.axis_index("col")
    top = n_row.bit_length() - 2
    col_bits = list(range(n_col.bit_length() - 1))

    col_blocks = features.shape[0] // BLK
    row_total = col_blocks * n_col // n_row
    per = row_total // n_col
    small, half = per // 2, row_total // 4
    slots = block_codes.shape[1]
    row_block, col_block = block_codes[0] // col_blocks, block_codes[0] % col_blocks
    owner, sub = (row_block // per) ^ c, row_block % per
    number = jnp.arange(slots, dtype=jnp.int32)
    live = number < block_count[0, 0]
    orders = [col_bits[1:] + col_bits[:1], col_bits]
    places = []
    for order in orders:
        places.append(sum(((owner >> bit) & 1) << (len(order) - 1 - k) for k, bit in enumerate(order)))
    chunk = sub // small
    place = jnp.where(chunk == 0, places[0], places[1]) * small + sub % small
    keep = place < half
    target = jnp.where(keep, chunk * half + place, place - half)
    part = jnp.where(live, jnp.where(keep, 2, chunk), 3)
    key = part * slots + number
    rank = jnp.sum((key[None, :] < key[:, None]).astype(jnp.int32), axis=1)
    word = (number << 16) | (col_block << 8) | target
    spot = jnp.arange(slots + 8, dtype=jnp.int32)
    words = jnp.sum(jnp.where(rank[None, :] == spot[:, None], word[None, :], 0), axis=1)
    ends = jnp.sum((part[None, :] < jnp.arange(8, dtype=jnp.int32)[:, None]).astype(jnp.int32), axis=1)
    words = jnp.concatenate([words, ends])
    blocks = relayout(block_values[0])

    mine = features.T
    index = [0, 1 << top]
    for bit in range(top):
        index = index + [i ^ (1 << bit) for i in index]
    pieces = weight.reshape(n_row, -1, weight.shape[1])[jnp.array(index) ^ r].reshape(weight.shape)
    parts = [mine, exchange(mine, "row", n_row, top)]
    parts[1], blocks, words, pieces = lax.optimization_barrier((parts[1], blocks, words, pieces))
    for bit in range(top):
        parts = parts + [exchange(p, "row", n_row, bit) for p in parts]

    table = make_table(parts)
    mul = lambda k, trash, sent: product(slots + 8 + k, words, blocks, table, trash, sent)
    sends = [mul(0, half, True), mul(1, half, True)]
    kept = mul(2, 2 * half, False)

    keeps = [(kept, 0), (kept, 1)]
    for k in range(len(col_bits)):
        for i in range(2):
            got = exchange(sends[i], "col", n_col, orders[i][k])
            if k < len(col_bits) - 1:
                total, sends[i] = add_halves(*keeps[i], got)
                keeps[i] = (total, 0)
            else:
                keeps[i], sends[i] = keeps[i][0], got
    return layer(keeps[0], sends[0], keeps[1], sends[1], pieces, bias[None, :])


def solution(mesh):
    in_specs = (P("col", "row"), P("row", "col"), P("row", "col"), P("row", "col", None), P(), P())
    out_specs = P(("row", "col"), None)
    body = functools.partial(shards, mesh.shape["row"], mesh.shape["col"])
    return jax.shard_map(body, mesh=mesh, in_specs=in_specs, out_specs=out_specs, check_vma=False)
```

```python
import functools

import jax
import jax.numpy as jnp
from jax import lax
from jax.experimental import pallas as pl
from jax.experimental.pallas import tpu as pltpu
from jax.sharding import PartitionSpec as P

BLK = 64
PAIR = BLK // 2
LANES = 2 * BLK
GROUP = 16
STEPS = 4
UNROLL = 16
SLOT_AT, SOURCE_AT = 13, 7
MIB = 1024 * 1024
SMEM = pl.BlockSpec(memory_space=pltpu.SMEM)
VMEM = pl.BlockSpec(memory_space=pltpu.VMEM)


def log2(size):
    return size.bit_length() - 1


def list_width(slots):
    return -(-(slots + 2 * UNROLL + 8) // LANES) * LANES


def make_lists(orders, per, col_bits, count, codes, words_ref):
    slots, width = codes.shape[1], words_ref.shape[1]
    small = per // 2
    half = small << (len(orders[0][0]) - 1)
    row_block, col_block = codes >> col_bits, codes & ((1 << col_bits) - 1)
    owner = (row_block >> log2(per)) ^ lax.axis_index("col")
    sub = row_block & (per - 1)
    part_rows, rest = sub >> log2(small), sub & (small - 1)
    number = lax.broadcasted_iota(jnp.int32, (1, slots), 1)
    same = lax.broadcasted_iota(jnp.int32, (slots, slots), 0) == lax.broadcasted_iota(jnp.int32, (slots, slots), 1)
    column = lambda row: jnp.sum(jnp.where(same, row, 0.0), axis=1, keepdims=True)
    spot = lax.broadcasted_iota(jnp.int32, (slots, width), 1).astype(jnp.float32)
    lane = lax.broadcasted_iota(jnp.int32, (1, width), 1)
    for f, pair in enumerate(orders):
        places = []
        for order in pair:
            place = jnp.zeros_like(owner)
            for k, bit in enumerate(order):
                place = place | (((owner >> bit) & 1) << (len(order) - 1 - k))
            places.append(place)
        place = (jnp.where(part_rows == 0, places[0], places[1]) << log2(small)) + rest
        keep = place < half
        target = jnp.where(keep, part_rows * half + place, place - half)
        group = jnp.where(number < count, jnp.where(keep, 2, part_rows), 3)
        key = (group * slots + number).astype(jnp.float32)
        word = ((number << SLOT_AT) | (col_block << SOURCE_AT) | target).astype(jnp.float32)
        rank = jnp.sum(jnp.where(key < column(key), 1.0, 0.0), axis=1, keepdims=True)
        words = jnp.sum(jnp.where(rank == spot, column(word), 0.0), axis=0, keepdims=True).astype(jnp.int32)
        for k in range(4):
            before = jnp.sum(jnp.where(group < k, 1.0, 0.0), axis=1, keepdims=True).astype(jnp.int32)
            words = jnp.where(lane == width - 8 + k, before, words)
        words_ref[f : f + 1, :] = words


def relayout_kernel(orders, per, col_bits, count_ref, codes_ref, values_hbm, out_ref, words_ref, held, scratch, arrived):
    step = values_hbm.shape[0] // STEPS
    copies = []
    for k in range(STEPS):
        rows = pl.ds(k * step, step)
        copies.append(pltpu.make_async_copy(values_hbm.at[rows], held.at[rows], arrived.at[k]))
        copies[k].start()
    make_lists(orders, per, col_bits, count_ref[0, 0], codes_ref[...], words_ref)

    def one(g, carry):
        slots = pl.ds(pl.multiple_of(g * GROUP, GROUP), GROUP)
        base = pl.multiple_of(g * (GROUP * PAIR), GROUP * PAIR)
        for p in range(PAIR):
            scratch[pl.ds(base + p * GROUP, GROUP), :] = held[slots, p * LANES : (p + 1) * LANES].astype(jnp.float32)
        for s in range(GROUP):
            rows = scratch[pl.ds(base + s, PAIR, stride=GROUP), :]
            out_ref[pl.ds(base + s * PAIR, PAIR), :] = rows.astype(out_ref.dtype)
        return carry

    groups = step // GROUP
    for k in range(STEPS):
        copies[k].wait()
        lax.fori_loop(k * groups, (k + 1) * groups, one, 0, unroll=2)


def relayout(orders, per, col_bits, count, codes, values):
    slots = values.shape[0]
    return pl.pallas_call(
        functools.partial(relayout_kernel, orders, per, col_bits),
        in_specs=[SMEM, VMEM, pl.BlockSpec(memory_space=pltpu.HBM)],
        out_specs=(VMEM, VMEM),
        out_shape=(
            jax.ShapeDtypeStruct((slots * PAIR, LANES), values.dtype),
            jax.ShapeDtypeStruct((2, list_width(slots)), jnp.int32),
        ),
        scratch_shapes=[
            pltpu.VMEM(values.shape, values.dtype),
            pltpu.VMEM((slots * PAIR, LANES), jnp.float32),
            pltpu.SemaphoreType.DMA((STEPS,)),
        ],
        cost_estimate=pl.CostEstimate(flops=0, bytes_accessed=4 * slots * BLK * BLK, transcendentals=0),
        compiler_params=pltpu.CompilerParams(vmem_limit_bytes=48 * MIB),
        name="relayout",
    )(count, codes, values)


def table_kernel(*refs):
    parts, table = refs[:-1], refs[-1]

    def build(q, carry):
        at = pl.ds(pl.multiple_of(q * LANES, LANES), LANES)
        x = [part[:, at].astype(jnp.float32) for part in parts]
        table[at, :] = jnp.concatenate(x + x, axis=0).T.astype(table.dtype)
        return carry

    lax.fori_loop(0, table.shape[0] // LANES, build, 0, unroll=4)


def make_table(parts):
    nodes = parts[0].shape[1]
    return pl.pallas_call(
        table_kernel,
        in_specs=[VMEM] * len(parts),
        out_specs=VMEM,
        out_shape=jax.ShapeDtypeStruct((nodes, LANES), jnp.bfloat16),
        compiler_params=pltpu.CompilerParams(vmem_limit_bytes=4 * MIB),
        cost_estimate=pl.CostEstimate(flops=0, bytes_accessed=nodes * LANES * 3, transcendentals=0),
        name="table",
    )(*parts)


def product_kernel(trash, feature_half, part, words_ref, blocks_ref, table_ref, *outs):
    pending, acc = outs[-1], outs[-2]
    bounds = words_ref.shape[1] - 8 + part
    start, end = words_ref[feature_half, bounds], words_ref[feature_half, bounds + 1]
    low = lax.broadcasted_iota(jnp.int32, (BLK, LANES), 1) < BLK
    acc[...] = jnp.zeros_like(acc)

    def step(g, carry):
        first = start + g * UNROLL
        products = []
        for u in range(UNROLL):
            word = words_ref[feature_half, first + u]
            block = blocks_ref[pl.ds(pl.multiple_of((word >> SLOT_AT) * PAIR, PAIR), PAIR), :]
            source = (word >> SOURCE_AT) & ((1 << (SLOT_AT - SOURCE_AT)) - 1)
            right = table_ref[pl.ds(pl.multiple_of(source * BLK, BLK), BLK), :]
            zero = jnp.zeros_like(right)
            right = jnp.concatenate([jnp.where(low, right, zero), jnp.where(low, zero, right)], axis=0)
            products.append(jnp.dot(block, right, preferred_element_type=jnp.float32))
        for u in range(UNROLL):
            i = first - UNROLL + u
            word = words_ref[feature_half, jnp.maximum(i, 0)]
            place = jnp.where((i >= start) & (i < end), word & ((1 << SOURCE_AT) - 1), trash)
            rows = pl.ds(pl.multiple_of(place * PAIR, PAIR), PAIR)
            acc[rows, :] = acc[rows, :] + pending[u * PAIR : (u + 1) * PAIR, :]
        for u in range(UNROLL):
            pending[u * PAIR : (u + 1) * PAIR, :] = products[u]
        return carry

    lax.fori_loop(0, (end - start + (UNROLL - 1)) // UNROLL + 1, step, 0)
    if len(outs) > 2:
        outs[0][...] = acc[: trash * PAIR, :].astype(outs[0].dtype)


def product(feature_half, part, words, blocks, table, trash, sent):
    full = jax.ShapeDtypeStruct(((trash + 1) * PAIR, LANES), jnp.float32)
    out = jax.ShapeDtypeStruct((trash * PAIR, LANES), jnp.bfloat16) if sent else full
    sums = [pltpu.VMEM(full.shape, full.dtype)] if sent else []
    return pl.pallas_call(
        functools.partial(product_kernel, trash, feature_half, part),
        in_specs=[SMEM, VMEM, VMEM],
        out_specs=VMEM,
        out_shape=out,
        scratch_shapes=sums + [pltpu.VMEM((UNROLL * PAIR, LANES), jnp.float32)],
        compiler_params=pltpu.CompilerParams(vmem_limit_bytes=8 * MIB),
        cost_estimate=pl.CostEstimate(flops=8 * trash * BLK * LANES * LANES, bytes_accessed=MIB, transcendentals=0),
        name="product_send" if sent else "product_keep",
    )(words, blocks, table)


def add_kernel(keep_ref, got_ref, next_ref, send_ref):
    half = next_ref.shape[0]
    next_ref[...] = keep_ref[:half, :] + got_ref[:half, :].astype(jnp.float32)
    send_ref[...] = (keep_ref[half:, :] + got_ref[half:, :].astype(jnp.float32)).astype(send_ref.dtype)


def add_halves(keep, which, got):
    rows, lanes = got.shape
    block = lambda n, i: pl.BlockSpec((n, lanes), lambda _: (i, 0))
    return pl.pallas_call(
        add_kernel,
        grid=(1,),
        in_specs=[block(rows, which), block(rows, 0)],
        out_specs=(block(rows // 2, 0), block(rows // 2, 0)),
        out_shape=(
            jax.ShapeDtypeStruct((rows // 2, lanes), jnp.float32),
            jax.ShapeDtypeStruct((rows // 2, lanes), jnp.bfloat16),
        ),
        compiler_params=pltpu.CompilerParams(vmem_limit_bytes=4 * MIB),
        cost_estimate=pl.CostEstimate(flops=rows * lanes, bytes_accessed=rows * lanes * 6, transcendentals=0),
        name="add",
    )(keep, got)


def layer_kernel(index, *refs):
    sums, (weight_ref, bias_ref, out_ref, wide, left, right) = refs[:8], refs[8:]
    r = lax.axis_index("row")
    wide[...] = weight_ref[...].astype(jnp.float32)
    size = wide.shape[0] // (2 * len(index[0]))
    halves = []
    for pieces in index:
        rows = [wide[pl.ds(pl.multiple_of((r ^ i) * size, size), size), :] for i in pieces]
        halves.append(jnp.concatenate(rows, axis=0).astype(jnp.bfloat16))
    zero = jnp.zeros_like(halves[0])
    even = jnp.concatenate([halves[0], zero, halves[1], zero], axis=0)
    odd = jnp.concatenate([zero, halves[0], zero, halves[1]], axis=0)
    rows = sums[0].shape[0]
    for k in range(2):
        aggregated = []
        for f in range(2):
            keep, got = sums[4 * f + 2 * k], sums[4 * f + 2 * k + 1]
            aggregated.append((keep[...] + got[...].astype(jnp.float32)).astype(jnp.bfloat16))
        both = jnp.concatenate(aggregated, axis=1)
        for h, w in enumerate((even, odd)):
            hidden = jnp.dot(both, w, preferred_element_type=jnp.float32) + bias_ref[...]
            hidden = jnp.maximum(hidden, 0.0)
            left[pl.ds(2 * rows * k + h, rows, stride=2), :] = hidden[:, :LANES]
            right[pl.ds(2 * rows * k + h, rows, stride=2), :] = hidden[:, LANES:]
    out_ref[:, :LANES] = left[...].astype(out_ref.dtype)
    out_ref[:, LANES:] = right[...].astype(out_ref.dtype)


def layer(index, sums, weight, bias):
    rows = 4 * sums[0].shape[0]
    return pl.pallas_call(
        functools.partial(layer_kernel, index),
        out_shape=jax.ShapeDtypeStruct((rows, weight.shape[1]), jnp.bfloat16),
        scratch_shapes=[pltpu.VMEM(weight.shape, jnp.float32)] + [pltpu.VMEM((rows, LANES), jnp.float32)] * 2,
        compiler_params=pltpu.CompilerParams(vmem_limit_bytes=8 * MIB),
        name="layer",
    )(*sums, weight, bias)


def exchange(x, axis, size, bit):
    return lax.ppermute(x, axis, [(i, i ^ (1 << bit)) for i in range(size)])


def shards(n_row, n_col, features, block_codes, block_count, block_values, weight, bias):
    top, col_axis_bits = log2(n_row) - 1, list(range(log2(n_col)))
    col_blocks = features.shape[0] // BLK
    row_total = col_blocks * n_col // n_row
    per = row_total // n_col
    half = row_total // 4

    z_first, x_first = col_axis_bits[1:] + col_axis_bits[:1], col_axis_bits
    orders = ((z_first, x_first), (x_first, x_first))

    def spread(pieces, index):
        for bit in range(top):
            pieces = pieces + [exchange(p, "row", n_row, bit) for p in pieces]
            index = index + [i ^ (1 << bit) for i in index]
        return pieces, index

    mine = features.T
    other = exchange(mine, "row", n_row, top)
    near, near_index = spread([mine], [0])
    blocks, words = relayout(orders, per, log2(col_blocks), block_count, block_codes, block_values[0])

    def products(f, table):
        sends = [product(f, k, words, blocks, table, half, True) for k in range(2)]
        kept = product(f, 2, words, blocks, table, 2 * half, False)
        return sends, [(kept, 0), (kept, 1)]

    table = make_table(near)
    first = product(0, 0, words, blocks, table, half, True)
    other, first = lax.optimization_barrier((other, first))
    far, far_index = spread([other], [1 << top])
    sends = [first, product(0, 1, words, blocks, table, half, True)]
    kept = product(0, 2, words, blocks, table, 2 * half, False)
    keeps = [(kept, 0), (kept, 1)]
    more_sends, more_keeps = products(1, make_table(far))
    sends, keeps = sends + more_sends, keeps + more_keeps

    chunk_orders = orders[0] + orders[1]
    for k in range(len(col_axis_bits)):
        for i in range(4):
            got = exchange(sends[i], "col", n_col, chunk_orders[i][k])
            if k < len(col_axis_bits) - 1:
                total, sends[i] = add_halves(*keeps[i], got)
                keeps[i] = (total, 0)
            else:
                keeps[i], sends[i] = keeps[i][0], got
    sums = [x for i in range(4) for x in (keeps[i], sends[i])]
    return layer((near_index, far_index), sums, weight, bias[None, :])


def solution(mesh):
    in_specs = (P("col", "row"), P("row", "col"), P("row", "col"), P("row", "col", None), P(), P())
    out_specs = P(("row", "col"), None)
    body = functools.partial(shards, mesh.shape["row"], mesh.shape["col"])
    return jax.shard_map(body, mesh=mesh, in_specs=in_specs, out_specs=out_specs, check_vma=False)
```

```python
import functools

import jax
import jax.numpy as jnp
from jax import lax
from jax.experimental import pallas as pl
from jax.experimental.pallas import tpu as pltpu
from jax.sharding import PartitionSpec as P

BLK = 64
PAIR = BLK // 2
LANES = 2 * BLK
GROUP = 16
STEPS = 4
UNROLL = 16
SLOT_AT, SOURCE_AT = 13, 7
MIB = 1024 * 1024
SMEM = pl.BlockSpec(memory_space=pltpu.SMEM)
VMEM = pl.BlockSpec(memory_space=pltpu.VMEM)


def log2(size):
    return size.bit_length() - 1


def list_width(slots):
    return -(-(slots + 2 * UNROLL + 8) // LANES) * LANES


def make_lists(orders, per, col_bits, count, codes, words_ref):
    slots, width = codes.shape[1], words_ref.shape[1]
    small = per // 2
    half = small << (len(orders[0][0]) - 1)
    row_block, col_block = codes >> col_bits, codes & ((1 << col_bits) - 1)
    owner = (row_block >> log2(per)) ^ lax.axis_index("col")
    sub = row_block & (per - 1)
    part_rows, rest = sub >> log2(small), sub & (small - 1)
    number = lax.broadcasted_iota(jnp.int32, (1, slots), 1)
    same = lax.broadcasted_iota(jnp.int32, (slots, slots), 0) == lax.broadcasted_iota(jnp.int32, (slots, slots), 1)
    column = lambda row: jnp.sum(jnp.where(same, row, 0.0), axis=1, keepdims=True)
    spot = lax.broadcasted_iota(jnp.int32, (slots, width), 1).astype(jnp.float32)
    lane = lax.broadcasted_iota(jnp.int32, (1, width), 1)
    for f, pair in enumerate(orders):
        places = []
        for order in pair:
            place = jnp.zeros_like(owner)
            for k, bit in enumerate(order):
                place = place | (((owner >> bit) & 1) << (len(order) - 1 - k))
            places.append(place)
        place = (jnp.where(part_rows == 0, places[0], places[1]) << log2(small)) + rest
        keep = place < half
        target = jnp.where(keep, part_rows * half + place, place - half)
        group = jnp.where(number < count, jnp.where(keep, 2, part_rows), 3)
        key = (group * slots + number).astype(jnp.float32)
        word = ((number << SLOT_AT) | (col_block << SOURCE_AT) | target).astype(jnp.float32)
        rank = jnp.sum(jnp.where(key < column(key), 1.0, 0.0), axis=1, keepdims=True)
        words = jnp.sum(jnp.where(rank == spot, column(word), 0.0), axis=0, keepdims=True).astype(jnp.int32)
        for k in range(4):
            before = jnp.sum(jnp.where(group < k, 1.0, 0.0), axis=1, keepdims=True).astype(jnp.int32)
            words = jnp.where(lane == width - 8 + k, before, words)
        words_ref[f : f + 1, :] = words


def relayout_kernel(orders, per, col_bits, count_ref, codes_hbm, values_hbm, out_ref, words_ref, codes, held, scratch, arrived, codes_arrived):
    codes_copy = pltpu.make_async_copy(codes_hbm, codes, codes_arrived)
    codes_copy.start()
    step = values_hbm.shape[0] // STEPS
    copies = []
    for k in range(STEPS):
        rows = pl.ds(k * step, step)
        copies.append(pltpu.make_async_copy(values_hbm.at[rows], held.at[rows], arrived.at[k]))
        copies[k].start()
    codes_copy.wait()
    make_lists(orders, per, col_bits, count_ref[0, 0], codes[...], words_ref)

    def one(g, carry):
        slots = pl.ds(pl.multiple_of(g * GROUP, GROUP), GROUP)
        base = pl.multiple_of(g * (GROUP * PAIR), GROUP * PAIR)
        for p in range(PAIR):
            scratch[pl.ds(base + p * GROUP, GROUP), :] = held[slots, p * LANES : (p + 1) * LANES].astype(jnp.float32)
        for s in range(GROUP):
            rows = scratch[pl.ds(base + s, PAIR, stride=GROUP), :]
            out_ref[pl.ds(base + s * PAIR, PAIR), :] = rows.astype(out_ref.dtype)
        return carry

    groups = step // GROUP
    for k in range(STEPS):
        copies[k].wait()
        lax.fori_loop(k * groups, (k + 1) * groups, one, 0, unroll=2)


def relayout(orders, per, col_bits, count, codes, values):
    slots = values.shape[0]
    return pl.pallas_call(
        functools.partial(relayout_kernel, orders, per, col_bits),
        in_specs=[SMEM] + [pl.BlockSpec(memory_space=pltpu.HBM)] * 2,
        out_specs=(VMEM, VMEM),
        out_shape=(
            jax.ShapeDtypeStruct((slots * PAIR, LANES), values.dtype),
            jax.ShapeDtypeStruct((2, list_width(slots)), jnp.int32),
        ),
        scratch_shapes=[
            pltpu.VMEM(codes.shape, codes.dtype),
            pltpu.VMEM(values.shape, values.dtype),
            pltpu.VMEM((slots * PAIR, LANES), jnp.float32),
            pltpu.SemaphoreType.DMA((STEPS,)),
            pltpu.SemaphoreType.DMA,
        ],
        cost_estimate=pl.CostEstimate(flops=0, bytes_accessed=4 * slots * BLK * BLK, transcendentals=0),
        compiler_params=pltpu.CompilerParams(vmem_limit_bytes=48 * MIB),
        name="relayout",
    )(count, codes, values)


def table_kernel(*refs):
    parts, table = refs[:-1], refs[-1]

    def build(q, carry):
        at = pl.ds(pl.multiple_of(q * LANES, LANES), LANES)
        x = [part[:, at].astype(jnp.float32) for part in parts]
        table[at, :] = jnp.concatenate(x + x, axis=0).T.astype(table.dtype)
        return carry

    lax.fori_loop(0, table.shape[0] // LANES, build, 0, unroll=4)


def make_table(parts):
    nodes = parts[0].shape[1]
    return pl.pallas_call(
        table_kernel,
        in_specs=[VMEM] * len(parts),
        out_specs=VMEM,
        out_shape=jax.ShapeDtypeStruct((nodes, LANES), jnp.bfloat16),
        compiler_params=pltpu.CompilerParams(vmem_limit_bytes=4 * MIB),
        cost_estimate=pl.CostEstimate(flops=0, bytes_accessed=nodes * LANES * 3, transcendentals=0),
        name="table",
    )(*parts)


def product_kernel(trash, feature_half, part, words_ref, blocks_ref, table_ref, *outs):
    pending, acc = outs[-1], outs[-2]
    bounds = words_ref.shape[1] - 8 + part
    start, end = words_ref[feature_half, bounds], words_ref[feature_half, bounds + 1]
    low = lax.broadcasted_iota(jnp.int32, (BLK, LANES), 1) < BLK
    acc[...] = jnp.zeros_like(acc)

    def step(g, carry):
        first = start + g * UNROLL
        products = []
        for u in range(UNROLL):
            word = words_ref[feature_half, first + u]
            block = blocks_ref[pl.ds(pl.multiple_of((word >> SLOT_AT) * PAIR, PAIR), PAIR), :]
            source = (word >> SOURCE_AT) & ((1 << (SLOT_AT - SOURCE_AT)) - 1)
            right = table_ref[pl.ds(pl.multiple_of(source * BLK, BLK), BLK), :]
            zero = jnp.zeros_like(right)
            right = jnp.concatenate([jnp.where(low, right, zero), jnp.where(low, zero, right)], axis=0)
            products.append(jnp.dot(block, right, preferred_element_type=jnp.float32))
        for u in range(UNROLL):
            i = first - UNROLL + u
            word = words_ref[feature_half, jnp.maximum(i, 0)]
            place = jnp.where((i >= start) & (i < end), word & ((1 << SOURCE_AT) - 1), trash)
            rows = pl.ds(pl.multiple_of(place * PAIR, PAIR), PAIR)
            acc[rows, :] = acc[rows, :] + pending[u * PAIR : (u + 1) * PAIR, :]
        for u in range(UNROLL):
            pending[u * PAIR : (u + 1) * PAIR, :] = products[u]
        return carry

    lax.fori_loop(0, (end - start + (UNROLL - 1)) // UNROLL + 1, step, 0)
    if len(outs) > 2:
        outs[0][...] = acc[: trash * PAIR, :].astype(outs[0].dtype)


def product(feature_half, part, words, blocks, table, trash, sent):
    full = jax.ShapeDtypeStruct(((trash + 1) * PAIR, LANES), jnp.float32)
    out = jax.ShapeDtypeStruct((trash * PAIR, LANES), jnp.bfloat16) if sent else full
    sums = [pltpu.VMEM(full.shape, full.dtype)] if sent else []
    return pl.pallas_call(
        functools.partial(product_kernel, trash, feature_half, part),
        in_specs=[SMEM, VMEM, VMEM],
        out_specs=VMEM,
        out_shape=out,
        scratch_shapes=sums + [pltpu.VMEM((UNROLL * PAIR, LANES), jnp.float32)],
        compiler_params=pltpu.CompilerParams(vmem_limit_bytes=8 * MIB),
        cost_estimate=pl.CostEstimate(flops=8 * trash * BLK * LANES * LANES, bytes_accessed=MIB, transcendentals=0),
        name="product_send" if sent else "product_keep",
    )(words, blocks, table)


def add_kernel(keep_ref, got_ref, next_ref, send_ref):
    half = next_ref.shape[0]
    next_ref[...] = keep_ref[:half, :] + got_ref[:half, :].astype(jnp.float32)
    send_ref[...] = (keep_ref[half:, :] + got_ref[half:, :].astype(jnp.float32)).astype(send_ref.dtype)


def add_halves(keep, which, got):
    rows, lanes = got.shape
    block = lambda n, i: pl.BlockSpec((n, lanes), lambda _: (i, 0))
    return pl.pallas_call(
        add_kernel,
        grid=(1,),
        in_specs=[block(rows, which), block(rows, 0)],
        out_specs=(block(rows // 2, 0), block(rows // 2, 0)),
        out_shape=(
            jax.ShapeDtypeStruct((rows // 2, lanes), jnp.float32),
            jax.ShapeDtypeStruct((rows // 2, lanes), jnp.bfloat16),
        ),
        compiler_params=pltpu.CompilerParams(vmem_limit_bytes=4 * MIB),
        cost_estimate=pl.CostEstimate(flops=rows * lanes, bytes_accessed=rows * lanes * 6, transcendentals=0),
        name="add",
    )(keep, got)


def layer_kernel(index, *refs):
    sums, (weight_ref, bias_ref, out_ref, wide, left, right) = refs[:8], refs[8:]
    r = lax.axis_index("row")
    wide[...] = weight_ref[...].astype(jnp.float32)
    size = wide.shape[0] // (2 * len(index[0]))
    halves = []
    for pieces in index:
        rows = [wide[pl.ds(pl.multiple_of((r ^ i) * size, size), size), :] for i in pieces]
        halves.append(jnp.concatenate(rows, axis=0).astype(jnp.bfloat16))
    zero = jnp.zeros_like(halves[0])
    even = jnp.concatenate([halves[0], zero, halves[1], zero], axis=0)
    odd = jnp.concatenate([zero, halves[0], zero, halves[1]], axis=0)
    rows = sums[0].shape[0]
    for k in range(2):
        aggregated = []
        for f in range(2):
            keep, got = sums[4 * f + 2 * k], sums[4 * f + 2 * k + 1]
            aggregated.append((keep[...] + got[...].astype(jnp.float32)).astype(jnp.bfloat16))
        both = jnp.concatenate(aggregated, axis=1)
        for h, w in enumerate((even, odd)):
            hidden = jnp.dot(both, w, preferred_element_type=jnp.float32) + bias_ref[...]
            hidden = jnp.maximum(hidden, 0.0)
            left[pl.ds(2 * rows * k + h, rows, stride=2), :] = hidden[:, :LANES]
            right[pl.ds(2 * rows * k + h, rows, stride=2), :] = hidden[:, LANES:]
    out_ref[:, :LANES] = left[...].astype(out_ref.dtype)
    out_ref[:, LANES:] = right[...].astype(out_ref.dtype)


def layer(index, sums, weight, bias):
    rows = 4 * sums[0].shape[0]
    return pl.pallas_call(
        functools.partial(layer_kernel, index),
        out_shape=jax.ShapeDtypeStruct((rows, weight.shape[1]), jnp.bfloat16),
        scratch_shapes=[pltpu.VMEM(weight.shape, jnp.float32)] + [pltpu.VMEM((rows, LANES), jnp.float32)] * 2,
        compiler_params=pltpu.CompilerParams(vmem_limit_bytes=8 * MIB),
        name="layer",
    )(*sums, weight, bias)


def exchange(x, axis, size, bit):
    return lax.ppermute(x, axis, [(i, i ^ (1 << bit)) for i in range(size)])


def shards(n_row, n_col, features, block_codes, block_count, block_values, weight, bias):
    top, col_axis_bits = log2(n_row) - 1, list(range(log2(n_col)))
    col_blocks = features.shape[0] // BLK
    row_total = col_blocks * n_col // n_row
    per = row_total // n_col
    half = row_total // 4

    z_first, x_first = col_axis_bits[1:] + col_axis_bits[:1], col_axis_bits
    orders = ((x_first, z_first), (x_first, z_first))

    def spread(pieces, index):
        for bit in range(top):
            pieces = pieces + [exchange(p, "row", n_row, bit) for p in pieces]
            index = index + [i ^ (1 << bit) for i in index]
        return pieces, index

    mine = features.T
    other = exchange(mine, "row", n_row, top)
    near, near_index = spread([mine], [0])
    blocks, words = relayout(orders, per, log2(col_blocks), block_count, block_codes, block_values[0])

    def products(f, table):
        sends = [product(f, k, words, blocks, table, half, True) for k in range(2)]
        kept = product(f, 2, words, blocks, table, 2 * half, False)
        return sends, [(kept, 0), (kept, 1)]

    table = make_table(near)
    first = product(0, 0, words, blocks, table, half, True)
    other, first = lax.optimization_barrier((other, first))
    far, far_index = spread([other], [1 << top])
    sends = [first, product(0, 1, words, blocks, table, half, True)]
    kept = product(0, 2, words, blocks, table, 2 * half, False)
    keeps = [(kept, 0), (kept, 1)]
    more_sends, more_keeps = products(1, make_table(far))
    sends, keeps = sends + more_sends, keeps + more_keeps

    chunk_orders = orders[0] + orders[1]
    for k in range(len(col_axis_bits)):
        for i in range(4):
            got = exchange(sends[i], "col", n_col, chunk_orders[i][k])
            if k < len(col_axis_bits) - 1:
                total, sends[i] = add_halves(*keeps[i], got)
                keeps[i] = (total, 0)
            else:
                keeps[i], sends[i] = keeps[i][0], got
    sums = [x for i in range(4) for x in (keeps[i], sends[i])]
    return layer((near_index, far_index), sums, weight, bias[None, :])


def solution(mesh):
    in_specs = (P("col", "row"), P("row", "col"), P("row", "col"), P("row", "col", None), P(), P())
    out_specs = P(("row", "col"), None)
    body = functools.partial(shards, mesh.shape["row"], mesh.shape["col"])
    return jax.shard_map(body, mesh=mesh, in_specs=in_specs, out_specs=out_specs, check_vma=False)
```

```python
import functools

import jax
import jax.numpy as jnp
from jax import lax
from jax.experimental import pallas as pl
from jax.experimental.pallas import tpu as pltpu
from jax.sharding import PartitionSpec as P

BLK = 64
PAIR = BLK // 2
LANES = 2 * BLK
GROUP = 16
STEPS = 4
UNROLL = 16
SLOT_AT, SOURCE_AT = 13, 7
MIB = 1024 * 1024
SMEM = pl.BlockSpec(memory_space=pltpu.SMEM)
VMEM = pl.BlockSpec(memory_space=pltpu.VMEM)


def log2(size):
    return size.bit_length() - 1


def list_width(slots):
    return -(-(slots + 2 * UNROLL + 8) // LANES) * LANES


def make_lists(orders, per, col_bits, count, codes, words_ref):
    slots, width = codes.shape[1], words_ref.shape[1]
    small = per // 2
    half = small << (len(orders[0][0]) - 1)
    row_block, col_block = codes >> col_bits, codes & ((1 << col_bits) - 1)
    owner = (row_block >> log2(per)) ^ lax.axis_index("col")
    sub = row_block & (per - 1)
    part_rows, rest = sub >> log2(small), sub & (small - 1)
    number = lax.broadcasted_iota(jnp.int32, (1, slots), 1)
    same = lax.broadcasted_iota(jnp.int32, (slots, slots), 0) == lax.broadcasted_iota(jnp.int32, (slots, slots), 1)
    column = lambda row: jnp.sum(jnp.where(same, row, 0.0), axis=1, keepdims=True)
    spot = lax.broadcasted_iota(jnp.int32, (slots, width), 1).astype(jnp.float32)
    lane = lax.broadcasted_iota(jnp.int32, (1, width), 1)
    for f, pair in enumerate(orders):
        places = []
        for order in pair:
            place = jnp.zeros_like(owner)
            for k, bit in enumerate(order):
                place = place | (((owner >> bit) & 1) << (len(order) - 1 - k))
            places.append(place)
        place = (jnp.where(part_rows == 0, places[0], places[1]) << log2(small)) + rest
        keep = place < half
        target = jnp.where(keep, part_rows * half + place, place - half)
        group = jnp.where(number < count, jnp.where(keep, 2, part_rows), 3)
        key = (group * slots + number).astype(jnp.float32)
        word = ((number << SLOT_AT) | (col_block << SOURCE_AT) | target).astype(jnp.float32)
        rank = jnp.sum(jnp.where(key < column(key), 1.0, 0.0), axis=1, keepdims=True)
        words = jnp.sum(jnp.where(rank == spot, column(word), 0.0), axis=0, keepdims=True).astype(jnp.int32)
        for k in range(4):
            before = jnp.sum(jnp.where(group < k, 1.0, 0.0), axis=1, keepdims=True).astype(jnp.int32)
            words = jnp.where(lane == width - 8 + k, before, words)
        words_ref[f : f + 1, :] = words


def relayout_kernel(orders, per, col_bits, count_ref, codes_hbm, values_hbm, out_ref, words_ref, codes, held, scratch, arrived, codes_arrived):
    codes_copy = pltpu.make_async_copy(codes_hbm, codes, codes_arrived)
    codes_copy.start()
    step = values_hbm.shape[0] // STEPS
    copies = []
    for k in range(STEPS):
        rows = pl.ds(k * step, step)
        copies.append(pltpu.make_async_copy(values_hbm.at[rows], held.at[rows], arrived.at[k]))
        copies[k].start()
    codes_copy.wait()
    make_lists(orders, per, col_bits, count_ref[0, 0], codes[...], words_ref)

    def one(g, carry):
        slots = pl.ds(pl.multiple_of(g * GROUP, GROUP), GROUP)
        base = pl.multiple_of(g * (GROUP * PAIR), GROUP * PAIR)
        for p in range(PAIR):
            scratch[pl.ds(base + p * GROUP, GROUP), :] = held[slots, p * LANES : (p + 1) * LANES].astype(jnp.float32)
        for s in range(GROUP):
            rows = scratch[pl.ds(base + s, PAIR, stride=GROUP), :]
            out_ref[pl.ds(base + s * PAIR, PAIR), :] = rows.astype(out_ref.dtype)
        return carry

    groups = step // GROUP
    for k in range(STEPS):
        copies[k].wait()
        lax.fori_loop(k * groups, (k + 1) * groups, one, 0, unroll=2)


def relayout(orders, per, col_bits, count, codes, values):
    slots = values.shape[0]
    return pl.pallas_call(
        functools.partial(relayout_kernel, orders, per, col_bits),
        in_specs=[SMEM] + [pl.BlockSpec(memory_space=pltpu.HBM)] * 2,
        out_specs=(VMEM, VMEM),
        out_shape=(
            jax.ShapeDtypeStruct((slots * PAIR, LANES), values.dtype),
            jax.ShapeDtypeStruct((2, list_width(slots)), jnp.int32),
        ),
        scratch_shapes=[
            pltpu.VMEM(codes.shape, codes.dtype),
            pltpu.VMEM(values.shape, values.dtype),
            pltpu.VMEM((slots * PAIR, LANES), jnp.float32),
            pltpu.SemaphoreType.DMA((STEPS,)),
            pltpu.SemaphoreType.DMA,
        ],
        cost_estimate=pl.CostEstimate(flops=0, bytes_accessed=4 * slots * BLK * BLK, transcendentals=0),
        compiler_params=pltpu.CompilerParams(vmem_limit_bytes=48 * MIB),
        name="relayout",
    )(count, codes, values)


def table_kernel(*refs):
    parts, table = refs[:-1], refs[-1]

    def build(q, carry):
        at = pl.ds(pl.multiple_of(q * LANES, LANES), LANES)
        x = [part[:, at].astype(jnp.float32) for part in parts]
        table[at, :] = jnp.concatenate(x + x, axis=0).T.astype(table.dtype)
        return carry

    lax.fori_loop(0, table.shape[0] // LANES, build, 0, unroll=4)


def make_table(parts):
    nodes = parts[0].shape[1]
    return pl.pallas_call(
        table_kernel,
        in_specs=[VMEM] * len(parts),
        out_specs=VMEM,
        out_shape=jax.ShapeDtypeStruct((nodes, LANES), jnp.bfloat16),
        compiler_params=pltpu.CompilerParams(vmem_limit_bytes=4 * MIB),
        cost_estimate=pl.CostEstimate(flops=0, bytes_accessed=nodes * LANES * 3, transcendentals=0),
        name="table",
    )(*parts)


def product_kernel(trash, feature_half, part, words_ref, blocks_ref, table_ref, *outs):
    pending, acc = outs[-1], outs[-2]
    bounds = words_ref.shape[1] - 8 + part
    start, end = words_ref[feature_half, bounds], words_ref[feature_half, bounds + 1]
    low = lax.broadcasted_iota(jnp.int32, (BLK, LANES), 1) < BLK
    acc[...] = jnp.zeros_like(acc)

    def add(first):
        for u in range(UNROLL):
            i = first + u
            word = words_ref[feature_half, jnp.maximum(i, 0)]
            place = jnp.where((i >= start) & (i < end), word & ((1 << SOURCE_AT) - 1), trash)
            rows = pl.ds(pl.multiple_of(place * PAIR, PAIR), PAIR)
            acc[rows, :] = acc[rows, :] + pending[u * PAIR : (u + 1) * PAIR, :]

    def step(g, carry):
        first = start + g * UNROLL
        products = []
        for u in range(UNROLL):
            word = words_ref[feature_half, first + u]
            block = blocks_ref[pl.ds(pl.multiple_of((word >> SLOT_AT) * PAIR, PAIR), PAIR), :]
            source = (word >> SOURCE_AT) & ((1 << (SLOT_AT - SOURCE_AT)) - 1)
            right = table_ref[pl.ds(pl.multiple_of(source * BLK, BLK), BLK), :]
            zero = jnp.zeros_like(right)
            right = jnp.concatenate([jnp.where(low, right, zero), jnp.where(low, zero, right)], axis=0)
            products.append(jnp.dot(block, right, preferred_element_type=jnp.float32))
        add(first - UNROLL)
        for u in range(UNROLL):
            pending[u * PAIR : (u + 1) * PAIR, :] = products[u]
        return carry

    groups = (end - start + (UNROLL - 1)) // UNROLL
    lax.fori_loop(0, groups, step, 0)
    add(start + (groups - 1) * UNROLL)
    if len(outs) > 2:
        outs[0][...] = acc[: trash * PAIR, :].astype(outs[0].dtype)


def product(feature_half, part, words, blocks, table, trash, sent):
    full = jax.ShapeDtypeStruct(((trash + 1) * PAIR, LANES), jnp.float32)
    out = jax.ShapeDtypeStruct((trash * PAIR, LANES), jnp.bfloat16) if sent else full
    sums = [pltpu.VMEM(full.shape, full.dtype)] if sent else []
    return pl.pallas_call(
        functools.partial(product_kernel, trash, feature_half, part),
        in_specs=[SMEM, VMEM, VMEM],
        out_specs=VMEM,
        out_shape=out,
        scratch_shapes=sums + [pltpu.VMEM((UNROLL * PAIR, LANES), jnp.float32)],
        compiler_params=pltpu.CompilerParams(vmem_limit_bytes=8 * MIB),
        cost_estimate=pl.CostEstimate(flops=8 * trash * BLK * LANES * LANES, bytes_accessed=MIB, transcendentals=0),
        name="product_send" if sent else "product_keep",
    )(words, blocks, table)


def add_kernel(keep_ref, got_ref, next_ref, send_ref):
    half = next_ref.shape[0]
    next_ref[...] = keep_ref[:half, :] + got_ref[:half, :].astype(jnp.float32)
    send_ref[...] = (keep_ref[half:, :] + got_ref[half:, :].astype(jnp.float32)).astype(send_ref.dtype)


def add_halves(keep, which, got):
    rows, lanes = got.shape
    block = lambda n, i: pl.BlockSpec((n, lanes), lambda _: (i, 0))
    return pl.pallas_call(
        add_kernel,
        grid=(1,),
        in_specs=[block(rows, which), block(rows, 0)],
        out_specs=(block(rows // 2, 0), block(rows // 2, 0)),
        out_shape=(
            jax.ShapeDtypeStruct((rows // 2, lanes), jnp.float32),
            jax.ShapeDtypeStruct((rows // 2, lanes), jnp.bfloat16),
        ),
        compiler_params=pltpu.CompilerParams(vmem_limit_bytes=4 * MIB),
        cost_estimate=pl.CostEstimate(flops=rows * lanes, bytes_accessed=rows * lanes * 6, transcendentals=0),
        name="add",
    )(keep, got)


def layer_kernel(index, *refs):
    sums, (weight_ref, bias_ref, out_ref, wide, left, right) = refs[:8], refs[8:]
    r = lax.axis_index("row")
    wide[...] = weight_ref[...].astype(jnp.float32)
    size = wide.shape[0] // (2 * len(index[0]))
    halves = []
    for pieces in index:
        rows = [wide[pl.ds(pl.multiple_of((r ^ i) * size, size), size), :] for i in pieces]
        halves.append(jnp.concatenate(rows, axis=0).astype(jnp.bfloat16))
    zero = jnp.zeros_like(halves[0])
    even = jnp.concatenate([halves[0], zero, halves[1], zero], axis=0)
    odd = jnp.concatenate([zero, halves[0], zero, halves[1]], axis=0)
    rows = sums[0].shape[0]
    for k in range(2):
        aggregated = []
        for f in range(2):
            keep, got = sums[4 * f + 2 * k], sums[4 * f + 2 * k + 1]
            aggregated.append((keep[...] + got[...].astype(jnp.float32)).astype(jnp.bfloat16))
        both = jnp.concatenate(aggregated, axis=1)
        for h, w in enumerate((even, odd)):
            hidden = jnp.dot(both, w, preferred_element_type=jnp.float32) + bias_ref[...]
            hidden = jnp.maximum(hidden, 0.0)
            left[pl.ds(2 * rows * k + h, rows, stride=2), :] = hidden[:, :LANES]
            right[pl.ds(2 * rows * k + h, rows, stride=2), :] = hidden[:, LANES:]
    out_ref[:, :LANES] = left[...].astype(out_ref.dtype)
    out_ref[:, LANES:] = right[...].astype(out_ref.dtype)


def layer(index, sums, weight, bias):
    rows = 4 * sums[0].shape[0]
    return pl.pallas_call(
        functools.partial(layer_kernel, index),
        out_shape=jax.ShapeDtypeStruct((rows, weight.shape[1]), jnp.bfloat16),
        scratch_shapes=[pltpu.VMEM(weight.shape, jnp.float32)] + [pltpu.VMEM((rows, LANES), jnp.float32)] * 2,
        compiler_params=pltpu.CompilerParams(vmem_limit_bytes=8 * MIB),
        name="layer",
    )(*sums, weight, bias)


def exchange(x, axis, size, bit):
    return lax.ppermute(x, axis, [(i, i ^ (1 << bit)) for i in range(size)])


def shards(n_row, n_col, features, block_codes, block_count, block_values, weight, bias):
    top, col_axis_bits = log2(n_row) - 1, list(range(log2(n_col)))
    col_blocks = features.shape[0] // BLK
    row_total = col_blocks * n_col // n_row
    per = row_total // n_col
    half = row_total // 4

    z_first, x_first = col_axis_bits[1:] + col_axis_bits[:1], col_axis_bits
    orders = ((x_first, z_first), (x_first, x_first))

    def spread(pieces, index):
        for bit in range(top):
            pieces = pieces + [exchange(p, "row", n_row, bit) for p in pieces]
            index = index + [i ^ (1 << bit) for i in index]
        return pieces, index

    mine = features.T
    other = exchange(mine, "row", n_row, top)
    near, near_index = spread([mine], [0])
    blocks, words = relayout(orders, per, log2(col_blocks), block_count, block_codes, block_values[0])

    table = make_table(near)
    first = product(0, 0, words, blocks, table, half, True)
    other, first = lax.optimization_barrier((other, first))
    far, far_index = spread([other], [1 << top])
    sends, keeps = [first, product(0, 1, words, blocks, table, half, True)], []
    for f in range(2):
        if f > 0:
            table = make_table(far)
            sends += [product(f, k, words, blocks, table, half, True) for k in range(2)]
        kept = product(f, 2, words, blocks, table, 2 * half, False)
        keeps += [(kept, 0), (kept, 1)]
        far[0], _ = lax.optimization_barrier((far[0], kept))

    chunk_orders = orders[0] + orders[1]
    for k in range(len(col_axis_bits)):
        for i in range(4):
            got = exchange(sends[i], "col", n_col, chunk_orders[i][k])
            if k < len(col_axis_bits) - 1:
                total, sends[i] = add_halves(*keeps[i], got)
                keeps[i] = (total, 0)
            else:
                keeps[i], sends[i] = keeps[i][0], got
    sums = [x for i in range(4) for x in (keeps[i], sends[i])]
    return layer((near_index, far_index), sums, weight, bias[None, :])


def solution(mesh):
    in_specs = (P("col", "row"), P("row", "col"), P("row", "col"), P("row", "col", None), P(), P())
    out_specs = P(("row", "col"), None)
    body = functools.partial(shards, mesh.shape["row"], mesh.shape["col"])
    return jax.shard_map(body, mesh=mesh, in_specs=in_specs, out_specs=out_specs, check_vma=False)
```

```python
import functools

import jax
import jax.numpy as jnp
from jax import lax
from jax.experimental import pallas as pl
from jax.experimental.pallas import tpu as pltpu
from jax.sharding import PartitionSpec as P

BLK = 64
PAIR = BLK // 2
LANES = 2 * BLK
GROUP = 16
STEPS = 4
UNROLL = 16
SLOT_AT, SOURCE_AT = 13, 7
MIB = 1024 * 1024
SMEM = pl.BlockSpec(memory_space=pltpu.SMEM)
VMEM = pl.BlockSpec(memory_space=pltpu.VMEM)


def log2(size):
    return size.bit_length() - 1


def list_width(slots):
    return -(-(slots + 2 * UNROLL + 8) // LANES) * LANES


def make_lists(orders, per, col_bits, count, codes, words_ref):
    slots, width = codes.shape[1], words_ref.shape[1]
    chunks = len(orders)
    small = per // chunks
    half = small << (len(orders[0]) - 1)
    row_block, col_block = codes >> col_bits, codes & ((1 << col_bits) - 1)
    owner = (row_block >> log2(per)) ^ lax.axis_index("col")
    sub = row_block & (per - 1)
    chunk, rest = sub >> log2(small), sub & (small - 1)
    number = lax.broadcasted_iota(jnp.int32, (1, slots), 1)
    same = lax.broadcasted_iota(jnp.int32, (slots, slots), 0) == lax.broadcasted_iota(jnp.int32, (slots, slots), 1)
    column = lambda row: jnp.sum(jnp.where(same, row, 0.0), axis=1, keepdims=True)
    spot = lax.broadcasted_iota(jnp.int32, (slots, width), 1).astype(jnp.float32)
    lane = lax.broadcasted_iota(jnp.int32, (1, width), 1)
    chosen = jnp.zeros_like(owner)
    for order in sorted(set(orders)):
        place = jnp.zeros_like(owner)
        for k, bit in enumerate(order):
            place = place | (((owner >> bit) & 1) << (len(order) - 1 - k))
        for i in range(chunks):
            if orders[i] == order:
                chosen = jnp.where(chunk == i, place, chosen)
    place = (chosen << log2(small)) + rest
    keep = place < half
    target = jnp.where(keep, chunk * half + place, place - half)
    group = jnp.where(number < count, jnp.where(keep, chunks, chunk), chunks + 1)
    key = (group * slots + number).astype(jnp.float32)
    word = ((number << SLOT_AT) | (col_block << SOURCE_AT) | target).astype(jnp.float32)
    rank = jnp.sum(jnp.where(key < column(key), 1.0, 0.0), axis=1, keepdims=True)
    words = jnp.sum(jnp.where(rank == spot, column(word), 0.0), axis=0, keepdims=True).astype(jnp.int32)
    for k in range(chunks + 2):
        before = jnp.sum(jnp.where(group < k, 1.0, 0.0), axis=1, keepdims=True).astype(jnp.int32)
        words = jnp.where(lane == width - 8 + k, before, words)
    words_ref[...] = words


def relayout_kernel(orders, per, col_bits, count_ref, codes_hbm, values_hbm, out_ref, words_ref, codes, held, scratch, arrived, codes_arrived):
    codes_copy = pltpu.make_async_copy(codes_hbm, codes, codes_arrived)
    codes_copy.start()
    step = values_hbm.shape[0] // STEPS
    copies = []
    for k in range(STEPS):
        rows = pl.ds(k * step, step)
        copies.append(pltpu.make_async_copy(values_hbm.at[rows], held.at[rows], arrived.at[k]))
        copies[k].start()
    codes_copy.wait()
    make_lists(orders, per, col_bits, count_ref[0, 0], codes[...], words_ref)

    def one(g, carry):
        slots = pl.ds(pl.multiple_of(g * GROUP, GROUP), GROUP)
        base = pl.multiple_of(g * (GROUP * PAIR), GROUP * PAIR)
        for p in range(PAIR):
            scratch[pl.ds(base + p * GROUP, GROUP), :] = held[slots, p * LANES : (p + 1) * LANES].astype(jnp.float32)
        for s in range(GROUP):
            rows = scratch[pl.ds(base + s, PAIR, stride=GROUP), :]
            out_ref[pl.ds(base + s * PAIR, PAIR), :] = rows.astype(out_ref.dtype)
        return carry

    groups = step // GROUP
    for k in range(STEPS):
        copies[k].wait()
        lax.fori_loop(k * groups, (k + 1) * groups, one, 0, unroll=2)


def relayout(orders, per, col_bits, count, codes, values):
    slots = values.shape[0]
    return pl.pallas_call(
        functools.partial(relayout_kernel, orders, per, col_bits),
        in_specs=[SMEM] + [pl.BlockSpec(memory_space=pltpu.HBM)] * 2,
        out_specs=(VMEM, VMEM),
        out_shape=(
            jax.ShapeDtypeStruct((slots * PAIR, LANES), values.dtype),
            jax.ShapeDtypeStruct((1, list_width(slots)), jnp.int32),
        ),
        scratch_shapes=[
            pltpu.VMEM(codes.shape, codes.dtype),
            pltpu.VMEM(values.shape, values.dtype),
            pltpu.VMEM((slots * PAIR, LANES), jnp.float32),
            pltpu.SemaphoreType.DMA((STEPS,)),
            pltpu.SemaphoreType.DMA,
        ],
        cost_estimate=pl.CostEstimate(flops=0, bytes_accessed=4 * slots * BLK * BLK, transcendentals=0),
        compiler_params=pltpu.CompilerParams(vmem_limit_bytes=48 * MIB),
        name="relayout",
    )(count, codes, values)


def table_kernel(*refs):
    parts, table = refs[:-1], refs[-1]

    def build(q, carry):
        at = pl.ds(pl.multiple_of(q * LANES, LANES), LANES)
        x = [part[:, at].astype(jnp.float32) for part in parts]
        table[at, :] = jnp.concatenate(x, axis=0).T.astype(table.dtype)
        return carry

    lax.fori_loop(0, table.shape[0] // LANES, build, 0, unroll=4)


def make_table(parts):
    nodes = parts[0].shape[1]
    return pl.pallas_call(
        table_kernel,
        in_specs=[VMEM] * len(parts),
        out_specs=VMEM,
        out_shape=jax.ShapeDtypeStruct((nodes, LANES), jnp.bfloat16),
        compiler_params=pltpu.CompilerParams(vmem_limit_bytes=4 * MIB),
        cost_estimate=pl.CostEstimate(flops=0, bytes_accessed=nodes * LANES * 3, transcendentals=0),
        name="table",
    )(*parts)


def product_kernel(trash, group, words_ref, blocks_ref, table_ref, *outs):
    pending, acc = outs[-1], outs[-2]
    bounds = words_ref.shape[1] - 8 + group
    start, end = words_ref[0, bounds], words_ref[0, bounds + 1]
    acc[...] = jnp.zeros_like(acc)

    def add(first):
        for u in range(UNROLL):
            i = first + u
            word = words_ref[0, jnp.maximum(i, 0)]
            place = jnp.where((i >= start) & (i < end), word & ((1 << SOURCE_AT) - 1), trash)
            rows = pl.ds(pl.multiple_of(place * PAIR, PAIR), PAIR)
            acc[rows, :] = acc[rows, :] + pending[u * PAIR : (u + 1) * PAIR, :]

    def step(g, carry):
        first = start + g * UNROLL
        products = []
        for u in range(UNROLL):
            word = words_ref[0, first + u]
            block = blocks_ref[pl.ds(pl.multiple_of((word >> SLOT_AT) * PAIR, PAIR), PAIR), :]
            source = (word >> SOURCE_AT) & ((1 << (SLOT_AT - SOURCE_AT)) - 1)
            part = table_ref[pl.ds(pl.multiple_of(source * BLK, BLK), BLK), :]
            zero = jnp.zeros_like(part)
            right = jnp.concatenate([jnp.concatenate([part, zero], axis=1), jnp.concatenate([zero, part], axis=1)], axis=0)
            products.append(jnp.dot(block, right, preferred_element_type=jnp.float32))
        add(first - UNROLL)
        for u in range(UNROLL):
            pending[u * PAIR : (u + 1) * PAIR, :] = products[u]
        return carry

    groups = (end - start + (UNROLL - 1)) // UNROLL
    lax.fori_loop(0, groups, step, 0)
    add(start + (groups - 1) * UNROLL)
    if len(outs) > 2:
        outs[0][...] = acc[: trash * PAIR, :].astype(outs[0].dtype)


def product(group, words, blocks, table, trash, sent):
    full = jax.ShapeDtypeStruct(((trash + 1) * PAIR, 2 * LANES), jnp.float32)
    out = jax.ShapeDtypeStruct((trash * PAIR, 2 * LANES), jnp.bfloat16) if sent else full
    sums = [pltpu.VMEM(full.shape, full.dtype)] if sent else []
    return pl.pallas_call(
        functools.partial(product_kernel, trash, group),
        in_specs=[SMEM, VMEM, VMEM],
        out_specs=VMEM,
        out_shape=out,
        scratch_shapes=sums + [pltpu.VMEM((UNROLL * PAIR, 2 * LANES), jnp.float32)],
        compiler_params=pltpu.CompilerParams(vmem_limit_bytes=8 * MIB),
        cost_estimate=pl.CostEstimate(flops=1, bytes_accessed=1, transcendentals=0),
        name="product_send" if sent else "product_keep",
    )(words, blocks, table)


def add_kernel(keep_ref, got_ref, next_ref, send_ref):
    half = next_ref.shape[0]
    next_ref[...] = keep_ref[:half, :] + got_ref[:half, :].astype(jnp.float32)
    send_ref[...] = (keep_ref[half:, :] + got_ref[half:, :].astype(jnp.float32)).astype(send_ref.dtype)


def add_halves(keep, which, got):
    rows, lanes = got.shape
    block = lambda n, i: pl.BlockSpec((n, lanes), lambda _: (i, 0))
    return pl.pallas_call(
        add_kernel,
        grid=(1,),
        in_specs=[block(rows, which), block(rows, 0)],
        out_specs=(block(rows // 2, 0), block(rows // 2, 0)),
        out_shape=(
            jax.ShapeDtypeStruct((rows // 2, lanes), jnp.float32),
            jax.ShapeDtypeStruct((rows // 2, lanes), jnp.bfloat16),
        ),
        compiler_params=pltpu.CompilerParams(vmem_limit_bytes=4 * MIB),
        cost_estimate=pl.CostEstimate(flops=rows * lanes, bytes_accessed=MIB, transcendentals=0),
        name="add",
    )(keep, got)


def layer_kernel(index, *refs):
    sums, (weight_ref, bias_ref, out_ref, wide, left, right) = refs[:-6], refs[-6:]
    r = lax.axis_index("row")
    wide[...] = weight_ref[...].astype(jnp.float32)
    size = wide.shape[0] // len(index)
    pieces = [wide[pl.ds(pl.multiple_of((r ^ i) * size, size), size), :] for i in index]
    weight = jnp.concatenate(pieces, axis=0).astype(jnp.bfloat16)
    rows = sums[0].shape[0]
    for k in range(len(sums) // 2):
        keep, got = sums[2 * k], sums[2 * k + 1]
        aggregated = (keep[...] + got[...].astype(jnp.float32)).astype(jnp.bfloat16)
        for h in range(2):
            part = aggregated[:, h * LANES : (h + 1) * LANES]
            hidden = jnp.dot(part, weight, preferred_element_type=jnp.float32) + bias_ref[...]
            hidden = jnp.maximum(hidden, 0.0)
            left[pl.ds(2 * rows * k + h, rows, stride=2), :] = hidden[:, :LANES]
            right[pl.ds(2 * rows * k + h, rows, stride=2), :] = hidden[:, LANES:]
    out_ref[:, :LANES] = left[...].astype(out_ref.dtype)
    out_ref[:, LANES:] = right[...].astype(out_ref.dtype)


def layer(index, sums, weight, bias):
    rows = len(sums) * sums[0].shape[0]
    return pl.pallas_call(
        functools.partial(layer_kernel, index),
        out_shape=jax.ShapeDtypeStruct((rows, weight.shape[1]), jnp.bfloat16),
        scratch_shapes=[pltpu.VMEM(weight.shape, jnp.float32)] + [pltpu.VMEM((rows, LANES), jnp.float32)] * 2,
        compiler_params=pltpu.CompilerParams(vmem_limit_bytes=8 * MIB),
        name="layer",
    )(*sums, weight, bias)


def exchange(x, axis, size, bit):
    return lax.ppermute(x, axis, [(i, i ^ (1 << bit)) for i in range(size)])


def shards(n_row, n_col, features, block_codes, block_count, block_values, weight, bias):
    top, col_axis_bits = log2(n_row) - 1, list(range(log2(n_col)))
    col_blocks = features.shape[0] // BLK
    row_total = col_blocks * n_col // n_row
    per = row_total // n_col

    z_first, x_first = tuple(col_axis_bits[1:] + col_axis_bits[:1]), tuple(col_axis_bits)
    orders = (x_first, z_first, x_first, x_first)
    chunks = len(orders)
    half = row_total // (2 * chunks)

    mine = features.T
    other = exchange(mine, "row", n_row, top)
    blocks, words = relayout(orders, per, log2(col_blocks), block_count, block_codes, block_values[0])
    other, blocks = lax.optimization_barrier((other, blocks))
    parts, index = [mine, other], [0, 1 << top]
    for bit in range(top):
        parts = parts + [exchange(p, "row", n_row, bit) for p in parts]
        index = index + [i ^ (1 << bit) for i in index]

    table = make_table(parts)
    sends = [product(k, words, blocks, table, half, True) for k in range(chunks)]
    kept = product(chunks, words, blocks, table, chunks * half, False)
    keeps = [(kept, k) for k in range(chunks)]
    for k in range(len(col_axis_bits)):
        for i in range(chunks):
            got = exchange(sends[i], "col", n_col, orders[i][k])
            if k < len(col_axis_bits) - 1:
                total, sends[i] = add_halves(*keeps[i], got)
                keeps[i] = (total, 0)
            else:
                keeps[i], sends[i] = keeps[i][0], got
    sums = [x for i in range(chunks) for x in (keeps[i], sends[i])]
    return layer(tuple(index), sums, weight, bias[None, :])


def solution(mesh):
    in_specs = (P("col", "row"), P("row", "col"), P("row", "col"), P("row", "col", None), P(), P())
    out_specs = P(("row", "col"), None)
    body = functools.partial(shards, mesh.shape["row"], mesh.shape["col"])
    return jax.shard_map(body, mesh=mesh, in_specs=in_specs, out_specs=out_specs, check_vma=False)
```

```python
import functools

import jax
import jax.numpy as jnp
from jax import lax
from jax.experimental import pallas as pl
from jax.experimental.pallas import tpu as pltpu
from jax.sharding import PartitionSpec as P

BLK = 64
PAIR = BLK // 2
LANES = 2 * BLK
GROUP = 16
STEPS = 4
UNROLL = 16
SLOT_AT, SOURCE_AT = 13, 7
MIB = 1024 * 1024
SMEM = pl.BlockSpec(memory_space=pltpu.SMEM)
VMEM = pl.BlockSpec(memory_space=pltpu.VMEM)


def log2(size):
    return size.bit_length() - 1


def list_width(slots):
    return -(-(slots + 2 * UNROLL + 8) // LANES) * LANES


def make_lists(chunks, col_bits, count, codes, words_ref):
    slots, width = codes.shape[1], words_ref.shape[1]
    per = sum(size for size, _ in chunks)
    row_block, col_block = codes >> col_bits, codes & ((1 << col_bits) - 1)
    owner = (row_block >> log2(per)) ^ lax.axis_index("col")
    sub = row_block & (per - 1)
    number = lax.broadcasted_iota(jnp.int32, (1, slots), 1)
    live = number < count
    group, target = jnp.full_like(codes, len(chunks) + 1), jnp.zeros_like(codes)
    first, base = 0, 0
    for c, (size, order) in enumerate(chunks):
        place = jnp.zeros_like(owner)
        for k, bit in enumerate(order):
            place = place | (((owner >> bit) & 1) << (len(order) - 1 - k))
        place = (place << log2(size)) + (sub - first)
        half = size << (len(order) - 1)
        keep = place < half
        here = live & (sub >= first) & (sub < first + size)
        target = jnp.where(here, jnp.where(keep, place + base, place - half), target)
        group = jnp.where(here, jnp.where(keep, len(chunks), c), group)
        first, base = first + size, base + half
    same = lax.broadcasted_iota(jnp.int32, (slots, slots), 0) == lax.broadcasted_iota(jnp.int32, (slots, slots), 1)
    column = lambda row: jnp.sum(jnp.where(same, row, 0.0), axis=1, keepdims=True)
    spot = lax.broadcasted_iota(jnp.int32, (slots, width), 1).astype(jnp.float32)
    lane = lax.broadcasted_iota(jnp.int32, (1, width), 1)
    key = (group * slots + number).astype(jnp.float32)
    word = ((number << SLOT_AT) | (col_block << SOURCE_AT) | target).astype(jnp.float32)
    rank = jnp.sum(jnp.where(key < column(key), 1.0, 0.0), axis=1, keepdims=True)
    words = jnp.sum(jnp.where(rank == spot, column(word), 0.0), axis=0, keepdims=True).astype(jnp.int32)
    for k in range(len(chunks) + 2):
        before = jnp.sum(jnp.where(group < k, 1.0, 0.0), axis=1, keepdims=True).astype(jnp.int32)
        words = jnp.where(lane == width - 8 + k, before, words)
    words_ref[...] = words


def relayout_kernel(chunks, col_bits, count_ref, codes_hbm, values_hbm, out_ref, words_ref, codes, held, scratch, arrived, codes_arrived):
    codes_copy = pltpu.make_async_copy(codes_hbm, codes, codes_arrived)
    codes_copy.start()
    step = values_hbm.shape[0] // STEPS
    copies = []
    for k in range(STEPS):
        rows = pl.ds(k * step, step)
        copies.append(pltpu.make_async_copy(values_hbm.at[rows], held.at[rows], arrived.at[k]))
        copies[k].start()
    codes_copy.wait()
    make_lists(chunks, col_bits, count_ref[0, 0], codes[...], words_ref)

    def one(g, carry):
        slots = pl.ds(pl.multiple_of(g * GROUP, GROUP), GROUP)
        base = pl.multiple_of(g * (GROUP * PAIR), GROUP * PAIR)
        for p in range(PAIR):
            scratch[pl.ds(base + p * GROUP, GROUP), :] = held[slots, p * LANES : (p + 1) * LANES].astype(jnp.float32)
        for s in range(GROUP):
            rows = scratch[pl.ds(base + s, PAIR, stride=GROUP), :]
            out_ref[pl.ds(base + s * PAIR, PAIR), :] = rows.astype(out_ref.dtype)
        return carry

    groups = step // GROUP
    for k in range(STEPS):
        copies[k].wait()
        lax.fori_loop(k * groups, (k + 1) * groups, one, 0, unroll=2)


def relayout(chunks, col_bits, count, codes, values):
    slots = values.shape[0]
    return pl.pallas_call(
        functools.partial(relayout_kernel, chunks, col_bits),
        in_specs=[SMEM] + [pl.BlockSpec(memory_space=pltpu.HBM)] * 2,
        out_specs=(VMEM, VMEM),
        out_shape=(
            jax.ShapeDtypeStruct((slots * PAIR, LANES), values.dtype),
            jax.ShapeDtypeStruct((1, list_width(slots)), jnp.int32),
        ),
        scratch_shapes=[
            pltpu.VMEM(codes.shape, codes.dtype),
            pltpu.VMEM(values.shape, values.dtype),
            pltpu.VMEM((slots * PAIR, LANES), jnp.float32),
            pltpu.SemaphoreType.DMA((STEPS,)),
            pltpu.SemaphoreType.DMA,
        ],
        cost_estimate=pl.CostEstimate(flops=0, bytes_accessed=4 * slots * BLK * BLK, transcendentals=0),
        compiler_params=pltpu.CompilerParams(vmem_limit_bytes=48 * MIB),
        name="relayout",
    )(count, codes, values)


def table_kernel(*refs):
    parts, table = refs[:-1], refs[-1]

    def build(q, carry):
        at = pl.ds(pl.multiple_of(q * LANES, LANES), LANES)
        x = [part[:, at].astype(jnp.float32) for part in parts]
        table[at, :] = jnp.concatenate(x + x, axis=0).T.astype(table.dtype)
        return carry

    lax.fori_loop(0, table.shape[0] // LANES, build, 0, unroll=4)


def make_table(parts):
    nodes = parts[0].shape[1]
    return pl.pallas_call(
        table_kernel,
        in_specs=[VMEM] * len(parts),
        out_specs=VMEM,
        out_shape=jax.ShapeDtypeStruct((nodes, LANES), jnp.bfloat16),
        compiler_params=pltpu.CompilerParams(vmem_limit_bytes=4 * MIB),
        cost_estimate=pl.CostEstimate(flops=1, bytes_accessed=1, transcendentals=0),
        name="table",
    )(*parts)


def product_kernel(trash, group, n_tables, words_ref, blocks_ref, *refs):
    tables, outs = refs[:n_tables], refs[n_tables:]
    pending, acc = outs[-1], outs[-2]
    bounds = words_ref.shape[1] - 8 + group
    start, end = words_ref[0, bounds], words_ref[0, bounds + 1]
    low = lax.broadcasted_iota(jnp.int32, (BLK, LANES), 1) < BLK
    acc[...] = jnp.zeros_like(acc)

    def add(first):
        for u in range(UNROLL):
            i = first + u
            word = words_ref[0, jnp.maximum(i, 0)]
            place = jnp.where((i >= start) & (i < end), word & ((1 << SOURCE_AT) - 1), trash)
            rows = pl.ds(pl.multiple_of(place * PAIR, PAIR), PAIR)
            acc[rows, :] = acc[rows, :] + pending[u * PAIR : (u + 1) * PAIR, :]

    def step(g, carry):
        first = start + g * UNROLL
        products = []
        for u in range(UNROLL):
            word = words_ref[0, first + u]
            block = blocks_ref[pl.ds(pl.multiple_of((word >> SLOT_AT) * PAIR, PAIR), PAIR), :]
            source = (word >> SOURCE_AT) & ((1 << (SLOT_AT - SOURCE_AT)) - 1)
            right = []
            for table in tables:
                part = table[pl.ds(pl.multiple_of(source * BLK, BLK), BLK), :]
                zero = jnp.zeros_like(part)
                right.append(jnp.concatenate([jnp.where(low, part, zero), jnp.where(low, zero, part)], axis=0))
            products.append(jnp.dot(block, jnp.concatenate(right, axis=1), preferred_element_type=jnp.float32))
        add(first - UNROLL)
        for u in range(UNROLL):
            pending[u * PAIR : (u + 1) * PAIR, :] = products[u]
        return carry

    groups = (end - start + (UNROLL - 1)) // UNROLL
    lax.fori_loop(0, groups, step, 0)
    add(start + (groups - 1) * UNROLL)
    if len(outs) > 2:
        outs[0][...] = acc[: trash * PAIR, :].astype(outs[0].dtype)


def product(group, words, blocks, tables, trash, sent):
    lanes = LANES * len(tables)
    full = jax.ShapeDtypeStruct(((trash + 1) * PAIR, lanes), jnp.float32)
    out = jax.ShapeDtypeStruct((trash * PAIR, lanes), jnp.bfloat16) if sent else full
    sums = [pltpu.VMEM(full.shape, full.dtype)] if sent else []
    return pl.pallas_call(
        functools.partial(product_kernel, trash, group, len(tables)),
        in_specs=[SMEM, VMEM] + [VMEM] * len(tables),
        out_specs=VMEM,
        out_shape=out,
        scratch_shapes=sums + [pltpu.VMEM((UNROLL * PAIR, lanes), jnp.float32)],
        compiler_params=pltpu.CompilerParams(vmem_limit_bytes=8 * MIB),
        cost_estimate=pl.CostEstimate(flops=1, bytes_accessed=1, transcendentals=0),
        name="product_send" if sent else "product_keep",
    )(words, blocks, *tables)


def add_kernel(keep_ref, *refs):
    parts, (next_ref, send_ref) = refs[:-2], refs[-2:]
    half, lanes = next_ref.shape[0], parts[0].shape[1]
    for i, got_ref in enumerate(parts):
        at = slice(i * lanes, (i + 1) * lanes)
        next_ref[:, at] = keep_ref[:half, at] + got_ref[:half, :].astype(jnp.float32)
        send_ref[:, at] = (keep_ref[half:, at] + got_ref[half:, :].astype(jnp.float32)).astype(send_ref.dtype)


def add_halves(keep, which, got):
    rows, lanes = got[0].shape[0], keep.shape[1]
    block = lambda n, lanes, i: pl.BlockSpec((n, lanes), lambda _: (i, 0))
    return pl.pallas_call(
        add_kernel,
        grid=(1,),
        in_specs=[block(rows, lanes, which)] + [block(*g.shape, 0) for g in got],
        out_specs=(block(rows // 2, lanes, 0), block(rows // 2, lanes, 0)),
        out_shape=(
            jax.ShapeDtypeStruct((rows // 2, lanes), jnp.float32),
            jax.ShapeDtypeStruct((rows // 2, lanes), jnp.bfloat16),
        ),
        compiler_params=pltpu.CompilerParams(vmem_limit_bytes=8 * MIB),
        cost_estimate=pl.CostEstimate(flops=rows * lanes, bytes_accessed=MIB, transcendentals=0),
        name="add",
    )(keep, *got)


def layer_kernel(index, *refs):
    sums, (weight_ref, bias_ref, out_ref, wide, left, right) = refs[:-6], refs[-6:]
    r = lax.axis_index("row")
    wide[...] = weight_ref[...].astype(jnp.float32)
    size = wide.shape[0] // (2 * len(index[0]))
    halves = []
    for pieces in index:
        rows = [wide[pl.ds(pl.multiple_of((r ^ i) * size, size), size), :] for i in pieces]
        halves.append(jnp.concatenate(rows, axis=0).astype(jnp.bfloat16))
    zero = jnp.zeros_like(halves[0])
    even = jnp.concatenate([halves[0], zero, halves[1], zero], axis=0)
    odd = jnp.concatenate([zero, halves[0], zero, halves[1]], axis=0)
    base = 0
    for k in range(len(sums) // 2):
        keep, got = sums[2 * k], sums[2 * k + 1]
        aggregated = (keep[...] + got[...].astype(jnp.float32)).astype(jnp.bfloat16)
        rows = got.shape[0]
        for h, w in enumerate((even, odd)):
            hidden = jnp.dot(aggregated, w, preferred_element_type=jnp.float32) + bias_ref[...]
            hidden = jnp.maximum(hidden, 0.0)
            left[pl.ds(base + h, rows, stride=2), :] = hidden[:, :LANES]
            right[pl.ds(base + h, rows, stride=2), :] = hidden[:, LANES:]
        base += 2 * rows
    out_ref[:, :LANES] = left[...].astype(out_ref.dtype)
    out_ref[:, LANES:] = right[...].astype(out_ref.dtype)


def layer(index, sums, weight, bias):
    rows = sum(x.shape[0] for x in sums)
    return pl.pallas_call(
        functools.partial(layer_kernel, index),
        out_shape=jax.ShapeDtypeStruct((rows, weight.shape[1]), jnp.bfloat16),
        scratch_shapes=[pltpu.VMEM(weight.shape, jnp.float32)] + [pltpu.VMEM((rows, LANES), jnp.float32)] * 2,
        compiler_params=pltpu.CompilerParams(vmem_limit_bytes=8 * MIB),
        name="layer",
    )(*sums, weight, bias)


def exchange(x, axis, size, bit):
    return lax.ppermute(x, axis, [(i, i ^ (1 << bit)) for i in range(size)])


def shards(n_row, n_col, features, block_codes, block_count, block_values, weight, bias):
    top, col_axis_bits = log2(n_row) - 1, list(range(log2(n_col)))
    col_blocks = features.shape[0] // BLK
    row_total = col_blocks * n_col // n_row
    per = row_total // n_col

    z_first, x_first = tuple(col_axis_bits[1:] + col_axis_bits[:1]), tuple(col_axis_bits)
    chunks = ((per // 2, x_first), (per // 4, x_first), (per // 4, z_first))
    halves = [size * n_col // 2 for size, _ in chunks]

    def spread(pieces, index):
        for bit in range(top):
            pieces = pieces + [exchange(p, "row", n_row, bit) for p in pieces]
            index = index + [i ^ (1 << bit) for i in index]
        return pieces, index

    mine = features.T
    other = exchange(mine, "row", n_row, top)
    near, near_index = spread([mine], [0])
    blocks, words = relayout(chunks, log2(col_blocks), block_count, block_codes, block_values[0])

    tables = [make_table(near)]
    first = product(0, words, blocks, tables, halves[0], True)
    other, first = lax.optimization_barrier((other, first))
    far, far_index = spread([other], [1 << top])
    tables.append(make_table(far))
    sends = [(first, product(0, words, blocks, tables[1:], halves[0], True))]
    sends += [(product(k, words, blocks, tables, halves[k], True),) for k in (1, 2)]
    gots = [[exchange(s, "col", n_col, order[0]) for s in send] for send, (_, order) in zip(sends, chunks)]
    words, gots[0][0] = lax.optimization_barrier((words, gots[0][0]))
    kept = product(len(chunks), words, blocks, tables, sum(halves), False)
    keeps = [(kept, sum(halves[:k]) // halves[k]) for k in range(len(chunks))]
    for k in range(len(col_axis_bits)):
        for i, (_, order) in enumerate(chunks):
            got = gots[i] if k == 0 else [exchange(sends[i][0], "col", n_col, order[k])]
            if k < len(col_axis_bits) - 1:
                total, send = add_halves(*keeps[i], got)
                keeps[i], sends[i] = (total, 0), (send,)
            else:
                keeps[i], sends[i] = keeps[i][0], got[0]
    sums = [x for pair in zip(keeps, sends) for x in pair]
    return layer((near_index, far_index), sums, weight, bias[None, :])


def solution(mesh):
    in_specs = (P("col", "row"), P("row", "col"), P("row", "col"), P("row", "col", None), P(), P())
    out_specs = P(("row", "col"), None)
    body = functools.partial(shards, mesh.shape["row"], mesh.shape["col"])
    return jax.shard_map(body, mesh=mesh, in_specs=in_specs, out_specs=out_specs, check_vma=False)
```

```python
import functools

import jax
import jax.numpy as jnp
from jax import lax
from jax.experimental import pallas as pl
from jax.experimental.pallas import tpu as pltpu
from jax.sharding import PartitionSpec as P

BLK = 64
PAIR = BLK // 2
LANES = 2 * BLK
GROUP = 16
STEPS = 4
UNROLL = 16
SLOT_AT, SOURCE_AT = 13, 7
MIB = 1024 * 1024
SMEM = pl.BlockSpec(memory_space=pltpu.SMEM)
VMEM = pl.BlockSpec(memory_space=pltpu.VMEM)


def log2(size):
    return size.bit_length() - 1


def list_width(slots):
    return -(-(slots + 2 * UNROLL + 8) // LANES) * LANES


def make_lists(chunks, col_bits, count, codes, words_ref):
    slots, width = codes.shape[1], words_ref.shape[1]
    per = sum(size for size, _, _ in chunks)
    row_block, col_block = codes >> col_bits, codes & ((1 << col_bits) - 1)
    owner = (row_block >> log2(per)) ^ lax.axis_index("col")
    sub = row_block & (per - 1)
    number = lax.broadcasted_iota(jnp.int32, (1, slots), 1)
    live = number < count
    group, target = jnp.full_like(codes, len(chunks) + 1), jnp.zeros_like(codes)
    first = 0
    for c, (size, base, order) in enumerate(chunks):
        place = jnp.zeros_like(owner)
        for k, bit in enumerate(order):
            place = place | (((owner >> bit) & 1) << (len(order) - 1 - k))
        place = (place << log2(size)) + (sub - first)
        half = size << (len(order) - 1)
        keep = place < half
        here = live & (sub >= first) & (sub < first + size)
        target = jnp.where(here, jnp.where(keep, place + base, place - half), target)
        group = jnp.where(here, jnp.where(keep, len(chunks), c), group)
        first += size
    same = lax.broadcasted_iota(jnp.int32, (slots, slots), 0) == lax.broadcasted_iota(jnp.int32, (slots, slots), 1)
    column = lambda row: jnp.sum(jnp.where(same, row, 0.0), axis=1, keepdims=True)
    spot = lax.broadcasted_iota(jnp.int32, (slots, width), 1).astype(jnp.float32)
    lane = lax.broadcasted_iota(jnp.int32, (1, width), 1)
    key = (group * slots + number).astype(jnp.float32)
    word = ((number << SLOT_AT) | (col_block << SOURCE_AT) | target).astype(jnp.float32)
    rank = jnp.sum(jnp.where(key < column(key), 1.0, 0.0), axis=1, keepdims=True)
    words = jnp.sum(jnp.where(rank == spot, column(word), 0.0), axis=0, keepdims=True).astype(jnp.int32)
    for k in range(len(chunks) + 2):
        before = jnp.sum(jnp.where(group < k, 1.0, 0.0), axis=1, keepdims=True).astype(jnp.int32)
        words = jnp.where(lane == width - 8 + k, before, words)
    words_ref[...] = words


def relayout_kernel(chunks, col_bits, count_ref, codes_hbm, values_hbm, out_ref, words_ref, codes, held, scratch, arrived, codes_arrived):
    codes_copy = pltpu.make_async_copy(codes_hbm, codes, codes_arrived)
    codes_copy.start()
    step = values_hbm.shape[0] // STEPS
    copies = []
    for k in range(STEPS):
        rows = pl.ds(k * step, step)
        copies.append(pltpu.make_async_copy(values_hbm.at[rows], held.at[rows], arrived.at[k]))
        copies[k].start()
    codes_copy.wait()
    make_lists(chunks, col_bits, count_ref[0, 0], codes[...], words_ref)

    def one(g, carry):
        slots = pl.ds(pl.multiple_of(g * GROUP, GROUP), GROUP)
        base = pl.multiple_of(g * (GROUP * PAIR), GROUP * PAIR)
        for p in range(PAIR):
            scratch[pl.ds(base + p * GROUP, GROUP), :] = held[slots, p * LANES : (p + 1) * LANES].astype(jnp.float32)
        for s in range(GROUP):
            rows = scratch[pl.ds(base + s, PAIR, stride=GROUP), :]
            out_ref[pl.ds(base + s * PAIR, PAIR), :] = rows.astype(out_ref.dtype)
        return carry

    groups = step // GROUP
    for k in range(STEPS):
        copies[k].wait()
        lax.fori_loop(k * groups, (k + 1) * groups, one, 0, unroll=2)


def relayout(chunks, col_bits, count, codes, values):
    slots = values.shape[0]
    return pl.pallas_call(
        functools.partial(relayout_kernel, chunks, col_bits),
        in_specs=[SMEM] + [pl.BlockSpec(memory_space=pltpu.HBM)] * 2,
        out_specs=(VMEM, VMEM),
        out_shape=(
            jax.ShapeDtypeStruct((slots * PAIR, LANES), values.dtype),
            jax.ShapeDtypeStruct((1, list_width(slots)), jnp.int32),
        ),
        scratch_shapes=[
            pltpu.VMEM(codes.shape, codes.dtype),
            pltpu.VMEM(values.shape, values.dtype),
            pltpu.VMEM((slots * PAIR, LANES), jnp.float32),
            pltpu.SemaphoreType.DMA((STEPS,)),
            pltpu.SemaphoreType.DMA,
        ],
        cost_estimate=pl.CostEstimate(flops=0, bytes_accessed=4 * slots * BLK * BLK, transcendentals=0),
        compiler_params=pltpu.CompilerParams(vmem_limit_bytes=48 * MIB),
        name="relayout",
    )(count, codes, values)


def table_kernel(*refs):
    parts, table = refs[:-1], refs[-1]

    def build(q, carry):
        at = pl.ds(pl.multiple_of(q * LANES, LANES), LANES)
        x = [part[:, at].astype(jnp.float32) for part in parts]
        table[at, :] = jnp.concatenate(x + x, axis=0).T.astype(table.dtype)
        return carry

    lax.fori_loop(0, table.shape[0] // LANES, build, 0, unroll=4)


def make_table(parts):
    nodes = parts[0].shape[1]
    return pl.pallas_call(
        table_kernel,
        in_specs=[VMEM] * len(parts),
        out_specs=VMEM,
        out_shape=jax.ShapeDtypeStruct((nodes, LANES), jnp.bfloat16),
        compiler_params=pltpu.CompilerParams(vmem_limit_bytes=4 * MIB),
        cost_estimate=pl.CostEstimate(flops=1, bytes_accessed=1, transcendentals=0),
        name="table",
    )(*parts)


def product_kernel(trash, group, n_tables, words_ref, blocks_ref, *refs):
    tables, outs = refs[:n_tables], refs[n_tables:]
    pending, acc = outs[-1], outs[-2]
    bounds = words_ref.shape[1] - 8 + group
    start, end = words_ref[0, bounds], words_ref[0, bounds + 1]
    low = lax.broadcasted_iota(jnp.int32, (BLK, LANES), 1) < BLK
    acc[...] = jnp.zeros_like(acc)

    def add(first):
        for u in range(UNROLL):
            i = first + u
            word = words_ref[0, jnp.maximum(i, 0)]
            place = jnp.where((i >= start) & (i < end), word & ((1 << SOURCE_AT) - 1), trash)
            rows = pl.ds(pl.multiple_of(place * PAIR, PAIR), PAIR)
            acc[rows, :] = acc[rows, :] + pending[u * PAIR : (u + 1) * PAIR, :]

    def step(g, carry):
        first = start + g * UNROLL
        products = []
        for u in range(UNROLL):
            word = words_ref[0, first + u]
            block = blocks_ref[pl.ds(pl.multiple_of((word >> SLOT_AT) * PAIR, PAIR), PAIR), :]
            source = (word >> SOURCE_AT) & ((1 << (SLOT_AT - SOURCE_AT)) - 1)
            right = []
            for table in tables:
                part = table[pl.ds(pl.multiple_of(source * BLK, BLK), BLK), :]
                zero = jnp.zeros_like(part)
                right.append(jnp.concatenate([jnp.where(low, part, zero), jnp.where(low, zero, part)], axis=0))
            products.append(jnp.dot(block, jnp.concatenate(right, axis=1), preferred_element_type=jnp.float32))
        add(first - UNROLL)
        for u in range(UNROLL):
            pending[u * PAIR : (u + 1) * PAIR, :] = products[u]
        return carry

    groups = (end - start + (UNROLL - 1)) // UNROLL
    lax.fori_loop(0, groups, step, 0)
    add(start + (groups - 1) * UNROLL)
    if len(outs) > 2:
        outs[0][...] = acc[: trash * PAIR, :].astype(outs[0].dtype)


def product(group, words, blocks, tables, trash, sent):
    lanes = LANES * len(tables)
    full = jax.ShapeDtypeStruct(((trash + 1) * PAIR, lanes), jnp.float32)
    out = jax.ShapeDtypeStruct((trash * PAIR, lanes), jnp.bfloat16) if sent else full
    sums = [pltpu.VMEM(full.shape, full.dtype)] if sent else []
    return pl.pallas_call(
        functools.partial(product_kernel, trash, group, len(tables)),
        in_specs=[SMEM, VMEM] + [VMEM] * len(tables),
        out_specs=VMEM,
        out_shape=out,
        scratch_shapes=sums + [pltpu.VMEM((UNROLL * PAIR, lanes), jnp.float32)],
        compiler_params=pltpu.CompilerParams(vmem_limit_bytes=8 * MIB),
        cost_estimate=pl.CostEstimate(flops=1, bytes_accessed=1, transcendentals=0),
        name="product_send" if sent else "product_keep",
    )(words, blocks, *tables)


def add_kernel(keep_ref, *refs):
    parts, (next_ref, send_ref) = refs[:-2], refs[-2:]
    half, lanes = next_ref.shape[0], parts[0].shape[1]
    for i, got_ref in enumerate(parts):
        at = slice(i * lanes, (i + 1) * lanes)
        next_ref[:, at] = keep_ref[:half, at] + got_ref[:half, :].astype(jnp.float32)
        send_ref[:, at] = (keep_ref[half:, at] + got_ref[half:, :].astype(jnp.float32)).astype(send_ref.dtype)


def add_halves(keep, which, got):
    rows, lanes = got[0].shape[0], keep.shape[1]
    block = lambda n, lanes, i: pl.BlockSpec((n, lanes), lambda _: (i, 0))
    return pl.pallas_call(
        add_kernel,
        grid=(1,),
        in_specs=[block(rows, lanes, which)] + [block(*g.shape, 0) for g in got],
        out_specs=(block(rows // 2, lanes, 0), block(rows // 2, lanes, 0)),
        out_shape=(
            jax.ShapeDtypeStruct((rows // 2, lanes), jnp.float32),
            jax.ShapeDtypeStruct((rows // 2, lanes), jnp.bfloat16),
        ),
        compiler_params=pltpu.CompilerParams(vmem_limit_bytes=8 * MIB),
        cost_estimate=pl.CostEstimate(flops=rows * lanes, bytes_accessed=MIB, transcendentals=0),
        name="add",
    )(keep, *got)


def layer_kernel(index, *refs):
    sums, (weight_ref, bias_ref, out_ref, wide, left, right) = refs[:-6], refs[-6:]
    r = lax.axis_index("row")
    wide[...] = weight_ref[...].astype(jnp.float32)
    size = wide.shape[0] // (2 * len(index[0]))
    halves = []
    for pieces in index:
        rows = [wide[pl.ds(pl.multiple_of((r ^ i) * size, size), size), :] for i in pieces]
        halves.append(jnp.concatenate(rows, axis=0).astype(jnp.bfloat16))
    zero = jnp.zeros_like(halves[0])
    even = jnp.concatenate([halves[0], zero, halves[1], zero], axis=0)
    odd = jnp.concatenate([zero, halves[0], zero, halves[1]], axis=0)
    base = 0
    for k in range(len(sums) // 2):
        keep, got = sums[2 * k], sums[2 * k + 1]
        aggregated = (keep[...] + got[...].astype(jnp.float32)).astype(jnp.bfloat16)
        rows = got.shape[0]
        for h, w in enumerate((even, odd)):
            hidden = jnp.dot(aggregated, w, preferred_element_type=jnp.float32) + bias_ref[...]
            hidden = jnp.maximum(hidden, 0.0)
            left[pl.ds(base + h, rows, stride=2), :] = hidden[:, :LANES]
            right[pl.ds(base + h, rows, stride=2), :] = hidden[:, LANES:]
        base += 2 * rows
    out_ref[:, :LANES] = left[...].astype(out_ref.dtype)
    out_ref[:, LANES:] = right[...].astype(out_ref.dtype)


def layer(index, sums, weight, bias):
    rows = sum(x.shape[0] for x in sums)
    return pl.pallas_call(
        functools.partial(layer_kernel, index),
        out_shape=jax.ShapeDtypeStruct((rows, weight.shape[1]), jnp.bfloat16),
        scratch_shapes=[pltpu.VMEM(weight.shape, jnp.float32)] + [pltpu.VMEM((rows, LANES), jnp.float32)] * 2,
        compiler_params=pltpu.CompilerParams(vmem_limit_bytes=8 * MIB),
        name="layer",
    )(*sums, weight, bias)


def exchange(x, axis, size, bit):
    return lax.ppermute(x, axis, [(i, i ^ (1 << bit)) for i in range(size)])


def shards(n_row, n_col, features, block_codes, block_count, block_values, weight, bias):
    top, col_axis_bits = log2(n_row) - 1, list(range(log2(n_col)))
    col_blocks = features.shape[0] // BLK
    row_total = col_blocks * n_col // n_row
    per = row_total // n_col

    z_first, x_first = tuple(col_axis_bits[1:] + col_axis_bits[:1]), tuple(col_axis_bits)
    quarter = per // 4
    part = quarter * n_col // 2
    chunks = ((quarter, 2 * part, z_first), (2 * quarter, 0, x_first), (quarter, 3 * part, x_first))
    halves = [size * n_col // 2 for size, _, _ in chunks]

    def spread(pieces, index):
        for bit in range(top):
            pieces = pieces + [exchange(p, "row", n_row, bit) for p in pieces]
            index = index + [i ^ (1 << bit) for i in index]
        return pieces, index

    mine = features.T
    other = exchange(mine, "row", n_row, top)
    near, near_index = spread([mine], [0])
    blocks, words = relayout(chunks, log2(col_blocks), block_count, block_codes, block_values[0])

    tables = [make_table(near)]
    early = product(1, words, blocks, tables, halves[1], True)
    other, early = lax.optimization_barrier((other, early))
    far, far_index = spread([other], [1 << top])
    tables.append(make_table(far))
    sends = [(product(0, words, blocks, tables, halves[0], True),)]
    words, _ = lax.optimization_barrier((words, sends[0]))
    sends.append((early, product(1, words, blocks, tables[1:], halves[1], True)))
    sends.append((product(2, words, blocks, tables, halves[2], True),))
    gots = [[exchange(s, "col", n_col, order[0]) for s in send] for send, (_, _, order) in zip(sends, chunks)]
    words, _, gots[1][0] = lax.optimization_barrier((words, sends, gots[1][0]))
    kept = product(len(chunks), words, blocks, tables, sum(halves), False)
    keeps = [(kept, base // size) for (_, base, _), size in zip(chunks, halves)]
    stages = len(col_axis_bits)
    turns = sorted((2 * k + (0, 1, 2.5)[i], k, i) for k in range(stages - 1) for i in range(len(chunks)))
    for _, k, i in turns:
        got = gots[i]
        if i == 1:
            got, _ = lax.optimization_barrier((got, keeps[0][0]))
        total, send = add_halves(*keeps[i], got)
        keeps[i], gots[i] = (total, 0), [exchange(send, "col", n_col, chunks[i][2][k + 1])]
    keeps, sends = [keep for keep, _ in keeps], [got[0] for got in gots]
    sums = [x for pair in zip(keeps, sends) for x in pair]
    return layer((near_index, far_index), sums, weight, bias[None, :])


def solution(mesh):
    in_specs = (P("col", "row"), P("row", "col"), P("row", "col"), P("row", "col", None), P(), P())
    out_specs = P(("row", "col"), None)
    body = functools.partial(shards, mesh.shape["row"], mesh.shape["col"])
    return jax.shard_map(body, mesh=mesh, in_specs=in_specs, out_specs=out_specs, check_vma=False)
```

```python
import functools

import jax
import jax.numpy as jnp
from jax import lax
from jax.experimental import pallas as pl
from jax.experimental.pallas import tpu as pltpu
from jax.sharding import PartitionSpec as P

BLK = 64
PAIR = BLK // 2
LANES = 2 * BLK
GROUP = 16
TOGETHER = 4
UNROLL = 16
SLOT_AT, SOURCE_AT = 13, 7
MIB = 1024 * 1024
SMEM = pl.BlockSpec(memory_space=pltpu.SMEM)
VMEM = pl.BlockSpec(memory_space=pltpu.VMEM)


def log2(size):
    return size.bit_length() - 1


def list_width(slots):
    return -(-(slots + 2 * UNROLL + 8) // LANES) * LANES


def make_lists(chunks, col_bits, count, codes, words_ref):
    slots, width = codes.shape[1], words_ref.shape[1]
    per = sum(size for size, _ in chunks)
    row_block, col_block = codes >> col_bits, codes & ((1 << col_bits) - 1)
    owner = (row_block >> log2(per)) ^ lax.axis_index("col")
    sub = row_block & (per - 1)
    number = lax.broadcasted_iota(jnp.int32, (1, slots), 1)
    live = number < count
    group, target = jnp.full_like(codes, len(chunks) + 1), jnp.zeros_like(codes)
    first, base = 0, 0
    for c, (size, order) in enumerate(chunks):
        place = jnp.zeros_like(owner)
        for k, bit in enumerate(order):
            place = place | (((owner >> bit) & 1) << (len(order) - 1 - k))
        place = (place << log2(size)) + (sub - first)
        half = size << (len(order) - 1)
        keep = place < half
        here = live & (sub >= first) & (sub < first + size)
        target = jnp.where(here, jnp.where(keep, place + base, place - half), target)
        group = jnp.where(here, jnp.where(keep, len(chunks), c), group)
        first, base = first + size, base + half
    same = lax.broadcasted_iota(jnp.int32, (slots, slots), 0) == lax.broadcasted_iota(jnp.int32, (slots, slots), 1)
    column = lambda row: jnp.sum(jnp.where(same, row, 0.0), axis=1, keepdims=True)
    spot = lax.broadcasted_iota(jnp.int32, (slots, width), 1).astype(jnp.float32)
    lane = lax.broadcasted_iota(jnp.int32, (1, width), 1)
    key = (group * slots + number).astype(jnp.float32)
    word = ((number << SLOT_AT) | (col_block << SOURCE_AT) | target).astype(jnp.float32)
    rank = jnp.sum(jnp.where(key < column(key), 1.0, 0.0), axis=1, keepdims=True)
    words = jnp.sum(jnp.where(rank == spot, column(word), 0.0), axis=0, keepdims=True).astype(jnp.int32)
    for k in range(len(chunks) + 2):
        before = jnp.sum(jnp.where(group < k, 1.0, 0.0), axis=1, keepdims=True).astype(jnp.int32)
        words = jnp.where(lane == width - 8 + k, before, words)
    words_ref[...] = words


def relayout_kernel(chunks, col_bits, count_ref, codes_hbm, values_hbm, out_ref, words_ref, codes, held, scratch, arrived, codes_arrived):
    codes_copy = pltpu.make_async_copy(codes_hbm, codes, codes_arrived)
    codes_copy.start()
    step = GROUP * TOGETHER

    def copy(k):
        rows = pl.ds(pl.multiple_of(k * step, step), step)
        return pltpu.make_async_copy(values_hbm.at[rows], held.at[rows], arrived.at[k])

    steps = values_hbm.shape[0] // step
    for k in range(steps):
        copy(k).start()
    codes_copy.wait()
    make_lists(chunks, col_bits, count_ref[0, 0], codes[...], words_ref)

    def one(k, carry):
        copy(k).wait()
        for g in range(TOGETHER):
            slots = pl.ds(pl.multiple_of(k * step + g * GROUP, GROUP), GROUP)
            for p in range(PAIR):
                wide = held[slots, p * LANES : (p + 1) * LANES].astype(jnp.float32)
                scratch[(g * PAIR + p) * GROUP : (g * PAIR + p + 1) * GROUP, :] = wide
        for g in range(TOGETHER):
            for s in range(GROUP):
                rows = scratch[pl.ds(g * PAIR * GROUP + s, PAIR, stride=GROUP), :]
                at = pl.multiple_of((k * step + g * GROUP + s) * PAIR, PAIR)
                out_ref[pl.ds(at, PAIR), :] = rows.astype(out_ref.dtype)
        return carry

    lax.fori_loop(0, steps, one, 0)


def relayout(chunks, col_bits, count, codes, values):
    slots = values.shape[0]
    return pl.pallas_call(
        functools.partial(relayout_kernel, chunks, col_bits),
        in_specs=[SMEM] + [pl.BlockSpec(memory_space=pltpu.HBM)] * 2,
        out_specs=(VMEM, VMEM),
        out_shape=(
            jax.ShapeDtypeStruct((slots * PAIR, LANES), values.dtype),
            jax.ShapeDtypeStruct((1, list_width(slots)), jnp.int32),
        ),
        scratch_shapes=[
            pltpu.VMEM(codes.shape, codes.dtype),
            pltpu.VMEM(values.shape, values.dtype),
            pltpu.VMEM((TOGETHER * GROUP * PAIR, LANES), jnp.float32),
            pltpu.SemaphoreType.DMA((slots // (GROUP * TOGETHER),)),
            pltpu.SemaphoreType.DMA,
        ],
        cost_estimate=pl.CostEstimate(flops=0, bytes_accessed=4 * slots * BLK * BLK, transcendentals=0),
        compiler_params=pltpu.CompilerParams(vmem_limit_bytes=48 * MIB),
        name="relayout",
    )(count, codes, values)


def table_kernel(*refs):
    parts, table = refs[:-1], refs[-1]
    kind = table.dtype if parts[0].shape[0] % 16 == 0 else jnp.float32

    def build(q, carry):
        at = pl.ds(pl.multiple_of(q * LANES, LANES), LANES)
        x = [part[:, at].astype(kind) for part in parts]
        table[at, :] = jnp.concatenate(x + x, axis=0).T.astype(table.dtype)
        return carry

    lax.fori_loop(0, table.shape[0] // LANES, build, 0, unroll=4)


def make_table(parts):
    nodes = parts[0].shape[1]
    return pl.pallas_call(
        table_kernel,
        in_specs=[VMEM] * len(parts),
        out_specs=VMEM,
        out_shape=jax.ShapeDtypeStruct((nodes, LANES), jnp.bfloat16),
        compiler_params=pltpu.CompilerParams(vmem_limit_bytes=4 * MIB),
        cost_estimate=pl.CostEstimate(flops=1, bytes_accessed=1, transcendentals=0),
        name="table",
    )(*parts)


def product_kernel(trash, group, n_tables, words_ref, blocks_ref, *refs):
    tables, outs = refs[:n_tables], refs[n_tables:]
    pending, acc = outs[-1], outs[-2]
    bounds = words_ref.shape[1] - 8 + group
    start, end = words_ref[0, bounds], words_ref[0, bounds + 1]
    low = lax.broadcasted_iota(jnp.int32, (BLK, LANES), 1) < BLK
    acc[...] = jnp.zeros_like(acc)

    def add(first):
        for u in range(UNROLL):
            i = first + u
            word = words_ref[0, jnp.maximum(i, 0)]
            place = jnp.where((i >= start) & (i < end), word & ((1 << SOURCE_AT) - 1), trash)
            rows = pl.ds(pl.multiple_of(place * PAIR, PAIR), PAIR)
            acc[rows, :] = acc[rows, :] + pending[u * PAIR : (u + 1) * PAIR, :]

    def step(g, carry):
        first = start + g * UNROLL
        products = []
        for u in range(UNROLL):
            word = words_ref[0, first + u]
            block = blocks_ref[pl.ds(pl.multiple_of((word >> SLOT_AT) * PAIR, PAIR), PAIR), :]
            source = (word >> SOURCE_AT) & ((1 << (SLOT_AT - SOURCE_AT)) - 1)
            right = []
            for table in tables:
                part = table[pl.ds(pl.multiple_of(source * BLK, BLK), BLK), :]
                zero = jnp.zeros_like(part)
                right.append(jnp.concatenate([jnp.where(low, part, zero), jnp.where(low, zero, part)], axis=0))
            products.append(jnp.dot(block, jnp.concatenate(right, axis=1), preferred_element_type=jnp.float32))
        add(first - UNROLL)
        for u in range(UNROLL):
            pending[u * PAIR : (u + 1) * PAIR, :] = products[u]
        return carry

    groups = (end - start + (UNROLL - 1)) // UNROLL
    lax.fori_loop(0, groups, step, 0)
    add(start + (groups - 1) * UNROLL)
    if len(outs) > 2:
        outs[0][...] = acc[: trash * PAIR, :].astype(outs[0].dtype)


def product(group, words, blocks, tables, trash, sent):
    lanes = LANES * len(tables)
    full = jax.ShapeDtypeStruct(((trash + 1) * PAIR, lanes), jnp.float32)
    out = jax.ShapeDtypeStruct((trash * PAIR, lanes), jnp.bfloat16) if sent else full
    sums = [pltpu.VMEM(full.shape, full.dtype)] if sent else []
    return pl.pallas_call(
        functools.partial(product_kernel, trash, group, len(tables)),
        in_specs=[SMEM, VMEM] + [VMEM] * len(tables),
        out_specs=VMEM,
        out_shape=out,
        scratch_shapes=sums + [pltpu.VMEM((UNROLL * PAIR, lanes), jnp.float32)],
        compiler_params=pltpu.CompilerParams(vmem_limit_bytes=8 * MIB),
        cost_estimate=pl.CostEstimate(flops=1, bytes_accessed=1, transcendentals=0),
        name="product_send" if sent else "product_keep",
    )(words, blocks, *tables)


def add_kernel(keep_ref, *refs):
    parts, (next_ref, send_ref) = refs[:-2], refs[-2:]
    half, lanes = next_ref.shape[0], parts[0].shape[1]
    for i, got_ref in enumerate(parts):
        at = slice(i * lanes, (i + 1) * lanes)
        next_ref[:, at] = keep_ref[:half, at] + got_ref[:half, :].astype(jnp.float32)
        send_ref[:, at] = (keep_ref[half:, at] + got_ref[half:, :].astype(jnp.float32)).astype(send_ref.dtype)


def add_halves(keep, which, got):
    rows, lanes = got[0].shape[0], keep.shape[1]
    block = lambda n, lanes, i: pl.BlockSpec((n, lanes), lambda _: (i, 0))
    return pl.pallas_call(
        add_kernel,
        grid=(1,),
        in_specs=[block(rows, lanes, which)] + [block(*g.shape, 0) for g in got],
        out_specs=(block(rows // 2, lanes, 0), block(rows // 2, lanes, 0)),
        out_shape=(
            jax.ShapeDtypeStruct((rows // 2, lanes), jnp.float32),
            jax.ShapeDtypeStruct((rows // 2, lanes), jnp.bfloat16),
        ),
        compiler_params=pltpu.CompilerParams(vmem_limit_bytes=8 * MIB),
        cost_estimate=pl.CostEstimate(flops=rows * lanes, bytes_accessed=MIB, transcendentals=0),
        name="add",
    )(keep, *got)


def layer_kernel(index, *refs):
    sums, (weight_ref, bias_ref, out_ref, wide, left, right) = refs[:-6], refs[-6:]
    r = lax.axis_index("row")
    wide[...] = weight_ref[...].astype(jnp.float32)
    size = wide.shape[0] // (2 * len(index[0]))
    halves = []
    for pieces in index:
        rows = [wide[pl.ds(pl.multiple_of((r ^ i) * size, size), size), :] for i in pieces]
        halves.append(jnp.concatenate(rows, axis=0).astype(jnp.bfloat16))
    zero = jnp.zeros_like(halves[0])
    even = jnp.concatenate([halves[0], zero, halves[1], zero], axis=0)
    odd = jnp.concatenate([zero, halves[0], zero, halves[1]], axis=0)
    base = 0
    for k in range(len(sums) // 2):
        keep, got = sums[2 * k], sums[2 * k + 1]
        aggregated = (keep[...] + got[...].astype(jnp.float32)).astype(jnp.bfloat16)
        rows = got.shape[0]
        for h, w in enumerate((even, odd)):
            hidden = jnp.dot(aggregated, w, preferred_element_type=jnp.float32) + bias_ref[...]
            hidden = jnp.maximum(hidden, 0.0)
            left[pl.ds(base + h, rows, stride=2), :] = hidden[:, :LANES]
            right[pl.ds(base + h, rows, stride=2), :] = hidden[:, LANES:]
        base += 2 * rows
    out_ref[:, :LANES] = left[...].astype(out_ref.dtype)
    out_ref[:, LANES:] = right[...].astype(out_ref.dtype)


def layer(index, sums, weight, bias):
    rows = sum(x.shape[0] for x in sums)
    return pl.pallas_call(
        functools.partial(layer_kernel, index),
        out_shape=jax.ShapeDtypeStruct((rows, weight.shape[1]), jnp.bfloat16),
        scratch_shapes=[pltpu.VMEM(weight.shape, jnp.float32)] + [pltpu.VMEM((rows, LANES), jnp.float32)] * 2,
        compiler_params=pltpu.CompilerParams(vmem_limit_bytes=8 * MIB),
        name="layer",
    )(*sums, weight, bias)


def exchange(x, axis, size, bit):
    return lax.ppermute(x, axis, [(i, i ^ (1 << bit)) for i in range(size)])


def shards(n_row, n_col, features, block_codes, block_count, block_values, weight, bias):
    top, col_axis_bits = log2(n_row) - 1, list(range(log2(n_col)))
    col_blocks = features.shape[0] // BLK
    row_total = col_blocks * n_col // n_row
    per = row_total // n_col

    z_first, x_first = tuple(col_axis_bits[1:] + col_axis_bits[:1]), tuple(col_axis_bits)
    chunks = ((per // 2, x_first), (per // 4, x_first), (per // 4, z_first))
    halves = [size * n_col // 2 for size, _ in chunks]

    def spread(pieces, index):
        for bit in range(top):
            pieces = pieces + [exchange(p, "row", n_row, bit) for p in pieces]
            index = index + [i ^ (1 << bit) for i in index]
        return pieces, index

    mine = features.T
    other = exchange(mine, "row", n_row, top)
    near, near_index = spread([mine], [0])
    blocks, words = relayout(chunks, log2(col_blocks), block_count, block_codes, block_values[0])

    tables = [make_table(near)]
    first = product(0, words, blocks, tables, halves[0], True)
    other, first = lax.optimization_barrier((other, first))
    far, far_index = spread([other], [1 << top])
    tables.append(make_table(far))
    sends = [(first, product(0, words, blocks, tables[1:], halves[0], True))]
    sends += [(product(k, words, blocks, tables, halves[k], True),) for k in (1, 2)]
    gots = [[exchange(s, "col", n_col, order[0]) for s in send] for send, (_, order) in zip(sends, chunks)]
    words, gots[0][0] = lax.optimization_barrier((words, gots[0][0]))
    kept = product(len(chunks), words, blocks, tables, sum(halves), False)
    keeps = [(kept, sum(halves[:k]) // halves[k]) for k in range(len(chunks))]
    for k in range(len(col_axis_bits)):
        for i, (_, order) in enumerate(chunks):
            got = gots[i] if k == 0 else [exchange(sends[i][0], "col", n_col, order[k])]
            if k < len(col_axis_bits) - 1:
                total, send = add_halves(*keeps[i], got)
                keeps[i], sends[i] = (total, 0), (send,)
            else:
                keeps[i], sends[i] = keeps[i][0], got[0]
    sums = [x for pair in zip(keeps, sends) for x in pair]
    return layer((near_index, far_index), sums, weight, bias[None, :])


def solution(mesh):
    in_specs = (P("col", "row"), P("row", "col"), P("row", "col"), P("row", "col", None), P(), P())
    out_specs = P(("row", "col"), None)
    body = functools.partial(shards, mesh.shape["row"], mesh.shape["col"])
    return jax.shard_map(body, mesh=mesh, in_specs=in_specs, out_specs=out_specs, check_vma=False)
```

```python
import functools

import jax
import jax.numpy as jnp
from jax import lax
from jax.experimental import pallas as pl
from jax.experimental.pallas import tpu as pltpu
from jax.sharding import PartitionSpec as P

BLK = 64
PAIR = BLK // 2
LANES = 2 * BLK
GROUP = 16
TOGETHER = 4
UNROLL = 16
SLOT_AT, SOURCE_AT = 13, 7
MIB = 1024 * 1024
SMEM = pl.BlockSpec(memory_space=pltpu.SMEM)
VMEM = pl.BlockSpec(memory_space=pltpu.VMEM)


def log2(size):
    return size.bit_length() - 1


def list_width(slots):
    return -(-(slots + 2 * UNROLL + 8) // LANES) * LANES


def make_lists(chunks, col_bits, count, codes, words_ref):
    slots, width = codes.shape[1], words_ref.shape[1]
    per = sum(size for size, _ in chunks)
    row_block, col_block = codes >> col_bits, codes & ((1 << col_bits) - 1)
    owner = (row_block >> log2(per)) ^ lax.axis_index("col")
    sub = row_block & (per - 1)
    number = lax.broadcasted_iota(jnp.int32, (1, slots), 1)
    live = number < count
    group, target = jnp.full_like(codes, len(chunks) + 1), jnp.zeros_like(codes)
    first, base = 0, 0
    for c, (size, order) in enumerate(chunks):
        place = jnp.zeros_like(owner)
        for k, bit in enumerate(order):
            place = place | (((owner >> bit) & 1) << (len(order) - 1 - k))
        place = (place << log2(size)) + (sub - first)
        half = size << (len(order) - 1)
        keep = place < half
        here = live & (sub >= first) & (sub < first + size)
        target = jnp.where(here, jnp.where(keep, place + base, place - half), target)
        group = jnp.where(here, jnp.where(keep, len(chunks), c), group)
        first, base = first + size, base + half
    same = lax.broadcasted_iota(jnp.int32, (slots, slots), 0) == lax.broadcasted_iota(jnp.int32, (slots, slots), 1)
    column = lambda row: jnp.sum(jnp.where(same, row, 0.0), axis=1, keepdims=True)
    spot = lax.broadcasted_iota(jnp.int32, (slots, width), 1).astype(jnp.float32)
    lane = lax.broadcasted_iota(jnp.int32, (1, width), 1)
    key = (group * slots + number).astype(jnp.float32)
    word = ((number << SLOT_AT) | (col_block << SOURCE_AT) | target).astype(jnp.float32)
    rank = jnp.sum(jnp.where(key < column(key), 1.0, 0.0), axis=1, keepdims=True)
    words = jnp.sum(jnp.where(rank == spot, column(word), 0.0), axis=0, keepdims=True).astype(jnp.int32)
    for k in range(len(chunks) + 2):
        before = jnp.sum(jnp.where(group < k, 1.0, 0.0), axis=1, keepdims=True).astype(jnp.int32)
        words = jnp.where(lane == width - 8 + k, before, words)
    words_ref[...] = words


def relayout_kernel(chunks, col_bits, count_ref, codes_hbm, values_hbm, out_ref, words_ref, codes, held, scratch, arrived, codes_arrived):
    codes_copy = pltpu.make_async_copy(codes_hbm, codes, codes_arrived)
    codes_copy.start()
    step = GROUP * TOGETHER

    def copy(k):
        rows = pl.ds(pl.multiple_of(k * step, step), step)
        return pltpu.make_async_copy(values_hbm.at[rows], held.at[rows], arrived.at[k])

    steps = values_hbm.shape[0] // step
    for k in range(steps):
        copy(k).start()
    codes_copy.wait()
    make_lists(chunks, col_bits, count_ref[0, 0], codes[...], words_ref)

    def one(k, carry):
        copy(k).wait()
        for g in range(TOGETHER):
            slots = pl.ds(pl.multiple_of(k * step + g * GROUP, GROUP), GROUP)
            for p in range(PAIR):
                wide = held[slots, p * LANES : (p + 1) * LANES].astype(jnp.float32)
                scratch[(g * PAIR + p) * GROUP : (g * PAIR + p + 1) * GROUP, :] = wide
        for g in range(TOGETHER):
            for s in range(GROUP):
                rows = scratch[pl.ds(g * PAIR * GROUP + s, PAIR, stride=GROUP), :]
                at = pl.multiple_of((k * step + g * GROUP + s) * PAIR, PAIR)
                out_ref[pl.ds(at, PAIR), :] = rows.astype(out_ref.dtype)
        return carry

    lax.fori_loop(0, steps, one, 0)


def relayout(chunks, col_bits, count, codes, values):
    slots = values.shape[0]
    return pl.pallas_call(
        functools.partial(relayout_kernel, chunks, col_bits),
        in_specs=[SMEM] + [pl.BlockSpec(memory_space=pltpu.HBM)] * 2,
        out_specs=(VMEM, VMEM),
        out_shape=(
            jax.ShapeDtypeStruct((slots * PAIR, LANES), values.dtype),
            jax.ShapeDtypeStruct((1, list_width(slots)), jnp.int32),
        ),
        scratch_shapes=[
            pltpu.VMEM(codes.shape, codes.dtype),
            pltpu.VMEM(values.shape, values.dtype),
            pltpu.VMEM((TOGETHER * GROUP * PAIR, LANES), jnp.float32),
            pltpu.SemaphoreType.DMA((slots // (GROUP * TOGETHER),)),
            pltpu.SemaphoreType.DMA,
        ],
        cost_estimate=pl.CostEstimate(flops=0, bytes_accessed=4 * slots * BLK * BLK, transcendentals=0),
        compiler_params=pltpu.CompilerParams(vmem_limit_bytes=48 * MIB),
        name="relayout",
    )(count, codes, values)


def table_kernel(*refs):
    parts, table = refs[:-1], refs[-1]
    kind = table.dtype if parts[0].shape[0] % 16 == 0 else jnp.float32

    def build(q, carry):
        at = pl.ds(pl.multiple_of(q * LANES, LANES), LANES)
        x = [part[:, at].astype(kind) for part in parts]
        table[at, :] = jnp.concatenate(x + x, axis=0).T.astype(table.dtype)
        return carry

    lax.fori_loop(0, table.shape[0] // LANES, build, 0, unroll=4)


def make_table(parts):
    nodes = parts[0].shape[1]
    return pl.pallas_call(
        table_kernel,
        in_specs=[VMEM] * len(parts),
        out_specs=VMEM,
        out_shape=jax.ShapeDtypeStruct((nodes, LANES), jnp.bfloat16),
        compiler_params=pltpu.CompilerParams(vmem_limit_bytes=4 * MIB),
        cost_estimate=pl.CostEstimate(flops=1, bytes_accessed=1, transcendentals=0),
        name="table",
    )(*parts)


def product_kernel(trash, group, n_tables, words_ref, blocks_ref, *refs):
    tables, outs = refs[:n_tables], refs[n_tables:]
    pending, acc = outs[-1], outs[-2]
    bounds = words_ref.shape[1] - 8 + group
    start, end = words_ref[0, bounds], words_ref[0, bounds + 1]
    low = lax.broadcasted_iota(jnp.int32, (BLK, LANES), 1) < BLK
    acc[...] = jnp.zeros_like(acc)

    def add(first):
        for u in range(UNROLL):
            i = first + u
            word = words_ref[0, jnp.maximum(i, 0)]
            place = jnp.where((i >= start) & (i < end), word & ((1 << SOURCE_AT) - 1), trash)
            rows = pl.ds(pl.multiple_of(place * PAIR, PAIR), PAIR)
            acc[rows, :] = acc[rows, :] + pending[u * PAIR : (u + 1) * PAIR, :]

    def step(g, carry):
        first = start + g * UNROLL
        products = []
        for u in range(UNROLL):
            word = words_ref[0, first + u]
            block = blocks_ref[pl.ds(pl.multiple_of((word >> SLOT_AT) * PAIR, PAIR), PAIR), :]
            source = (word >> SOURCE_AT) & ((1 << (SLOT_AT - SOURCE_AT)) - 1)
            right = []
            for table in tables:
                part = table[pl.ds(pl.multiple_of(source * BLK, BLK), BLK), :]
                zero = jnp.zeros_like(part)
                right.append(jnp.concatenate([jnp.where(low, part, zero), jnp.where(low, zero, part)], axis=0))
            products.append(jnp.dot(block, jnp.concatenate(right, axis=1), preferred_element_type=jnp.float32))
        add(first - UNROLL)
        for u in range(UNROLL):
            pending[u * PAIR : (u + 1) * PAIR, :] = products[u]
        return carry

    groups = (end - start + (UNROLL - 1)) // UNROLL
    lax.fori_loop(0, groups, step, 0)
    add(start + (groups - 1) * UNROLL)
    if len(outs) > 2:
        outs[0][...] = acc[: trash * PAIR, :].astype(outs[0].dtype)


def product(group, words, blocks, tables, trash, sent):
    lanes = LANES * len(tables)
    full = jax.ShapeDtypeStruct(((trash + 1) * PAIR, lanes), jnp.float32)
    out = jax.ShapeDtypeStruct((trash * PAIR, lanes), jnp.bfloat16) if sent else full
    sums = [pltpu.VMEM(full.shape, full.dtype)] if sent else []
    return pl.pallas_call(
        functools.partial(product_kernel, trash, group, len(tables)),
        in_specs=[SMEM, VMEM] + [VMEM] * len(tables),
        out_specs=VMEM,
        out_shape=out,
        scratch_shapes=sums + [pltpu.VMEM((UNROLL * PAIR, lanes), jnp.float32)],
        compiler_params=pltpu.CompilerParams(vmem_limit_bytes=8 * MIB),
        cost_estimate=pl.CostEstimate(flops=1, bytes_accessed=1, transcendentals=0),
        name="product_send" if sent else "product_keep",
    )(words, blocks, *tables)


def add_kernel(keep_ref, *refs):
    parts, (next_ref, send_ref) = refs[:-2], refs[-2:]
    half, lanes = next_ref.shape[0], parts[0].shape[1]
    for i, got_ref in enumerate(parts):
        at = slice(i * lanes, (i + 1) * lanes)
        next_ref[:, at] = keep_ref[:half, at] + got_ref[:half, :].astype(jnp.float32)
        send_ref[:, at] = (keep_ref[half:, at] + got_ref[half:, :].astype(jnp.float32)).astype(send_ref.dtype)


def add_halves(keep, which, got):
    rows, lanes = got[0].shape[0], keep.shape[1]
    block = lambda n, lanes, i: pl.BlockSpec((n, lanes), lambda _: (i, 0))
    return pl.pallas_call(
        add_kernel,
        grid=(1,),
        in_specs=[block(rows, lanes, which)] + [block(*g.shape, 0) for g in got],
        out_specs=(block(rows // 2, lanes, 0), block(rows // 2, lanes, 0)),
        out_shape=(
            jax.ShapeDtypeStruct((rows // 2, lanes), jnp.float32),
            jax.ShapeDtypeStruct((rows // 2, lanes), jnp.bfloat16),
        ),
        compiler_params=pltpu.CompilerParams(vmem_limit_bytes=8 * MIB),
        cost_estimate=pl.CostEstimate(flops=rows * lanes, bytes_accessed=MIB, transcendentals=0),
        name="add",
    )(keep, *got)


def layer_kernel(index, *refs):
    sums, (weight_ref, bias_ref, out_ref, wide, left, right) = refs[:-6], refs[-6:]
    r = lax.axis_index("row")
    wide[...] = weight_ref[...].astype(jnp.float32)
    size = wide.shape[0] // (2 * len(index[0]))
    halves = []
    for pieces in index:
        rows = [wide[pl.ds(pl.multiple_of((r ^ i) * size, size), size), :] for i in pieces]
        halves.append(jnp.concatenate(rows, axis=0).astype(jnp.bfloat16))
    zero = jnp.zeros_like(halves[0])
    even = jnp.concatenate([halves[0], zero, halves[1], zero], axis=0)
    odd = jnp.concatenate([zero, halves[0], zero, halves[1]], axis=0)
    base = 0
    for k in range(len(sums) // 2):
        keep, got = sums[2 * k], sums[2 * k + 1]
        aggregated = (keep[...] + got[...].astype(jnp.float32)).astype(jnp.bfloat16)
        rows = got.shape[0]
        for h, w in enumerate((even, odd)):
            hidden = jnp.dot(aggregated, w, preferred_element_type=jnp.float32) + bias_ref[...]
            hidden = jnp.maximum(hidden, 0.0)
            left[pl.ds(base + h, rows, stride=2), :] = hidden[:, :LANES]
            right[pl.ds(base + h, rows, stride=2), :] = hidden[:, LANES:]
        base += 2 * rows
    out_ref[:, :LANES] = left[...].astype(out_ref.dtype)
    out_ref[:, LANES:] = right[...].astype(out_ref.dtype)


def layer(index, sums, weight, bias):
    rows = sum(x.shape[0] for x in sums)
    return pl.pallas_call(
        functools.partial(layer_kernel, index),
        out_shape=jax.ShapeDtypeStruct((rows, weight.shape[1]), jnp.bfloat16),
        scratch_shapes=[pltpu.VMEM(weight.shape, jnp.float32)] + [pltpu.VMEM((rows, LANES), jnp.float32)] * 2,
        compiler_params=pltpu.CompilerParams(vmem_limit_bytes=8 * MIB),
        name="layer",
    )(*sums, weight, bias)


def exchange(x, axis, size, bit):
    return lax.ppermute(x, axis, [(i, i ^ (1 << bit)) for i in range(size)])


def shards(n_row, n_col, features, block_codes, block_count, block_values, weight, bias):
    top, col_axis_bits = log2(n_row) - 1, list(range(log2(n_col)))
    col_blocks = features.shape[0] // BLK
    row_total = col_blocks * n_col // n_row
    per = row_total // n_col

    z_first, x_first = tuple(col_axis_bits[-1:] + col_axis_bits[:-1]), tuple(col_axis_bits)
    chunks = ((per // 2, x_first), (per // 4, x_first), (per // 4, z_first))
    halves = [size * n_col // 2 for size, _ in chunks]

    def spread(pieces, index):
        for bit in range(top):
            pieces = pieces + [exchange(p, "row", n_row, bit) for p in pieces]
            index = index + [i ^ (1 << bit) for i in index]
        return pieces, index

    mine = features.T
    other = exchange(mine, "row", n_row, top)
    near, near_index = spread([mine], [0])
    blocks, words = relayout(chunks, log2(col_blocks), block_count, block_codes, block_values[0])

    tables = [make_table(near)]
    first = product(0, words, blocks, tables, halves[0], True)
    other, first = lax.optimization_barrier((other, first))
    far, far_index = spread([other], [1 << top])
    tables.append(make_table(far))
    sends = [(first, product(0, words, blocks, tables[1:], halves[0], True))]
    sends += [(product(k, words, blocks, tables, halves[k], True),) for k in (1, 2)]
    gots = [[exchange(s, "col", n_col, order[0]) for s in send] for send, (_, order) in zip(sends, chunks)]
    words, gots[0][0] = lax.optimization_barrier((words, gots[0][0]))
    kept = product(len(chunks), words, blocks, tables, sum(halves), False)
    keeps = [(kept, sum(halves[:k]) // halves[k]) for k in range(len(chunks))]
    for k in range(len(col_axis_bits)):
        for i, (_, order) in enumerate(chunks):
            got = gots[i] if k == 0 else [exchange(sends[i][0], "col", n_col, order[k])]
            if k < len(col_axis_bits) - 1:
                total, send = add_halves(*keeps[i], got)
                keeps[i], sends[i] = (total, 0), (send,)
            else:
                keeps[i], sends[i] = keeps[i][0], got[0]
    sums = [x for pair in zip(keeps, sends) for x in pair]
    return layer((near_index, far_index), sums, weight, bias[None, :])


def solution(mesh):
    in_specs = (P("col", "row"), P("row", "col"), P("row", "col"), P("row", "col", None), P(), P())
    out_specs = P(("row", "col"), None)
    body = functools.partial(shards, mesh.shape["row"], mesh.shape["col"])
    return jax.shard_map(body, mesh=mesh, in_specs=in_specs, out_specs=out_specs, check_vma=False)
```

```python
import functools

import jax
import jax.numpy as jnp
from jax import lax
from jax.experimental import pallas as pl
from jax.experimental.pallas import tpu as pltpu
from jax.sharding import PartitionSpec as P

BLK = 64
PAIR = BLK // 2
LANES = 2 * BLK
GROUP = 16
TOGETHER = 4
UNROLL = 16
SLOT_AT, SOURCE_AT = 13, 7
MIB = 1024 * 1024
SMEM = pl.BlockSpec(memory_space=pltpu.SMEM)
VMEM = pl.BlockSpec(memory_space=pltpu.VMEM)


def log2(size):
    return size.bit_length() - 1


def list_width(slots):
    return -(-(slots + 2 * UNROLL + 8) // LANES) * LANES


def make_lists(chunks, col_bits, count, codes, words_ref):
    slots, width = codes.shape[1], words_ref.shape[1]
    per = sum(size for size, _ in chunks)
    row_block, col_block = codes >> col_bits, codes & ((1 << col_bits) - 1)
    owner = (row_block >> log2(per)) ^ lax.axis_index("col")
    sub = row_block & (per - 1)
    number = lax.broadcasted_iota(jnp.int32, (1, slots), 1)
    live = number < count
    group, target = jnp.full_like(codes, len(chunks) + 1), jnp.zeros_like(codes)
    first, base = 0, 0
    for c, (size, order) in enumerate(chunks):
        place = jnp.zeros_like(owner)
        for k, bit in enumerate(order):
            place = place | (((owner >> bit) & 1) << (len(order) - 1 - k))
        place = (place << log2(size)) + (sub - first)
        half = size << (len(order) - 1)
        keep = place < half
        here = live & (sub >= first) & (sub < first + size)
        target = jnp.where(here, jnp.where(keep, place + base, place - half), target)
        group = jnp.where(here, jnp.where(keep, len(chunks), c), group)
        first, base = first + size, base + half
    same = lax.broadcasted_iota(jnp.int32, (slots, slots), 0) == lax.broadcasted_iota(jnp.int32, (slots, slots), 1)
    column = lambda row: jnp.sum(jnp.where(same, row, 0.0), axis=1, keepdims=True)
    spot = lax.broadcasted_iota(jnp.int32, (slots, width), 1).astype(jnp.float32)
    lane = lax.broadcasted_iota(jnp.int32, (1, width), 1)
    key = (group * slots + number).astype(jnp.float32)
    word = ((number << SLOT_AT) | (col_block << SOURCE_AT) | target).astype(jnp.float32)
    rank = jnp.sum(jnp.where(key < column(key), 1.0, 0.0), axis=1, keepdims=True)
    words = jnp.sum(jnp.where(rank == spot, column(word), 0.0), axis=0, keepdims=True).astype(jnp.int32)
    for k in range(len(chunks) + 2):
        before = jnp.sum(jnp.where(group < k, 1.0, 0.0), axis=1, keepdims=True).astype(jnp.int32)
        words = jnp.where(lane == width - 8 + k, before, words)
    words_ref[...] = words


def relayout_kernel(chunks, col_bits, count_ref, codes_hbm, values_hbm, out_ref, words_ref, codes, held, scratch, arrived, codes_arrived):
    codes_copy = pltpu.make_async_copy(codes_hbm, codes, codes_arrived)
    codes_copy.start()
    step = GROUP * TOGETHER

    def copy(k):
        rows = pl.ds(pl.multiple_of(k * step, step), step)
        return pltpu.make_async_copy(values_hbm.at[rows], held.at[rows], arrived.at[k])

    steps = values_hbm.shape[0] // step
    for k in range(steps):
        copy(k).start()
    codes_copy.wait()
    make_lists(chunks, col_bits, count_ref[0, 0], codes[...], words_ref)

    def one(k, carry):
        copy(k).wait()
        for g in range(TOGETHER):
            slots = pl.ds(pl.multiple_of(k * step + g * GROUP, GROUP), GROUP)
            for p in range(PAIR):
                wide = held[slots, p * LANES : (p + 1) * LANES].astype(jnp.float32)
                scratch[(g * PAIR + p) * GROUP : (g * PAIR + p + 1) * GROUP, :] = wide
        for g in range(TOGETHER):
            for s in range(GROUP):
                rows = scratch[pl.ds(g * PAIR * GROUP + s, PAIR, stride=GROUP), :]
                at = pl.multiple_of((k * step + g * GROUP + s) * PAIR, PAIR)
                out_ref[pl.ds(at, PAIR), :] = rows.astype(out_ref.dtype)
        return carry

    lax.fori_loop(0, steps, one, 0)


def relayout(chunks, col_bits, count, codes, values):
    slots = values.shape[0]
    return pl.pallas_call(
        functools.partial(relayout_kernel, chunks, col_bits),
        in_specs=[SMEM] + [pl.BlockSpec(memory_space=pltpu.HBM)] * 2,
        out_specs=(VMEM, VMEM),
        out_shape=(
            jax.ShapeDtypeStruct((slots * PAIR, LANES), values.dtype),
            jax.ShapeDtypeStruct((1, list_width(slots)), jnp.int32),
        ),
        scratch_shapes=[
            pltpu.VMEM(codes.shape, codes.dtype),
            pltpu.VMEM(values.shape, values.dtype),
            pltpu.VMEM((TOGETHER * GROUP * PAIR, LANES), jnp.float32),
            pltpu.SemaphoreType.DMA((slots // (GROUP * TOGETHER),)),
            pltpu.SemaphoreType.DMA,
        ],
        cost_estimate=pl.CostEstimate(flops=0, bytes_accessed=4 * slots * BLK * BLK, transcendentals=0),
        compiler_params=pltpu.CompilerParams(vmem_limit_bytes=48 * MIB),
        name="relayout",
    )(count, codes, values)


def table_kernel(*refs):
    parts, table = refs[:-1], refs[-1]
    kind = table.dtype if parts[0].shape[0] % 16 == 0 else jnp.float32

    def build(q, carry):
        at = pl.ds(pl.multiple_of(q * LANES, LANES), LANES)
        x = [part[:, at].astype(kind) for part in parts]
        table[at, :] = jnp.concatenate(x + x, axis=0).T.astype(table.dtype)
        return carry

    lax.fori_loop(0, table.shape[0] // LANES, build, 0, unroll=4)


def make_table(parts):
    nodes = parts[0].shape[1]
    return pl.pallas_call(
        table_kernel,
        in_specs=[VMEM] * len(parts),
        out_specs=VMEM,
        out_shape=jax.ShapeDtypeStruct((nodes, LANES), jnp.bfloat16),
        compiler_params=pltpu.CompilerParams(vmem_limit_bytes=4 * MIB),
        cost_estimate=pl.CostEstimate(flops=1, bytes_accessed=1, transcendentals=0),
        name="table",
    )(*parts)


def product_kernel(trash, group, n_tables, words_ref, blocks_ref, *refs):
    tables, outs = refs[:n_tables], refs[n_tables:]
    pending, acc = outs[-1], outs[-2]
    bounds = words_ref.shape[1] - 8 + group
    start, end = words_ref[0, bounds], words_ref[0, bounds + 1]
    low = lax.broadcasted_iota(jnp.int32, (BLK, LANES), 1) < BLK
    acc[...] = jnp.zeros_like(acc)

    def add(first):
        for u in range(UNROLL):
            i = first + u
            word = words_ref[0, jnp.maximum(i, 0)]
            place = jnp.where((i >= start) & (i < end), word & ((1 << SOURCE_AT) - 1), trash)
            rows = pl.ds(pl.multiple_of(place * PAIR, PAIR), PAIR)
            acc[rows, :] = acc[rows, :] + pending[u * PAIR : (u + 1) * PAIR, :]

    def step(g, carry):
        first = start + g * UNROLL
        products = []
        for u in range(UNROLL):
            word = words_ref[0, first + u]
            block = blocks_ref[pl.ds(pl.multiple_of((word >> SLOT_AT) * PAIR, PAIR), PAIR), :]
            source = (word >> SOURCE_AT) & ((1 << (SLOT_AT - SOURCE_AT)) - 1)
            right = []
            for table in tables:
                part = table[pl.ds(pl.multiple_of(source * BLK, BLK), BLK), :]
                zero = jnp.zeros_like(part)
                right.append(jnp.concatenate([jnp.where(low, part, zero), jnp.where(low, zero, part)], axis=0))
            products.append(jnp.dot(block, jnp.concatenate(right, axis=1), preferred_element_type=jnp.float32))
        add(first - UNROLL)
        for u in range(UNROLL):
            pending[u * PAIR : (u + 1) * PAIR, :] = products[u]
        return carry

    groups = (end - start + (UNROLL - 1)) // UNROLL
    lax.fori_loop(0, groups, step, 0)
    add(start + (groups - 1) * UNROLL)
    if len(outs) > 2:
        outs[0][...] = acc[: trash * PAIR, :].astype(outs[0].dtype)


def product(group, words, blocks, tables, trash, sent):
    lanes = LANES * len(tables)
    full = jax.ShapeDtypeStruct(((trash + 1) * PAIR, lanes), jnp.float32)
    out = jax.ShapeDtypeStruct((trash * PAIR, lanes), jnp.bfloat16) if sent else full
    sums = [pltpu.VMEM(full.shape, full.dtype)] if sent else []
    return pl.pallas_call(
        functools.partial(product_kernel, trash, group, len(tables)),
        in_specs=[SMEM, VMEM] + [VMEM] * len(tables),
        out_specs=VMEM,
        out_shape=out,
        scratch_shapes=sums + [pltpu.VMEM((UNROLL * PAIR, lanes), jnp.float32)],
        compiler_params=pltpu.CompilerParams(vmem_limit_bytes=8 * MIB),
        cost_estimate=pl.CostEstimate(flops=1, bytes_accessed=1, transcendentals=0),
        name="product_send" if sent else "product_keep",
    )(words, blocks, *tables)


def add_kernel(*refs):
    parts, (next_ref, send_ref) = refs[:-2], refs[-2:]
    half, first = next_ref.shape[0], 0
    for keep_ref, got_ref in zip(parts[::2], parts[1::2]):
        at = slice(first, first + got_ref.shape[1])
        next_ref[:, at] = keep_ref[:half, :] + got_ref[:half, :].astype(jnp.float32)
        send_ref[:, at] = (keep_ref[half:, :] + got_ref[half:, :].astype(jnp.float32)).astype(send_ref.dtype)
        first = at.stop


def add_halves(parts):
    rows, lanes = parts[0][2].shape[0], sum(got.shape[1] for _, _, got in parts)
    block = lambda shape, place: pl.BlockSpec(shape, lambda _: place)
    specs = [s for _, place, got in parts for s in (block(got.shape, place), block(got.shape, (0, 0)))]
    half = (rows // 2, lanes)
    return pl.pallas_call(
        add_kernel,
        grid=(1,),
        in_specs=specs,
        out_specs=(block(half, (0, 0)),) * 2,
        out_shape=(jax.ShapeDtypeStruct(half, jnp.float32), jax.ShapeDtypeStruct(half, jnp.bfloat16)),
        compiler_params=pltpu.CompilerParams(vmem_limit_bytes=8 * MIB),
        cost_estimate=pl.CostEstimate(flops=rows * lanes, bytes_accessed=MIB, transcendentals=0),
        name="add",
    )(*[x for keep, _, got in parts for x in (keep, got)])


def layer_kernel(index, *refs):
    sums, (weight_ref, bias_ref, out_ref, wide, left, right) = refs[:-6], refs[-6:]
    r = lax.axis_index("row")
    wide[...] = weight_ref[...].astype(jnp.float32)
    size = wide.shape[0] // (2 * len(index[0]))
    halves = []
    for pieces in index:
        rows = [wide[pl.ds(pl.multiple_of((r ^ i) * size, size), size), :] for i in pieces]
        halves.append(jnp.concatenate(rows, axis=0).astype(jnp.bfloat16))
    zero = jnp.zeros_like(halves[0])
    even = jnp.concatenate([halves[0], zero, halves[1], zero], axis=0)
    odd = jnp.concatenate([zero, halves[0], zero, halves[1]], axis=0)
    base = 0
    for k in range(len(sums) // 2):
        keep, got = sums[2 * k], sums[2 * k + 1]
        aggregated = (keep[...] + got[...].astype(jnp.float32)).astype(jnp.bfloat16)
        rows = got.shape[0]
        for h, w in enumerate((even, odd)):
            hidden = jnp.dot(aggregated, w, preferred_element_type=jnp.float32) + bias_ref[...]
            hidden = jnp.maximum(hidden, 0.0)
            left[pl.ds(base + h, rows, stride=2), :] = hidden[:, :LANES]
            right[pl.ds(base + h, rows, stride=2), :] = hidden[:, LANES:]
        base += 2 * rows
    out_ref[:, :LANES] = left[...].astype(out_ref.dtype)
    out_ref[:, LANES:] = right[...].astype(out_ref.dtype)


def layer(index, sums, weight, bias):
    rows = sum(x.shape[0] for x in sums)
    return pl.pallas_call(
        functools.partial(layer_kernel, index),
        out_shape=jax.ShapeDtypeStruct((rows, weight.shape[1]), jnp.bfloat16),
        scratch_shapes=[pltpu.VMEM(weight.shape, jnp.float32)] + [pltpu.VMEM((rows, LANES), jnp.float32)] * 2,
        compiler_params=pltpu.CompilerParams(vmem_limit_bytes=8 * MIB),
        name="layer",
    )(*sums, weight, bias)


def exchange(x, axis, size, bit):
    return lax.ppermute(x, axis, [(i, i ^ (1 << bit)) for i in range(size)])


def shards(n_row, n_col, features, block_codes, block_count, block_values, weight, bias):
    top, col_axis_bits = log2(n_row) - 1, list(range(log2(n_col)))
    col_blocks = features.shape[0] // BLK
    row_total = col_blocks * n_col // n_row
    per = row_total // n_col

    z_first, x_first = tuple(col_axis_bits[1:] + col_axis_bits[:1]), tuple(col_axis_bits)
    chunks = ((per // 2, x_first), (per // 4, x_first), (per // 4, z_first))
    halves = [size * n_col // 2 for size, _ in chunks]

    def spread(pieces, index):
        for bit in range(top):
            pieces = pieces + [exchange(p, "row", n_row, bit) for p in pieces]
            index = index + [i ^ (1 << bit) for i in index]
        return pieces, index

    mine = features.T
    other = exchange(mine, "row", n_row, top)
    near, near_index = spread([mine], [0])
    blocks, words = relayout(chunks, log2(col_blocks), block_count, block_codes, block_values[0])

    tables = [make_table(near)]
    first = product(0, words, blocks, tables, halves[0], True)
    other, first = lax.optimization_barrier((other, first))
    far, far_index = spread([other], [1 << top])
    tables.append(make_table(far))
    sends = [(first, product(0, words, blocks, tables[1:], halves[0], True))]
    sends += [(product(k, words, blocks, tables, halves[k], True),) for k in (1, 2)]
    gots = [[exchange(s, "col", n_col, order[0]) for s in send] for send, (_, order) in zip(sends, chunks)]
    words, gots[0][0] = lax.optimization_barrier((words, gots[0][0]))
    kept = product(len(chunks), words, blocks, tables, sum(halves), False)
    kept_at = [sum(halves[:k]) // halves[k] for k in range(len(chunks))]
    parts = [[(kept, (at, f), got) for f, got in enumerate(g)] for at, g in zip(kept_at, gots)]
    for k in range(1, len(col_axis_bits)):
        for i, (_, order) in enumerate(chunks):
            joined = [[part] for part in parts[i]] if k == 1 else [parts[i]]
            sums = [add_halves(j) for j in joined]
            parts[i] = [(total, (0, 0), exchange(send, "col", n_col, order[k])) for total, send in sums]
    keeps, sends = [p[0][0] for p in parts], [p[0][2] for p in parts]
    sums = [x for pair in zip(keeps, sends) for x in pair]
    return layer((near_index, far_index), sums, weight, bias[None, :])


def solution(mesh):
    in_specs = (P("col", "row"), P("row", "col"), P("row", "col"), P("row", "col", None), P(), P())
    out_specs = P(("row", "col"), None)
    body = functools.partial(shards, mesh.shape["row"], mesh.shape["col"])
    return jax.shard_map(body, mesh=mesh, in_specs=in_specs, out_specs=out_specs, check_vma=False)
```

```python
import functools

import jax
import jax.numpy as jnp
from jax import lax
from jax.experimental import pallas as pl
from jax.experimental.pallas import tpu as pltpu
from jax.sharding import PartitionSpec as P

BLK = 64
PAIR = BLK // 2
LANES = 2 * BLK
GROUP = 16
TOGETHER = 4
UNROLL = 16
SLOT_AT, SOURCE_AT = 13, 7
MIB = 1024 * 1024
SMEM = pl.BlockSpec(memory_space=pltpu.SMEM)
VMEM = pl.BlockSpec(memory_space=pltpu.VMEM)


def log2(size):
    return size.bit_length() - 1


def list_width(slots):
    return -(-(slots + 2 * UNROLL + 8) // LANES) * LANES


def make_lists(chunks, col_bits, count, codes, words_ref):
    slots, width = codes.shape[1], words_ref.shape[1]
    per = sum(size for size, _ in chunks)
    row_block, col_block = codes >> col_bits, codes & ((1 << col_bits) - 1)
    owner = (row_block >> log2(per)) ^ lax.axis_index("col")
    sub = row_block & (per - 1)
    number = lax.broadcasted_iota(jnp.int32, (1, slots), 1)
    live = number < count
    group, target = jnp.full_like(codes, len(chunks) + 1), jnp.zeros_like(codes)
    first, base = 0, 0
    for c, (size, order) in enumerate(chunks):
        place = jnp.zeros_like(owner)
        for k, bit in enumerate(order):
            place = place | (((owner >> bit) & 1) << (len(order) - 1 - k))
        place = (place << log2(size)) + (sub - first)
        half = size << (len(order) - 1)
        keep = place < half
        here = live & (sub >= first) & (sub < first + size)
        target = jnp.where(here, jnp.where(keep, place + base, place - half), target)
        group = jnp.where(here, jnp.where(keep, len(chunks), c), group)
        first, base = first + size, base + half
    same = lax.broadcasted_iota(jnp.int32, (slots, slots), 0) == lax.broadcasted_iota(jnp.int32, (slots, slots), 1)
    column = lambda row: jnp.sum(jnp.where(same, row, 0.0), axis=1, keepdims=True)
    spot = lax.broadcasted_iota(jnp.int32, (slots, width), 1).astype(jnp.float32)
    lane = lax.broadcasted_iota(jnp.int32, (1, width), 1)
    key = (group * slots + number).astype(jnp.float32)
    word = ((number << SLOT_AT) | (col_block << SOURCE_AT) | target).astype(jnp.float32)
    rank = jnp.sum(jnp.where(key < column(key), 1.0, 0.0), axis=1, keepdims=True)
    words = jnp.sum(jnp.where(rank == spot, column(word), 0.0), axis=0, keepdims=True).astype(jnp.int32)
    for k in range(len(chunks) + 2):
        before = jnp.sum(jnp.where(group < k, 1.0, 0.0), axis=1, keepdims=True).astype(jnp.int32)
        words = jnp.where(lane == width - 8 + k, before, words)
    words_ref[...] = words


def relayout_kernel(chunks, col_bits, count_ref, codes_hbm, values_hbm, out_ref, words_ref, codes, held, scratch, arrived, codes_arrived):
    codes_copy = pltpu.make_async_copy(codes_hbm, codes, codes_arrived)
    codes_copy.start()
    step = GROUP * TOGETHER

    def copy(k):
        rows = pl.ds(pl.multiple_of(k * step, step), step)
        return pltpu.make_async_copy(values_hbm.at[rows], held.at[rows], arrived.at[k])

    steps = values_hbm.shape[0] // step
    for k in range(steps):
        copy(k).start()
    codes_copy.wait()
    make_lists(chunks, col_bits, count_ref[0, 0], codes[...], words_ref)

    def one(k, carry):
        copy(k).wait()
        for g in range(TOGETHER):
            slots = pl.ds(pl.multiple_of(k * step + g * GROUP, GROUP), GROUP)
            for p in range(PAIR):
                wide = held[slots, p * LANES : (p + 1) * LANES].astype(jnp.float32)
                scratch[(g * PAIR + p) * GROUP : (g * PAIR + p + 1) * GROUP, :] = wide
        for g in range(TOGETHER):
            for s in range(GROUP):
                rows = scratch[pl.ds(g * PAIR * GROUP + s, PAIR, stride=GROUP), :]
                at = pl.multiple_of((k * step + g * GROUP + s) * PAIR, PAIR)
                out_ref[pl.ds(at, PAIR), :] = rows.astype(out_ref.dtype)
        return carry

    lax.fori_loop(0, steps, one, 0)


def relayout(chunks, col_bits, count, codes, values):
    slots = values.shape[0]
    return pl.pallas_call(
        functools.partial(relayout_kernel, chunks, col_bits),
        in_specs=[SMEM] + [pl.BlockSpec(memory_space=pltpu.HBM)] * 2,
        out_specs=(VMEM, VMEM),
        out_shape=(
            jax.ShapeDtypeStruct((slots * PAIR, LANES), values.dtype),
            jax.ShapeDtypeStruct((1, list_width(slots)), jnp.int32),
        ),
        scratch_shapes=[
            pltpu.VMEM(codes.shape, codes.dtype),
            pltpu.VMEM(values.shape, values.dtype),
            pltpu.VMEM((TOGETHER * GROUP * PAIR, LANES), jnp.float32),
            pltpu.SemaphoreType.DMA((slots // (GROUP * TOGETHER),)),
            pltpu.SemaphoreType.DMA,
        ],
        cost_estimate=pl.CostEstimate(flops=0, bytes_accessed=4 * slots * BLK * BLK, transcendentals=0),
        compiler_params=pltpu.CompilerParams(vmem_limit_bytes=48 * MIB),
        name="relayout",
    )(count, codes, values)


def table_kernel(*refs):
    parts, table = refs[:-1], refs[-1]
    kind = table.dtype if parts[0].shape[0] % 16 == 0 else jnp.float32

    def build(q, carry):
        at = pl.ds(pl.multiple_of(q * LANES, LANES), LANES)
        x = [part[:, at].astype(kind) for part in parts]
        table[at, :] = jnp.concatenate(x + x, axis=0).T.astype(table.dtype)
        return carry

    lax.fori_loop(0, table.shape[0] // LANES, build, 0, unroll=4)


def make_table(parts):
    nodes = parts[0].shape[1]
    return pl.pallas_call(
        table_kernel,
        in_specs=[VMEM] * len(parts),
        out_specs=VMEM,
        out_shape=jax.ShapeDtypeStruct((nodes, LANES), jnp.bfloat16),
        compiler_params=pltpu.CompilerParams(vmem_limit_bytes=4 * MIB),
        cost_estimate=pl.CostEstimate(flops=1, bytes_accessed=1, transcendentals=0),
        name="table",
    )(*parts)


def product_kernel(trash, group, n_tables, words_ref, blocks_ref, *refs):
    tables, outs = refs[:n_tables], refs[n_tables:]
    pending, acc = outs[-1], outs[-2]
    bounds = words_ref.shape[1] - 8 + group
    start, end = words_ref[0, bounds], words_ref[0, bounds + 1]
    low = lax.broadcasted_iota(jnp.int32, (BLK, LANES), 1) < BLK
    acc[...] = jnp.zeros_like(acc)

    def add(first):
        for u in range(UNROLL):
            i = first + u
            word = words_ref[0, jnp.maximum(i, 0)]
            place = jnp.where((i >= start) & (i < end), word & ((1 << SOURCE_AT) - 1), trash)
            rows = pl.ds(pl.multiple_of(place * PAIR, PAIR), PAIR)
            acc[rows, :] = acc[rows, :] + pending[u * PAIR : (u + 1) * PAIR, :]

    def step(g, carry):
        first = start + g * UNROLL
        products = []
        for u in range(UNROLL):
            word = words_ref[0, first + u]
            block = blocks_ref[pl.ds(pl.multiple_of((word >> SLOT_AT) * PAIR, PAIR), PAIR), :]
            source = (word >> SOURCE_AT) & ((1 << (SLOT_AT - SOURCE_AT)) - 1)
            right = []
            for table in tables:
                part = table[pl.ds(pl.multiple_of(source * BLK, BLK), BLK), :]
                zero = jnp.zeros_like(part)
                right.append(jnp.concatenate([jnp.where(low, part, zero), jnp.where(low, zero, part)], axis=0))
            products.append(jnp.dot(block, jnp.concatenate(right, axis=1), preferred_element_type=jnp.float32))
        add(first - UNROLL)
        for u in range(UNROLL):
            pending[u * PAIR : (u + 1) * PAIR, :] = products[u]
        return carry

    groups = (end - start + (UNROLL - 1)) // UNROLL
    lax.fori_loop(0, groups, step, 0)
    add(start + (groups - 1) * UNROLL)
    if len(outs) > 2:
        outs[0][...] = acc[: trash * PAIR, :].astype(outs[0].dtype)


def product(group, words, blocks, tables, trash, sent):
    lanes = LANES * len(tables)
    full = jax.ShapeDtypeStruct(((trash + 1) * PAIR, lanes), jnp.float32)
    out = jax.ShapeDtypeStruct((trash * PAIR, lanes), jnp.bfloat16) if sent else full
    sums = [pltpu.VMEM(full.shape, full.dtype)] if sent else []
    return pl.pallas_call(
        functools.partial(product_kernel, trash, group, len(tables)),
        in_specs=[SMEM, VMEM] + [VMEM] * len(tables),
        out_specs=VMEM,
        out_shape=out,
        scratch_shapes=sums + [pltpu.VMEM((UNROLL * PAIR, lanes), jnp.float32)],
        compiler_params=pltpu.CompilerParams(vmem_limit_bytes=8 * MIB),
        cost_estimate=pl.CostEstimate(flops=1, bytes_accessed=1, transcendentals=0),
        name="product_send" if sent else "product_keep",
    )(words, blocks, *tables)


def add_kernel(keep_ref, got_ref, next_ref, send_ref):
    half = next_ref.shape[0]
    next_ref[...] = keep_ref[:half, :] + got_ref[:half, :].astype(jnp.float32)
    send_ref[...] = (keep_ref[half:, :] + got_ref[half:, :].astype(jnp.float32)).astype(send_ref.dtype)


def add_halves(keep, place, got):
    rows, lanes = got.shape
    half = (rows // 2, lanes)
    block = lambda shape, place: pl.BlockSpec(shape, lambda _: place)
    return pl.pallas_call(
        add_kernel,
        grid=(1,),
        in_specs=[block(got.shape, place), block(got.shape, (0, 0))],
        out_specs=(block(half, (0, 0)),) * 2,
        out_shape=(jax.ShapeDtypeStruct(half, jnp.float32), jax.ShapeDtypeStruct(half, jnp.bfloat16)),
        compiler_params=pltpu.CompilerParams(vmem_limit_bytes=8 * MIB),
        cost_estimate=pl.CostEstimate(flops=rows * lanes, bytes_accessed=MIB, transcendentals=0),
        name="add",
    )(keep, got)


def layer_kernel(index, counts, *refs):
    sums, (weight_ref, bias_ref, out_ref, wide, left, right) = list(refs[:-6]), refs[-6:]
    r = lax.axis_index("row")
    wide[...] = weight_ref[...].astype(jnp.float32)
    size = wide.shape[0] // (2 * len(index[0]))
    halves = []
    for pieces in index:
        rows = [wide[pl.ds(pl.multiple_of((r ^ i) * size, size), size), :] for i in pieces]
        halves.append(jnp.concatenate(rows, axis=0).astype(jnp.bfloat16))
    zero = jnp.zeros_like(halves[0])
    even = jnp.concatenate([halves[0], zero, halves[1], zero], axis=0)
    odd = jnp.concatenate([zero, halves[0], zero, halves[1]], axis=0)
    base = 0
    for count in counts:
        pairs = [(sums.pop(0), sums.pop(0)) for _ in range(count // 2)]
        aggregated = [(keep[...] + got[...].astype(jnp.float32)).astype(jnp.bfloat16) for keep, got in pairs]
        aggregated = jnp.concatenate(aggregated, axis=1)
        rows = aggregated.shape[0]
        for h, w in enumerate((even, odd)):
            hidden = jnp.dot(aggregated, w, preferred_element_type=jnp.float32) + bias_ref[...]
            hidden = jnp.maximum(hidden, 0.0)
            left[pl.ds(base + h, rows, stride=2), :] = hidden[:, :LANES]
            right[pl.ds(base + h, rows, stride=2), :] = hidden[:, LANES:]
        base += 2 * rows
    out_ref[:, :LANES] = left[...].astype(out_ref.dtype)
    out_ref[:, LANES:] = right[...].astype(out_ref.dtype)


def layer(index, sums, weight, bias):
    rows = sum(2 * part[0].shape[0] for part in sums)
    return pl.pallas_call(
        functools.partial(layer_kernel, index, [len(part) for part in sums]),
        out_shape=jax.ShapeDtypeStruct((rows, weight.shape[1]), jnp.bfloat16),
        scratch_shapes=[pltpu.VMEM(weight.shape, jnp.float32)] + [pltpu.VMEM((rows, LANES), jnp.float32)] * 2,
        compiler_params=pltpu.CompilerParams(vmem_limit_bytes=8 * MIB),
        name="layer",
    )(*[x for part in sums for x in part], weight, bias)


def exchange(x, axis, size, bit):
    return lax.ppermute(x, axis, [(i, i ^ (1 << bit)) for i in range(size)])


def shards(n_row, n_col, features, block_codes, block_count, block_values, weight, bias):
    top, col_axis_bits = log2(n_row) - 1, list(range(log2(n_col)))
    col_blocks = features.shape[0] // BLK
    row_total = col_blocks * n_col // n_row
    per = row_total // n_col

    z_first, x_first = tuple(col_axis_bits[1:] + col_axis_bits[:1]), tuple(col_axis_bits)
    chunks = ((per // 2, x_first), (per // 4, x_first), (per // 4, z_first))
    halves = [size * n_col // 2 for size, _ in chunks]

    def spread(pieces, index):
        for bit in range(top):
            pieces = pieces + [exchange(p, "row", n_row, bit) for p in pieces]
            index = index + [i ^ (1 << bit) for i in index]
        return pieces, index

    mine = features.T
    other = exchange(mine, "row", n_row, top)
    near, near_index = spread([mine], [0])
    blocks, words = relayout(chunks, log2(col_blocks), block_count, block_codes, block_values[0])

    tables = [make_table(near)]
    first = product(0, words, blocks, tables, halves[0], True)
    other, first = lax.optimization_barrier((other, first))
    far, far_index = spread([other], [1 << top])
    tables.append(make_table(far))
    sends = [(first, product(0, words, blocks, tables[1:], halves[0], True))]
    sends += [(product(k, words, blocks, tables, halves[k], True),) for k in (1, 2)]
    gots = [[exchange(s, "col", n_col, order[0]) for s in send] for send, (_, order) in zip(sends, chunks)]
    words, gots[0][0] = lax.optimization_barrier((words, gots[0][0]))
    kept = product(len(chunks), words, blocks, tables, sum(halves), False)
    kept_at = [sum(halves[:k]) // halves[k] for k in range(len(chunks))]
    parts = [[(kept, (at, f), got) for f, got in enumerate(g)] for at, g in zip(kept_at, gots)]
    for k in range(1, len(col_axis_bits)):
        for i, (_, order) in enumerate(chunks):
            sums = [add_halves(*part) for part in parts[i]]
            parts[i] = [(total, (0, 0), exchange(send, "col", n_col, order[k])) for total, send in sums]
    sums = [[x for keep, _, got in part for x in (keep, got)] for part in parts]
    return layer((near_index, far_index), sums, weight, bias[None, :])


def solution(mesh):
    in_specs = (P("col", "row"), P("row", "col"), P("row", "col"), P("row", "col", None), P(), P())
    out_specs = P(("row", "col"), None)
    body = functools.partial(shards, mesh.shape["row"], mesh.shape["col"])
    return jax.shard_map(body, mesh=mesh, in_specs=in_specs, out_specs=out_specs, check_vma=False)
```

```python
import functools

import jax
import jax.numpy as jnp
from jax import lax
from jax.experimental import pallas as pl
from jax.experimental.pallas import tpu as pltpu
from jax.sharding import PartitionSpec as P

BLK = 64
PAIR = BLK // 2
LANES = 2 * BLK
GROUP = 16
TOGETHER = 4
UNROLL = 16
SLOT_AT, SOURCE_AT = 13, 7
MIB = 1024 * 1024
SMEM = pl.BlockSpec(memory_space=pltpu.SMEM)
VMEM = pl.BlockSpec(memory_space=pltpu.VMEM)


def log2(size):
    return size.bit_length() - 1


def list_width(slots):
    return -(-(slots + 2 * UNROLL + 8) // LANES) * LANES


def make_lists(chunks, col_bits, count, codes, words_ref):
    slots, width = codes.shape[1], words_ref.shape[1]
    per = sum(size for size, _ in chunks)
    row_block, col_block = codes >> col_bits, codes & ((1 << col_bits) - 1)
    owner = (row_block >> log2(per)) ^ lax.axis_index("col")
    sub = row_block & (per - 1)
    number = lax.broadcasted_iota(jnp.int32, (1, slots), 1)
    live = number < count
    group, target = jnp.full_like(codes, len(chunks) + 1), jnp.zeros_like(codes)
    first, base = 0, 0
    for c, (size, order) in enumerate(chunks):
        place = jnp.zeros_like(owner)
        for k, bit in enumerate(order):
            place = place | (((owner >> bit) & 1) << (len(order) - 1 - k))
        place = (place << log2(size)) + (sub - first)
        half = size << (len(order) - 1)
        keep = place < half
        here = live & (sub >= first) & (sub < first + size)
        target = jnp.where(here, jnp.where(keep, place + base, place - half), target)
        group = jnp.where(here, jnp.where(keep, len(chunks), c), group)
        first, base = first + size, base + half
    same = lax.broadcasted_iota(jnp.int32, (slots, slots), 0) == lax.broadcasted_iota(jnp.int32, (slots, slots), 1)
    column = lambda row: jnp.sum(jnp.where(same, row, 0.0), axis=1, keepdims=True)
    spot = lax.broadcasted_iota(jnp.int32, (slots, width), 1).astype(jnp.float32)
    lane = lax.broadcasted_iota(jnp.int32, (1, width), 1)
    key = (group * slots + number).astype(jnp.float32)
    word = ((number << SLOT_AT) | (col_block << SOURCE_AT) | target).astype(jnp.float32)
    rank = jnp.sum(jnp.where(key < column(key), 1.0, 0.0), axis=1, keepdims=True)
    words = jnp.sum(jnp.where(rank == spot, column(word), 0.0), axis=0, keepdims=True).astype(jnp.int32)
    for k in range(len(chunks) + 2):
        before = jnp.sum(jnp.where(group < k, 1.0, 0.0), axis=1, keepdims=True).astype(jnp.int32)
        words = jnp.where(lane == width - 8 + k, before, words)
    words_ref[...] = words


def relayout_kernel(chunks, col_bits, count_ref, codes_hbm, values_hbm, out_ref, words_ref, codes, held, scratch, arrived, codes_arrived):
    codes_copy = pltpu.make_async_copy(codes_hbm, codes, codes_arrived)
    codes_copy.start()
    step = GROUP * TOGETHER

    def copy(k):
        rows = pl.ds(pl.multiple_of(k * step, step), step)
        return pltpu.make_async_copy(values_hbm.at[rows], held.at[rows], arrived.at[k])

    steps = values_hbm.shape[0] // step
    for k in range(steps):
        copy(k).start()
    codes_copy.wait()
    make_lists(chunks, col_bits, count_ref[0, 0], codes[...], words_ref)

    def one(k, carry):
        copy(k).wait()
        for g in range(TOGETHER):
            slots = pl.ds(pl.multiple_of(k * step + g * GROUP, GROUP), GROUP)
            for p in range(PAIR):
                wide = held[slots, p * LANES : (p + 1) * LANES].astype(jnp.float32)
                scratch[(g * PAIR + p) * GROUP : (g * PAIR + p + 1) * GROUP, :] = wide
        for g in range(TOGETHER):
            for s in range(GROUP):
                rows = scratch[pl.ds(g * PAIR * GROUP + s, PAIR, stride=GROUP), :]
                at = pl.multiple_of((k * step + g * GROUP + s) * PAIR, PAIR)
                out_ref[pl.ds(at, PAIR), :] = rows.astype(out_ref.dtype)
        return carry

    lax.fori_loop(0, steps, one, 0)


def relayout(chunks, col_bits, count, codes, values):
    slots = values.shape[0]
    return pl.pallas_call(
        functools.partial(relayout_kernel, chunks, col_bits),
        in_specs=[SMEM] + [pl.BlockSpec(memory_space=pltpu.HBM)] * 2,
        out_specs=(VMEM, VMEM),
        out_shape=(
            jax.ShapeDtypeStruct((slots * PAIR, LANES), values.dtype),
            jax.ShapeDtypeStruct((1, list_width(slots)), jnp.int32),
        ),
        scratch_shapes=[
            pltpu.VMEM(codes.shape, codes.dtype),
            pltpu.VMEM(values.shape, values.dtype),
            pltpu.VMEM((TOGETHER * GROUP * PAIR, LANES), jnp.float32),
            pltpu.SemaphoreType.DMA((slots // (GROUP * TOGETHER),)),
            pltpu.SemaphoreType.DMA,
        ],
        cost_estimate=pl.CostEstimate(flops=0, bytes_accessed=4 * slots * BLK * BLK, transcendentals=0),
        compiler_params=pltpu.CompilerParams(vmem_limit_bytes=48 * MIB),
        name="relayout",
    )(count, codes, values)


def table_kernel(*refs):
    parts, table = refs[:-1], refs[-1]
    kind = table.dtype if parts[0].shape[0] % 16 == 0 else jnp.float32

    def build(q, carry):
        at = pl.ds(pl.multiple_of(q * LANES, LANES), LANES)
        x = [part[:, at].astype(kind) for part in parts]
        table[at, :] = jnp.concatenate(x + x, axis=0).T.astype(table.dtype)
        return carry

    lax.fori_loop(0, table.shape[0] // LANES, build, 0, unroll=4)


def make_table(parts):
    nodes = parts[0].shape[1]
    return pl.pallas_call(
        table_kernel,
        in_specs=[VMEM] * len(parts),
        out_specs=VMEM,
        out_shape=jax.ShapeDtypeStruct((nodes, LANES), jnp.bfloat16),
        compiler_params=pltpu.CompilerParams(vmem_limit_bytes=4 * MIB),
        cost_estimate=pl.CostEstimate(flops=1, bytes_accessed=1, transcendentals=0),
        name="table",
    )(*parts)


def product_kernel(trash, group, n_tables, words_ref, blocks_ref, *refs):
    tables, outs = refs[:n_tables], refs[n_tables:]
    pending, acc = outs[-1], outs[-2]
    bounds = words_ref.shape[1] - 8 + group
    start, end = words_ref[0, bounds], words_ref[0, bounds + 1]
    low = lax.broadcasted_iota(jnp.int32, (BLK, LANES), 1) < BLK
    acc[...] = jnp.zeros_like(acc)

    def add(first):
        for u in range(UNROLL):
            i = first + u
            word = words_ref[0, jnp.maximum(i, 0)]
            place = jnp.where((i >= start) & (i < end), word & ((1 << SOURCE_AT) - 1), trash)
            rows = pl.ds(pl.multiple_of(place * PAIR, PAIR), PAIR)
            acc[rows, :] = acc[rows, :] + pending[u * PAIR : (u + 1) * PAIR, :]

    def step(g, carry):
        first = start + g * UNROLL
        products = []
        for u in range(UNROLL):
            word = words_ref[0, first + u]
            block = blocks_ref[pl.ds(pl.multiple_of((word >> SLOT_AT) * PAIR, PAIR), PAIR), :]
            source = (word >> SOURCE_AT) & ((1 << (SLOT_AT - SOURCE_AT)) - 1)
            right = []
            for table in tables:
                part = table[pl.ds(pl.multiple_of(source * BLK, BLK), BLK), :]
                zero = jnp.zeros_like(part)
                right.append(jnp.concatenate([jnp.where(low, part, zero), jnp.where(low, zero, part)], axis=0))
            products.append(jnp.dot(block, jnp.concatenate(right, axis=1), preferred_element_type=jnp.float32))
        add(first - UNROLL)
        for u in range(UNROLL):
            pending[u * PAIR : (u + 1) * PAIR, :] = products[u]
        return carry

    groups = (end - start + (UNROLL - 1)) // UNROLL
    lax.fori_loop(0, groups, step, 0)
    add(start + (groups - 1) * UNROLL)
    if len(outs) > 2:
        outs[0][...] = acc[: trash * PAIR, :].astype(outs[0].dtype)


def product(group, words, blocks, tables, trash, sent):
    lanes = LANES * len(tables)
    full = jax.ShapeDtypeStruct(((trash + 1) * PAIR, lanes), jnp.float32)
    out = jax.ShapeDtypeStruct((trash * PAIR, lanes), jnp.bfloat16) if sent else full
    sums = [pltpu.VMEM(full.shape, full.dtype)] if sent else []
    return pl.pallas_call(
        functools.partial(product_kernel, trash, group, len(tables)),
        in_specs=[SMEM, VMEM] + [VMEM] * len(tables),
        out_specs=VMEM,
        out_shape=out,
        scratch_shapes=sums + [pltpu.VMEM((UNROLL * PAIR, lanes), jnp.float32)],
        compiler_params=pltpu.CompilerParams(vmem_limit_bytes=8 * MIB),
        cost_estimate=pl.CostEstimate(flops=1, bytes_accessed=1, transcendentals=0),
        name="product_send" if sent else "product_keep",
    )(words, blocks, *tables)


def add_kernel(keep_ref, got_ref, next_ref, send_ref):
    half = next_ref.shape[0]
    next_ref[...] = keep_ref[:half, :] + got_ref[:half, :].astype(jnp.float32)
    send_ref[...] = (keep_ref[half:, :] + got_ref[half:, :].astype(jnp.float32)).astype(send_ref.dtype)


def add_halves(keep, place, got):
    rows, lanes = got.shape
    half = (rows // 2, lanes)
    block = lambda shape, place: pl.BlockSpec(shape, lambda _: place)
    return pl.pallas_call(
        add_kernel,
        grid=(1,),
        in_specs=[block(got.shape, place), block(got.shape, (0, 0))],
        out_specs=(block(half, (0, 0)),) * 2,
        out_shape=(jax.ShapeDtypeStruct(half, jnp.float32), jax.ShapeDtypeStruct(half, jnp.bfloat16)),
        compiler_params=pltpu.CompilerParams(vmem_limit_bytes=8 * MIB),
        cost_estimate=pl.CostEstimate(flops=rows * lanes, bytes_accessed=MIB, transcendentals=0),
        name="add",
    )(keep, got)


def layer_rows(sums, even, odd, bias_ref, out_hbm, first, left, right, result, sem):
    base = 0
    for pairs in sums:
        aggregated = [(keep[...] + got[...].astype(jnp.float32)).astype(jnp.bfloat16) for keep, got in pairs]
        aggregated = jnp.concatenate(aggregated, axis=1)
        rows = aggregated.shape[0]
        for h, w in enumerate((even, odd)):
            hidden = jnp.dot(aggregated, w, preferred_element_type=jnp.float32) + bias_ref[...]
            hidden = jnp.maximum(hidden, 0.0)
            left[pl.ds(base + h, rows, stride=2), :] = hidden[:, :LANES]
            right[pl.ds(base + h, rows, stride=2), :] = hidden[:, LANES:]
        base += 2 * rows
    result[:, :LANES] = left[...].astype(result.dtype)
    result[:, LANES:] = right[...].astype(result.dtype)
    copy = pltpu.make_async_copy(result, out_hbm.at[pl.ds(first, base)], sem)
    copy.start()
    copy.wait()


def grouped(refs, counts):
    refs, groups = list(refs), []
    for count in counts:
        groups.append([(refs.pop(0), refs.pop(0)) for _ in range(count)])
    return groups


def first_layer_kernel(index, counts, first, *refs):
    sums = grouped(refs, counts)
    weight_ref, bias_ref, out_hbm, even_ref, odd_ref, wide, *scratch = refs[2 * sum(counts) :]
    r = lax.axis_index("row")
    wide[...] = weight_ref[...].astype(jnp.float32)
    size = wide.shape[0] // (2 * len(index[0]))
    halves = []
    for pieces in index:
        rows = [wide[pl.ds(pl.multiple_of((r ^ i) * size, size), size), :] for i in pieces]
        halves.append(jnp.concatenate(rows, axis=0).astype(jnp.bfloat16))
    zero = jnp.zeros_like(halves[0])
    even_ref[...] = jnp.concatenate([halves[0], zero, halves[1], zero], axis=0)
    odd_ref[...] = jnp.concatenate([zero, halves[0], zero, halves[1]], axis=0)
    layer_rows(sums, even_ref[...], odd_ref[...], bias_ref, out_hbm, first, *scratch)


def last_layer_kernel(counts, first, *refs):
    sums = grouped(refs, counts)
    even_ref, odd_ref, bias_ref, _, out_hbm, *scratch = refs[2 * sum(counts) :]
    layer_rows(sums, even_ref[...], odd_ref[...], bias_ref, out_hbm, first, *scratch)


def layer_scratch(rows, lanes):
    wide = [pltpu.VMEM((rows, LANES), jnp.float32)] * 2
    return wide + [pltpu.VMEM((rows, lanes), jnp.bfloat16), pltpu.SemaphoreType.DMA]


def layer(index, sums, weight, bias):
    counts = [len(part) // 2 for part in sums]
    sizes = [2 * part[0].shape[0] for part in sums]
    lanes = weight.shape[1]
    anywhere = pl.BlockSpec(memory_space=pl.ANY)
    params = pltpu.CompilerParams(vmem_limit_bytes=8 * MIB)
    shape = jax.ShapeDtypeStruct((sum(sizes), lanes), jnp.bfloat16)
    expanded = jax.ShapeDtypeStruct((2 * LANES, lanes), jnp.bfloat16)
    flat = [x for part in sums[1:] for x in part]
    out, even, odd = pl.pallas_call(
        functools.partial(first_layer_kernel, index, counts[1:], sizes[0]),
        in_specs=[VMEM] * (len(flat) + 2),
        out_specs=(anywhere, VMEM, VMEM),
        out_shape=(shape, expanded, expanded),
        scratch_shapes=[pltpu.VMEM(weight.shape, jnp.float32)] + layer_scratch(sum(sizes[1:]), lanes),
        compiler_params=params,
        name="layer_first",
    )(*flat, weight, bias)
    flat, out = lax.optimization_barrier((sums[0], out))
    return pl.pallas_call(
        functools.partial(last_layer_kernel, counts[:1], 0),
        in_specs=[VMEM] * (len(flat) + 3) + [anywhere],
        out_specs=anywhere,
        out_shape=shape,
        input_output_aliases={len(flat) + 3: 0},
        scratch_shapes=layer_scratch(sizes[0], lanes),
        compiler_params=params,
        name="layer_last",
    )(*flat, even, odd, bias, out)


def exchange(x, axis, size, bit):
    return lax.ppermute(x, axis, [(i, i ^ (1 << bit)) for i in range(size)])


def shards(n_row, n_col, features, block_codes, block_count, block_values, weight, bias):
    top, col_axis_bits = log2(n_row) - 1, list(range(log2(n_col)))
    col_blocks = features.shape[0] // BLK
    row_total = col_blocks * n_col // n_row
    per = row_total // n_col

    z_first, x_first = tuple(col_axis_bits[1:] + col_axis_bits[:1]), tuple(col_axis_bits)
    chunks = ((per // 2, x_first), (per // 4, x_first), (per // 4, z_first))
    halves = [size * n_col // 2 for size, _ in chunks]

    def spread(pieces, index):
        for bit in range(top):
            pieces = pieces + [exchange(p, "row", n_row, bit) for p in pieces]
            index = index + [i ^ (1 << bit) for i in index]
        return pieces, index

    mine = features.T
    other = exchange(mine, "row", n_row, top)
    near, near_index = spread([mine], [0])
    blocks, words = relayout(chunks, log2(col_blocks), block_count, block_codes, block_values[0])

    tables = [make_table(near)]
    first = product(0, words, blocks, tables, halves[0], True)
    other, first = lax.optimization_barrier((other, first))
    far, far_index = spread([other], [1 << top])
    tables.append(make_table(far))
    sends = [(first, product(0, words, blocks, tables[1:], halves[0], True))]
    sends += [(product(k, words, blocks, tables, halves[k], True),) for k in (1, 2)]
    gots = [[exchange(s, "col", n_col, order[0]) for s in send] for send, (_, order) in zip(sends, chunks)]
    words, gots[0][0] = lax.optimization_barrier((words, gots[0][0]))
    kept = product(len(chunks), words, blocks, tables, sum(halves), False)
    kept_at = [sum(halves[:k]) // halves[k] for k in range(len(chunks))]
    parts = [[(kept, (at, f), got) for f, got in enumerate(g)] for at, g in zip(kept_at, gots)]
    for k in range(1, len(col_axis_bits)):
        for i, (_, order) in enumerate(chunks):
            sums = [add_halves(*part) for part in parts[i]]
            parts[i] = [(total, (0, 0), exchange(send, "col", n_col, order[k])) for total, send in sums]
    sums = [[x for keep, _, got in part for x in (keep, got)] for part in parts]
    return layer((near_index, far_index), sums, weight, bias[None, :])


def solution(mesh):
    in_specs = (P("col", "row"), P("row", "col"), P("row", "col"), P("row", "col", None), P(), P())
    out_specs = P(("row", "col"), None)
    body = functools.partial(shards, mesh.shape["row"], mesh.shape["col"])
    return jax.shard_map(body, mesh=mesh, in_specs=in_specs, out_specs=out_specs, check_vma=False)
```

```python
import functools

import jax
import jax.numpy as jnp
from jax import lax
from jax.experimental import pallas as pl
from jax.experimental.pallas import tpu as pltpu
from jax.sharding import PartitionSpec as P

BLK = 64
PAIR = BLK // 2
LANES = 2 * BLK
GROUP = 16
TOGETHER = 4
UNROLL = 16
SLOT_AT, SOURCE_AT = 13, 7
MIB = 1024 * 1024
SMEM = pl.BlockSpec(memory_space=pltpu.SMEM)
VMEM = pl.BlockSpec(memory_space=pltpu.VMEM)


def log2(size):
    return size.bit_length() - 1


def list_width(slots):
    return -(-(slots + 2 * UNROLL + 8) // LANES) * LANES


def make_lists(chunks, col_bits, count, codes, words_ref):
    slots, width = codes.shape[1], words_ref.shape[1]
    per = sum(size for size, _ in chunks)
    row_block, col_block = codes >> col_bits, codes & ((1 << col_bits) - 1)
    owner = (row_block >> log2(per)) ^ lax.axis_index("col")
    sub = row_block & (per - 1)
    number = lax.broadcasted_iota(jnp.int32, (1, slots), 1)
    live = number < count
    group, target = jnp.full_like(codes, len(chunks) + 1), jnp.zeros_like(codes)
    first, base = 0, 0
    for c, (size, order) in enumerate(chunks):
        place = jnp.zeros_like(owner)
        for k, bit in enumerate(order):
            place = place | (((owner >> bit) & 1) << (len(order) - 1 - k))
        place = (place << log2(size)) + (sub - first)
        half = size << (len(order) - 1)
        keep = place < half
        here = live & (sub >= first) & (sub < first + size)
        target = jnp.where(here, jnp.where(keep, place + base, place - half), target)
        group = jnp.where(here, jnp.where(keep, len(chunks), c), group)
        first, base = first + size, base + half
    same = lax.broadcasted_iota(jnp.int32, (slots, slots), 0) == lax.broadcasted_iota(jnp.int32, (slots, slots), 1)
    column = lambda row: jnp.sum(jnp.where(same, row, 0.0), axis=1, keepdims=True)
    spot = lax.broadcasted_iota(jnp.int32, (slots, width), 1).astype(jnp.float32)
    lane = lax.broadcasted_iota(jnp.int32, (1, width), 1)
    key = (group * slots + number).astype(jnp.float32)
    word = ((number << SLOT_AT) | (col_block << SOURCE_AT) | target).astype(jnp.float32)
    rank = jnp.sum(jnp.where(key < column(key), 1.0, 0.0), axis=1, keepdims=True)
    words = jnp.sum(jnp.where(rank == spot, column(word), 0.0), axis=0, keepdims=True).astype(jnp.int32)
    for k in range(len(chunks) + 2):
        before = jnp.sum(jnp.where(group < k, 1.0, 0.0), axis=1, keepdims=True).astype(jnp.int32)
        words = jnp.where(lane == width - 8 + k, before, words)
    words_ref[...] = words


def relayout_kernel(chunks, col_bits, count_ref, codes_hbm, values_hbm, out_ref, words_ref, codes, held, scratch, arrived, codes_arrived):
    codes_copy = pltpu.make_async_copy(codes_hbm, codes, codes_arrived)
    codes_copy.start()
    step = GROUP * TOGETHER

    def copy(k):
        rows = pl.ds(pl.multiple_of(k * step, step), step)
        return pltpu.make_async_copy(values_hbm.at[rows], held.at[rows], arrived.at[k])

    steps = values_hbm.shape[0] // step
    for k in range(steps):
        copy(k).start()
    codes_copy.wait()
    make_lists(chunks, col_bits, count_ref[0, 0], codes[...], words_ref)

    def one(k, carry):
        copy(k).wait()
        for g in range(TOGETHER):
            slots = pl.ds(pl.multiple_of(k * step + g * GROUP, GROUP), GROUP)
            for p in range(PAIR):
                wide = held[slots, p * LANES : (p + 1) * LANES].astype(jnp.float32)
                scratch[(g * PAIR + p) * GROUP : (g * PAIR + p + 1) * GROUP, :] = wide
        for g in range(TOGETHER):
            for s in range(GROUP):
                rows = scratch[pl.ds(g * PAIR * GROUP + s, PAIR, stride=GROUP), :]
                at = pl.multiple_of((k * step + g * GROUP + s) * PAIR, PAIR)
                out_ref[pl.ds(at, PAIR), :] = rows.astype(out_ref.dtype)
        return carry

    lax.fori_loop(0, steps, one, 0)


def relayout(chunks, col_bits, count, codes, values):
    slots = values.shape[0]
    return pl.pallas_call(
        functools.partial(relayout_kernel, chunks, col_bits),
        in_specs=[SMEM] + [pl.BlockSpec(memory_space=pltpu.HBM)] * 2,
        out_specs=(VMEM, VMEM),
        out_shape=(
            jax.ShapeDtypeStruct((slots * PAIR, LANES), values.dtype),
            jax.ShapeDtypeStruct((1, list_width(slots)), jnp.int32),
        ),
        scratch_shapes=[
            pltpu.VMEM(codes.shape, codes.dtype),
            pltpu.VMEM(values.shape, values.dtype),
            pltpu.VMEM((TOGETHER * GROUP * PAIR, LANES), jnp.float32),
            pltpu.SemaphoreType.DMA((slots // (GROUP * TOGETHER),)),
            pltpu.SemaphoreType.DMA,
        ],
        cost_estimate=pl.CostEstimate(flops=0, bytes_accessed=4 * slots * BLK * BLK, transcendentals=0),
        compiler_params=pltpu.CompilerParams(vmem_limit_bytes=48 * MIB),
        name="relayout",
    )(count, codes, values)


def table_kernel(*refs):
    parts, table = refs[:-1], refs[-1]
    kind = table.dtype if parts[0].shape[0] % 16 == 0 else jnp.float32

    def build(q, carry):
        at = pl.ds(pl.multiple_of(q * LANES, LANES), LANES)
        x = [part[:, at].astype(kind) for part in parts]
        table[at, :] = jnp.concatenate(x + x, axis=0).T.astype(table.dtype)
        return carry

    lax.fori_loop(0, table.shape[0] // LANES, build, 0, unroll=4)


def make_table(parts):
    nodes = parts[0].shape[1]
    return pl.pallas_call(
        table_kernel,
        in_specs=[VMEM] * len(parts),
        out_specs=VMEM,
        out_shape=jax.ShapeDtypeStruct((nodes, LANES), jnp.bfloat16),
        compiler_params=pltpu.CompilerParams(vmem_limit_bytes=4 * MIB),
        cost_estimate=pl.CostEstimate(flops=1, bytes_accessed=1, transcendentals=0),
        name="table",
    )(*parts)


def product_kernel(trash, group, n_tables, words_ref, blocks_ref, *refs):
    tables, outs = refs[:n_tables], refs[n_tables:]
    pending, acc = outs[-1], outs[-2]
    bounds = words_ref.shape[1] - 8 + group
    start, end = words_ref[0, bounds], words_ref[0, bounds + 1]
    low = lax.broadcasted_iota(jnp.int32, (BLK, LANES), 1) < BLK
    acc[...] = jnp.zeros_like(acc)

    def add(first):
        for u in range(UNROLL):
            i = first + u
            word = words_ref[0, jnp.maximum(i, 0)]
            place = jnp.where((i >= start) & (i < end), word & ((1 << SOURCE_AT) - 1), trash)
            rows = pl.ds(pl.multiple_of(place * PAIR, PAIR), PAIR)
            acc[rows, :] = acc[rows, :] + pending[u * PAIR : (u + 1) * PAIR, :]

    def step(g, carry):
        first = start + g * UNROLL
        products = []
        for u in range(UNROLL):
            word = words_ref[0, first + u]
            block = blocks_ref[pl.ds(pl.multiple_of((word >> SLOT_AT) * PAIR, PAIR), PAIR), :]
            source = (word >> SOURCE_AT) & ((1 << (SLOT_AT - SOURCE_AT)) - 1)
            right = []
            for table in tables:
                part = table[pl.ds(pl.multiple_of(source * BLK, BLK), BLK), :]
                zero = jnp.zeros_like(part)
                right.append(jnp.concatenate([jnp.where(low, part, zero), jnp.where(low, zero, part)], axis=0))
            products.append(jnp.dot(block, jnp.concatenate(right, axis=1), preferred_element_type=jnp.float32))
        add(first - UNROLL)
        for u in range(UNROLL):
            pending[u * PAIR : (u + 1) * PAIR, :] = products[u]
        return carry

    groups = (end - start + (UNROLL - 1)) // UNROLL
    lax.fori_loop(0, groups, step, 0)
    add(start + (groups - 1) * UNROLL)
    if len(outs) > 2:
        outs[0][...] = acc[: trash * PAIR, :].astype(outs[0].dtype)


def product(group, words, blocks, tables, trash, sent):
    lanes = LANES * len(tables)
    full = jax.ShapeDtypeStruct(((trash + 1) * PAIR, lanes), jnp.float32)
    out = jax.ShapeDtypeStruct((trash * PAIR, lanes), jnp.bfloat16) if sent else full
    sums = [pltpu.VMEM(full.shape, full.dtype)] if sent else []
    return pl.pallas_call(
        functools.partial(product_kernel, trash, group, len(tables)),
        in_specs=[SMEM, VMEM] + [VMEM] * len(tables),
        out_specs=VMEM,
        out_shape=out,
        scratch_shapes=sums + [pltpu.VMEM((UNROLL * PAIR, lanes), jnp.float32)],
        compiler_params=pltpu.CompilerParams(vmem_limit_bytes=8 * MIB),
        cost_estimate=pl.CostEstimate(flops=1, bytes_accessed=1, transcendentals=0),
        name="product_send" if sent else "product_keep",
    )(words, blocks, *tables)


def add_kernel(keep_ref, got_ref, next_ref, send_ref):
    half = next_ref.shape[0]
    next_ref[...] = keep_ref[:half, :] + got_ref[:half, :].astype(jnp.float32)
    send_ref[...] = (keep_ref[half:, :] + got_ref[half:, :].astype(jnp.float32)).astype(send_ref.dtype)


def add_halves(keep, place, got):
    rows, lanes = got.shape
    half = (rows // 2, lanes)
    block = lambda shape, place: pl.BlockSpec(shape, lambda _: place)
    return pl.pallas_call(
        add_kernel,
        grid=(1,),
        in_specs=[block(got.shape, place), block(got.shape, (0, 0))],
        out_specs=(block(half, (0, 0)),) * 2,
        out_shape=(jax.ShapeDtypeStruct(half, jnp.float32), jax.ShapeDtypeStruct(half, jnp.bfloat16)),
        compiler_params=pltpu.CompilerParams(vmem_limit_bytes=8 * MIB),
        cost_estimate=pl.CostEstimate(flops=rows * lanes, bytes_accessed=MIB, transcendentals=0),
        name="add",
    )(keep, got)


def layer_kernel(index, counts, *refs):
    sums, (weight_ref, bias_ref, out_ref, wide, left, right) = list(refs[:-6]), refs[-6:]
    r = lax.axis_index("row")
    wide[...] = weight_ref[...].astype(jnp.float32)
    size = wide.shape[0] // (2 * len(index[0]))
    halves = []
    for pieces in index:
        rows = [wide[pl.ds(pl.multiple_of((r ^ i) * size, size), size), :] for i in pieces]
        halves.append(jnp.concatenate(rows, axis=0).astype(jnp.bfloat16))
    zero = jnp.zeros_like(halves[0])
    even = jnp.concatenate([halves[0], zero, halves[1], zero], axis=0)
    odd = jnp.concatenate([zero, halves[0], zero, halves[1]], axis=0)
    base = 0
    for count in counts:
        pairs = [(sums.pop(0), sums.pop(0)) for _ in range(count // 2)]
        aggregated = [(keep[...] + got[...].astype(jnp.float32)).astype(jnp.bfloat16) for keep, got in pairs]
        aggregated = jnp.concatenate(aggregated, axis=1)
        rows = aggregated.shape[0]
        for h, w in enumerate((even, odd)):
            hidden = jnp.dot(aggregated, w, preferred_element_type=jnp.float32) + bias_ref[...]
            hidden = jnp.maximum(hidden, 0.0)
            left[pl.ds(base + h, rows, stride=2), :] = hidden[:, :LANES]
            right[pl.ds(base + h, rows, stride=2), :] = hidden[:, LANES:]
        base += 2 * rows
    out_ref[:, :LANES] = left[...].astype(out_ref.dtype)
    out_ref[:, LANES:] = right[...].astype(out_ref.dtype)


def layer(index, sums, weight, bias):
    rows = sum(2 * part[0].shape[0] for part in sums)
    return pl.pallas_call(
        functools.partial(layer_kernel, index, [len(part) for part in sums]),
        out_shape=jax.ShapeDtypeStruct((rows, weight.shape[1]), jnp.bfloat16),
        scratch_shapes=[pltpu.VMEM(weight.shape, jnp.float32)] + [pltpu.VMEM((rows, LANES), jnp.float32)] * 2,
        compiler_params=pltpu.CompilerParams(vmem_limit_bytes=8 * MIB),
        name="layer",
    )(*[x for part in sums for x in part], weight, bias)


def exchange(x, axis, size, bit):
    return lax.ppermute(x, axis, [(i, i ^ (1 << bit)) for i in range(size)])


def shards(n_row, n_col, features, block_codes, block_count, block_values, weight, bias):
    top, col_axis_bits = log2(n_row) - 1, list(range(log2(n_col)))
    col_blocks = features.shape[0] // BLK
    row_total = col_blocks * n_col // n_row
    per = row_total // n_col

    z_first, x_first = tuple(col_axis_bits[1:] + col_axis_bits[:1]), tuple(col_axis_bits)
    chunks = ((per // 2, x_first), (per // 4, x_first), (per // 4, z_first))
    halves = [size * n_col // 2 for size, _ in chunks]

    def spread(pieces, index):
        for bit in range(top):
            pieces = pieces + [exchange(p, "row", n_row, bit) for p in pieces]
            index = index + [i ^ (1 << bit) for i in index]
        return pieces, index

    mine = features.T
    other = exchange(mine, "row", n_row, top)
    near, near_index = spread([mine], [0])
    blocks, words = relayout(chunks, log2(col_blocks), block_count, block_codes, block_values[0])

    tables = [make_table(near)]
    first = product(0, words, blocks, tables, halves[0], True)
    other, first = lax.optimization_barrier((other, first))
    far, far_index = spread([other], [1 << top])
    tables.append(make_table(far))
    others = [product(k, words, blocks, tables, halves[k], True) for k in (1, 2)]
    send = lambda x, k: exchange(x, "col", n_col, chunks[k][1][0])
    gots = [[send(first, 0)]] + [[send(x, k)] for k, x in enumerate(others, 1)]
    words, gots[0][0], _ = lax.optimization_barrier((words, gots[0][0], others))
    kept = product(len(chunks), words, blocks, tables, sum(halves), False)
    words, _ = lax.optimization_barrier((words, kept))
    gots[0].append(send(product(0, words, blocks, tables[1:], halves[0], True), 0))
    kept_at = [sum(halves[:k]) // halves[k] for k in range(len(chunks))]
    parts = [[(kept, (at, f), got) for f, got in enumerate(g)] for at, g in zip(kept_at, gots)]
    for k in range(1, len(col_axis_bits)):
        for i, (_, order) in enumerate(chunks):
            sums = [add_halves(*part) for part in parts[i]]
            parts[i] = [(total, (0, 0), exchange(send, "col", n_col, order[k])) for total, send in sums]
    sums = [[x for keep, _, got in part for x in (keep, got)] for part in parts]
    return layer((near_index, far_index), sums, weight, bias[None, :])


def solution(mesh):
    in_specs = (P("col", "row"), P("row", "col"), P("row", "col"), P("row", "col", None), P(), P())
    out_specs = P(("row", "col"), None)
    body = functools.partial(shards, mesh.shape["row"], mesh.shape["col"])
    return jax.shard_map(body, mesh=mesh, in_specs=in_specs, out_specs=out_specs, check_vma=False)
```

```python
import functools

import jax
import jax.numpy as jnp
from jax import lax
from jax.experimental import pallas as pl
from jax.experimental.pallas import tpu as pltpu
from jax.sharding import PartitionSpec as P

BLK = 64
PAIR = BLK // 2
LANES = 2 * BLK
GROUP = 16
TOGETHER = 4
UNROLL = 16
SLOT_AT, SOURCE_AT = 13, 7
MIB = 1024 * 1024
SMEM = pl.BlockSpec(memory_space=pltpu.SMEM)
VMEM = pl.BlockSpec(memory_space=pltpu.VMEM)


def log2(size):
    return size.bit_length() - 1


def list_width(slots):
    return -(-(slots + 2 * UNROLL + 8) // LANES) * LANES


def make_lists(chunks, col_bits, count, codes, words_ref):
    slots, width = codes.shape[1], words_ref.shape[1]
    per = sum(size for size, _ in chunks)
    row_block, col_block = codes >> col_bits, codes & ((1 << col_bits) - 1)
    owner = (row_block >> log2(per)) ^ lax.axis_index("col")
    sub = row_block & (per - 1)
    number = lax.broadcasted_iota(jnp.int32, (1, slots), 1)
    live = number < count
    group, target = jnp.full_like(codes, len(chunks) + 1), jnp.zeros_like(codes)
    first, base = 0, 0
    for c, (size, order) in enumerate(chunks):
        place = jnp.zeros_like(owner)
        for k, bit in enumerate(order):
            place = place | (((owner >> bit) & 1) << (len(order) - 1 - k))
        place = (place << log2(size)) + (sub - first)
        half = size << (len(order) - 1)
        keep = place < half
        here = live & (sub >= first) & (sub < first + size)
        target = jnp.where(here, jnp.where(keep, place + base, place - half), target)
        group = jnp.where(here, jnp.where(keep, len(chunks), c), group)
        first, base = first + size, base + half
    same = lax.broadcasted_iota(jnp.int32, (slots, slots), 0) == lax.broadcasted_iota(jnp.int32, (slots, slots), 1)
    column = lambda row: jnp.sum(jnp.where(same, row, 0.0), axis=1, keepdims=True)
    spot = lax.broadcasted_iota(jnp.int32, (slots, width), 1).astype(jnp.float32)
    lane = lax.broadcasted_iota(jnp.int32, (1, width), 1)
    key = (group * slots + number).astype(jnp.float32)
    word = ((number << SLOT_AT) | (col_block << SOURCE_AT) | target).astype(jnp.float32)
    rank = jnp.sum(jnp.where(key < column(key), 1.0, 0.0), axis=1, keepdims=True)
    words = jnp.sum(jnp.where(rank == spot, column(word), 0.0), axis=0, keepdims=True).astype(jnp.int32)
    for k in range(len(chunks) + 2):
        before = jnp.sum(jnp.where(group < k, 1.0, 0.0), axis=1, keepdims=True).astype(jnp.int32)
        words = jnp.where(lane == width - 8 + k, before, words)
    words_ref[...] = words


def relayout_kernel(chunks, col_bits, count_ref, codes_hbm, values_hbm, out_ref, words_ref, codes, held, scratch, arrived, codes_arrived):
    codes_copy = pltpu.make_async_copy(codes_hbm, codes, codes_arrived)
    codes_copy.start()
    step = GROUP * TOGETHER

    def copy(k):
        rows = pl.ds(pl.multiple_of(k * step, step), step)
        return pltpu.make_async_copy(values_hbm.at[rows], held.at[rows], arrived.at[k])

    steps = values_hbm.shape[0] // step
    for k in range(steps):
        copy(k).start()
    codes_copy.wait()
    make_lists(chunks, col_bits, count_ref[0, 0], codes[...], words_ref)

    def one(k, carry):
        copy(k).wait()
        for g in range(TOGETHER):
            slots = pl.ds(pl.multiple_of(k * step + g * GROUP, GROUP), GROUP)
            for p in range(PAIR):
                wide = held[slots, p * LANES : (p + 1) * LANES].astype(jnp.float32)
                scratch[(g * PAIR + p) * GROUP : (g * PAIR + p + 1) * GROUP, :] = wide
        for g in range(TOGETHER):
            for s in range(GROUP):
                rows = scratch[pl.ds(g * PAIR * GROUP + s, PAIR, stride=GROUP), :]
                at = pl.multiple_of((k * step + g * GROUP + s) * PAIR, PAIR)
                out_ref[pl.ds(at, PAIR), :] = rows.astype(out_ref.dtype)
        return carry

    lax.fori_loop(0, steps, one, 0)


def relayout(chunks, col_bits, count, codes, values):
    slots = values.shape[0]
    return pl.pallas_call(
        functools.partial(relayout_kernel, chunks, col_bits),
        in_specs=[SMEM] + [pl.BlockSpec(memory_space=pltpu.HBM)] * 2,
        out_specs=(VMEM, VMEM),
        out_shape=(
            jax.ShapeDtypeStruct((slots * PAIR, LANES), values.dtype),
            jax.ShapeDtypeStruct((1, list_width(slots)), jnp.int32),
        ),
        scratch_shapes=[
            pltpu.VMEM(codes.shape, codes.dtype),
            pltpu.VMEM(values.shape, values.dtype),
            pltpu.VMEM((TOGETHER * GROUP * PAIR, LANES), jnp.float32),
            pltpu.SemaphoreType.DMA((slots // (GROUP * TOGETHER),)),
            pltpu.SemaphoreType.DMA,
        ],
        cost_estimate=pl.CostEstimate(flops=0, bytes_accessed=4 * slots * BLK * BLK, transcendentals=0),
        compiler_params=pltpu.CompilerParams(vmem_limit_bytes=48 * MIB),
        name="relayout",
    )(count, codes, values)


def table_kernel(*refs):
    parts, table = refs[:-1], refs[-1]
    kind = table.dtype if parts[0].shape[0] % 16 == 0 else jnp.float32

    def build(q, carry):
        at = pl.ds(pl.multiple_of(q * LANES, LANES), LANES)
        x = [part[:, at].astype(kind) for part in parts]
        table[at, :] = jnp.concatenate(x + x, axis=0).T.astype(table.dtype)
        return carry

    lax.fori_loop(0, table.shape[0] // LANES, build, 0, unroll=4)


def make_table(parts):
    nodes = parts[0].shape[1]
    return pl.pallas_call(
        table_kernel,
        in_specs=[VMEM] * len(parts),
        out_specs=VMEM,
        out_shape=jax.ShapeDtypeStruct((nodes, LANES), jnp.bfloat16),
        compiler_params=pltpu.CompilerParams(vmem_limit_bytes=4 * MIB),
        cost_estimate=pl.CostEstimate(flops=1, bytes_accessed=1, transcendentals=0),
        name="table",
    )(*parts)


def product_kernel(trash, group, n_tables, words_ref, blocks_ref, *refs):
    tables, outs = refs[:n_tables], refs[n_tables:]
    pending, acc = outs[-1], outs[-2]
    bounds = words_ref.shape[1] - 8 + group
    start, end = words_ref[0, bounds], words_ref[0, bounds + 1]
    low = lax.broadcasted_iota(jnp.int32, (BLK, LANES), 1) < BLK
    acc[...] = jnp.zeros_like(acc)

    def add(first):
        for u in range(UNROLL):
            i = first + u
            word = words_ref[0, jnp.maximum(i, 0)]
            place = jnp.where((i >= start) & (i < end), word & ((1 << SOURCE_AT) - 1), trash)
            rows = pl.ds(pl.multiple_of(place * PAIR, PAIR), PAIR)
            acc[rows, :] = acc[rows, :] + pending[u * PAIR : (u + 1) * PAIR, :]

    def step(g, carry):
        first = start + g * UNROLL
        products = []
        for u in range(UNROLL):
            word = words_ref[0, first + u]
            block = blocks_ref[pl.ds(pl.multiple_of((word >> SLOT_AT) * PAIR, PAIR), PAIR), :]
            source = (word >> SOURCE_AT) & ((1 << (SLOT_AT - SOURCE_AT)) - 1)
            right = []
            for table in tables:
                part = table[pl.ds(pl.multiple_of(source * BLK, BLK), BLK), :]
                zero = jnp.zeros_like(part)
                right.append(jnp.concatenate([jnp.where(low, part, zero), jnp.where(low, zero, part)], axis=0))
            products.append(jnp.dot(block, jnp.concatenate(right, axis=1), preferred_element_type=jnp.float32))
        add(first - UNROLL)
        for u in range(UNROLL):
            pending[u * PAIR : (u + 1) * PAIR, :] = products[u]
        return carry

    groups = (end - start + (UNROLL - 1)) // UNROLL
    lax.fori_loop(0, groups, step, 0)
    add(start + (groups - 1) * UNROLL)
    if len(outs) > 2:
        outs[0][...] = acc[: trash * PAIR, :].astype(outs[0].dtype)


def product(group, words, blocks, tables, trash, sent):
    lanes = LANES * len(tables)
    full = jax.ShapeDtypeStruct(((trash + 1) * PAIR, lanes), jnp.float32)
    out = jax.ShapeDtypeStruct((trash * PAIR, lanes), jnp.bfloat16) if sent else full
    sums = [pltpu.VMEM(full.shape, full.dtype)] if sent else []
    return pl.pallas_call(
        functools.partial(product_kernel, trash, group, len(tables)),
        in_specs=[SMEM, VMEM] + [VMEM] * len(tables),
        out_specs=VMEM,
        out_shape=out,
        scratch_shapes=sums + [pltpu.VMEM((UNROLL * PAIR, lanes), jnp.float32)],
        compiler_params=pltpu.CompilerParams(vmem_limit_bytes=8 * MIB),
        cost_estimate=pl.CostEstimate(flops=1, bytes_accessed=1, transcendentals=0),
        name="product_send" if sent else "product_keep",
    )(words, blocks, *tables)


def add_kernel(keep_ref, got_ref, next_ref, send_ref):
    half = next_ref.shape[0]
    next_ref[...] = keep_ref[:half, :] + got_ref[:half, :].astype(jnp.float32)
    send_ref[...] = (keep_ref[half:, :] + got_ref[half:, :].astype(jnp.float32)).astype(send_ref.dtype)


def add_halves(keep, place, got):
    rows, lanes = got.shape
    half = (rows // 2, lanes)
    block = lambda shape, place: pl.BlockSpec(shape, lambda _: place)
    return pl.pallas_call(
        add_kernel,
        grid=(1,),
        in_specs=[block(got.shape, place), block(got.shape, (0, 0))],
        out_specs=(block(half, (0, 0)),) * 2,
        out_shape=(jax.ShapeDtypeStruct(half, jnp.float32), jax.ShapeDtypeStruct(half, jnp.bfloat16)),
        compiler_params=pltpu.CompilerParams(vmem_limit_bytes=8 * MIB),
        cost_estimate=pl.CostEstimate(flops=rows * lanes, bytes_accessed=MIB, transcendentals=0),
        name="add",
    )(keep, got)


def join_kernel(keep0, got0, keep1, got1, next0, next1, send_ref):
    at = 0
    for keep, got, next_ref in ((keep0, got0, next0), (keep1, got1, next1)):
        half = next_ref.shape[0]
        next_ref[...] = keep[:half, :] + got[:half, :].astype(jnp.float32)
        rest = (keep[half:, :] + got[half:, :].astype(jnp.float32)).astype(send_ref.dtype)
        for lane in range(0, rest.shape[1], LANES):
            send_ref[at : at + half, :] = rest[:, lane : lane + LANES]
            at += half


def add_and_join(keep0, got0, keep1, got1):
    half = [(got.shape[0] // 2, got.shape[1]) for got in (got0, got1)]
    rows = sum(n * lanes // LANES for n, lanes in half)
    return pl.pallas_call(
        join_kernel,
        in_specs=[VMEM] * 4,
        out_specs=[VMEM] * 3,
        out_shape=[jax.ShapeDtypeStruct(h, jnp.float32) for h in half] + [jax.ShapeDtypeStruct((rows, LANES), jnp.bfloat16)],
        compiler_params=pltpu.CompilerParams(vmem_limit_bytes=8 * MIB),
        cost_estimate=pl.CostEstimate(flops=rows * LANES, bytes_accessed=MIB, transcendentals=0),
        name="join",
    )(keep0, got0, keep1, got1)


def rows_of(keep, got):
    n, total = keep.shape[0], got.shape[0]
    if keep.shape == got.shape:
        return got[...]
    if keep.shape[1] == got.shape[1]:
        return got[:n, :]
    return jnp.concatenate([got[total - 2 * n : total - n, :], got[total - n :, :]], axis=1)


def layer_kernel(index, counts, *refs):
    sums, (weight_ref, bias_ref, out_ref, wide, left, right) = list(refs[:-6]), refs[-6:]
    r = lax.axis_index("row")
    wide[...] = weight_ref[...].astype(jnp.float32)
    size = wide.shape[0] // (2 * len(index[0]))
    halves = []
    for pieces in index:
        rows = [wide[pl.ds(pl.multiple_of((r ^ i) * size, size), size), :] for i in pieces]
        halves.append(jnp.concatenate(rows, axis=0).astype(jnp.bfloat16))
    zero = jnp.zeros_like(halves[0])
    even = jnp.concatenate([halves[0], zero, halves[1], zero], axis=0)
    odd = jnp.concatenate([zero, halves[0], zero, halves[1]], axis=0)
    base = 0
    for count in counts:
        pairs = [(sums.pop(0), sums.pop(0)) for _ in range(count // 2)]
        aggregated = [(keep[...] + rows_of(keep, got).astype(jnp.float32)).astype(jnp.bfloat16) for keep, got in pairs]
        aggregated = jnp.concatenate(aggregated, axis=1)
        rows = aggregated.shape[0]
        for h, w in enumerate((even, odd)):
            hidden = jnp.dot(aggregated, w, preferred_element_type=jnp.float32) + bias_ref[...]
            hidden = jnp.maximum(hidden, 0.0)
            left[pl.ds(base + h, rows, stride=2), :] = hidden[:, :LANES]
            right[pl.ds(base + h, rows, stride=2), :] = hidden[:, LANES:]
        base += 2 * rows
    out_ref[:, :LANES] = left[...].astype(out_ref.dtype)
    out_ref[:, LANES:] = right[...].astype(out_ref.dtype)


def layer(index, sums, weight, bias):
    rows = sum(2 * part[0].shape[0] for part in sums)
    return pl.pallas_call(
        functools.partial(layer_kernel, index, [len(part) for part in sums]),
        out_shape=jax.ShapeDtypeStruct((rows, weight.shape[1]), jnp.bfloat16),
        scratch_shapes=[pltpu.VMEM(weight.shape, jnp.float32)] + [pltpu.VMEM((rows, LANES), jnp.float32)] * 2,
        compiler_params=pltpu.CompilerParams(vmem_limit_bytes=8 * MIB),
        name="layer",
    )(*[x for part in sums for x in part], weight, bias)


def exchange(x, axis, size, bit):
    return lax.ppermute(x, axis, [(i, i ^ (1 << bit)) for i in range(size)])


def shards(n_row, n_col, features, block_codes, block_count, block_values, weight, bias):
    top, col_axis_bits = log2(n_row) - 1, list(range(log2(n_col)))
    col_blocks = features.shape[0] // BLK
    row_total = col_blocks * n_col // n_row
    per = row_total // n_col

    z_first, x_first = tuple(col_axis_bits[1:] + col_axis_bits[:1]), tuple(col_axis_bits)
    chunks = ((per // 2, x_first), (per // 4, x_first), (per // 4, z_first))
    halves = [size * n_col // 2 for size, _ in chunks]

    def spread(pieces, index):
        for bit in range(top):
            pieces = pieces + [exchange(p, "row", n_row, bit) for p in pieces]
            index = index + [i ^ (1 << bit) for i in index]
        return pieces, index

    mine = features.T
    other = exchange(mine, "row", n_row, top)
    near, near_index = spread([mine], [0])
    blocks, words = relayout(chunks, log2(col_blocks), block_count, block_codes, block_values[0])

    tables = [make_table(near)]
    first = product(0, words, blocks, tables, halves[0], True)
    other, first = lax.optimization_barrier((other, first))
    far, far_index = spread([other], [1 << top])
    tables.append(make_table(far))
    sends = [(first, product(0, words, blocks, tables[1:], halves[0], True))]
    sends += [(product(k, words, blocks, tables, halves[k], True),) for k in (1, 2)]
    gots = [[exchange(s, "col", n_col, order[0]) for s in send] for send, (_, order) in zip(sends, chunks)]
    words, gots[0][0] = lax.optimization_barrier((words, gots[0][0]))
    kept = product(len(chunks), words, blocks, tables, sum(halves), False)
    kept_at = [sum(halves[:k]) // halves[k] for k in range(len(chunks))]
    parts = [[(kept, (at, f), got) for f, got in enumerate(g)] for at, g in zip(kept_at, gots)]
    last = len(col_axis_bits) - 1
    for k in range(1, last + 1):
        for i in (2, 0, 1):
            order, todo = chunks[i][1], parts[i]
            if k == last and i < 2:
                todo = parts[i][1:]
                if i == 1:
                    (keep0, _, got0), (keep1, _, got1) = parts[0][0], parts[1][0]
                    got0, _ = lax.optimization_barrier((got0, parts[2][0][0]))
                    total0, total1, send = add_and_join(keep0, got0, keep1, got1)
                    both = exchange(send, "col", n_col, order[k])
                    parts[0][0], parts[1][0] = (total0, (0, 0), both), (total1, (0, 0), both)
            sums = [add_halves(*part) for part in todo]
            done = [(total, (0, 0), exchange(send, "col", n_col, order[k])) for total, send in sums]
            parts[i] = parts[i][: len(parts[i]) - len(todo)] + done
            if k == 1 and i == 2:
                keep, place, got = parts[1][0]
                parts[1][0] = (keep, place, lax.optimization_barrier((got, done[0][0]))[0])
    sums = [[x for keep, _, got in part for x in (keep, got)] for part in parts]
    return layer((near_index, far_index), sums, weight, bias[None, :])


def solution(mesh):
    in_specs = (P("col", "row"), P("row", "col"), P("row", "col"), P("row", "col", None), P(), P())
    out_specs = P(("row", "col"), None)
    body = functools.partial(shards, mesh.shape["row"], mesh.shape["col"])
    return jax.shard_map(body, mesh=mesh, in_specs=in_specs, out_specs=out_specs, check_vma=False)
```

```python
import functools

import jax
import jax.numpy as jnp
from jax import lax
from jax.experimental import pallas as pl
from jax.experimental.pallas import tpu as pltpu
from jax.sharding import PartitionSpec as P

BLK = 64
PAIR = BLK // 2
LANES = 2 * BLK
GROUP = 16
TOGETHER = 4
UNROLL = 24
SLOT_AT, SOURCE_AT = 13, 7
MIB = 1024 * 1024
SMEM = pl.BlockSpec(memory_space=pltpu.SMEM)
VMEM = pl.BlockSpec(memory_space=pltpu.VMEM)


def log2(size):
    return size.bit_length() - 1


def list_width(slots):
    return -(-(slots + 2 * UNROLL + 8) // LANES) * LANES


def make_lists(chunks, col_bits, count, codes, words_ref):
    slots, width = codes.shape[1], words_ref.shape[1]
    per = sum(size for size, _ in chunks)
    row_block, col_block = codes >> col_bits, codes & ((1 << col_bits) - 1)
    owner = (row_block >> log2(per)) ^ lax.axis_index("col")
    sub = row_block & (per - 1)
    number = lax.broadcasted_iota(jnp.int32, (1, slots), 1)
    live = number < count
    group, target = jnp.full_like(codes, len(chunks) + 1), jnp.zeros_like(codes)
    first, base = 0, 0
    for c, (size, order) in enumerate(chunks):
        place = jnp.zeros_like(owner)
        for k, bit in enumerate(order):
            place = place | (((owner >> bit) & 1) << (len(order) - 1 - k))
        place = (place << log2(size)) + (sub - first)
        half = size << (len(order) - 1)
        keep = place < half
        here = live & (sub >= first) & (sub < first + size)
        target = jnp.where(here, jnp.where(keep, place + base, place - half), target)
        group = jnp.where(here, jnp.where(keep, len(chunks), c), group)
        first, base = first + size, base + half
    same = lax.broadcasted_iota(jnp.int32, (slots, slots), 0) == lax.broadcasted_iota(jnp.int32, (slots, slots), 1)
    column = lambda row: jnp.sum(jnp.where(same, row, 0.0), axis=1, keepdims=True)
    spot = lax.broadcasted_iota(jnp.int32, (slots, width), 1).astype(jnp.float32)
    lane = lax.broadcasted_iota(jnp.int32, (1, width), 1)
    key = (group * slots + number).astype(jnp.float32)
    word = ((number << SLOT_AT) | (col_block << SOURCE_AT) | target).astype(jnp.float32)
    rank = jnp.sum(jnp.where(key < column(key), 1.0, 0.0), axis=1, keepdims=True)
    words = jnp.sum(jnp.where(rank == spot, column(word), 0.0), axis=0, keepdims=True).astype(jnp.int32)
    for k in range(len(chunks) + 2):
        before = jnp.sum(jnp.where(group < k, 1.0, 0.0), axis=1, keepdims=True).astype(jnp.int32)
        words = jnp.where(lane == width - 8 + k, before, words)
    words_ref[...] = words


def relayout_kernel(chunks, col_bits, count_ref, codes_hbm, values_hbm, out_ref, words_ref, codes, held, scratch, arrived, codes_arrived):
    codes_copy = pltpu.make_async_copy(codes_hbm, codes, codes_arrived)
    codes_copy.start()
    step = GROUP * TOGETHER

    def copy(k):
        rows = pl.ds(pl.multiple_of(k * step, step), step)
        return pltpu.make_async_copy(values_hbm.at[rows], held.at[rows], arrived.at[k])

    steps = values_hbm.shape[0] // step
    for k in range(steps):
        copy(k).start()
    codes_copy.wait()
    make_lists(chunks, col_bits, count_ref[0, 0], codes[...], words_ref)

    def one(k, carry):
        copy(k).wait()
        for g in range(TOGETHER):
            slots = pl.ds(pl.multiple_of(k * step + g * GROUP, GROUP), GROUP)
            for p in range(PAIR):
                wide = held[slots, p * LANES : (p + 1) * LANES].astype(jnp.float32)
                scratch[(g * PAIR + p) * GROUP : (g * PAIR + p + 1) * GROUP, :] = wide
        for g in range(TOGETHER):
            for s in range(GROUP):
                rows = scratch[pl.ds(g * PAIR * GROUP + s, PAIR, stride=GROUP), :]
                at = pl.multiple_of((k * step + g * GROUP + s) * PAIR, PAIR)
                out_ref[pl.ds(at, PAIR), :] = rows.astype(out_ref.dtype)
        return carry

    lax.fori_loop(0, steps, one, 0)


def relayout(chunks, col_bits, count, codes, values):
    slots = values.shape[0]
    return pl.pallas_call(
        functools.partial(relayout_kernel, chunks, col_bits),
        in_specs=[SMEM] + [pl.BlockSpec(memory_space=pltpu.HBM)] * 2,
        out_specs=(VMEM, VMEM),
        out_shape=(
            jax.ShapeDtypeStruct((slots * PAIR, LANES), values.dtype),
            jax.ShapeDtypeStruct((1, list_width(slots)), jnp.int32),
        ),
        scratch_shapes=[
            pltpu.VMEM(codes.shape, codes.dtype),
            pltpu.VMEM(values.shape, values.dtype),
            pltpu.VMEM((TOGETHER * GROUP * PAIR, LANES), jnp.float32),
            pltpu.SemaphoreType.DMA((slots // (GROUP * TOGETHER),)),
            pltpu.SemaphoreType.DMA,
        ],
        cost_estimate=pl.CostEstimate(flops=0, bytes_accessed=4 * slots * BLK * BLK, transcendentals=0),
        compiler_params=pltpu.CompilerParams(vmem_limit_bytes=48 * MIB),
        name="relayout",
    )(count, codes, values)


def table_kernel(*refs):
    parts, table = refs[:-1], refs[-1]
    kind = table.dtype if parts[0].shape[0] % 16 == 0 else jnp.float32

    def build(q, carry):
        at = pl.ds(pl.multiple_of(q * LANES, LANES), LANES)
        x = [part[:, at].astype(kind) for part in parts]
        table[at, :] = jnp.concatenate(x + x, axis=0).T.astype(table.dtype)
        return carry

    lax.fori_loop(0, table.shape[0] // LANES, build, 0, unroll=4)


def make_table(parts):
    nodes = parts[0].shape[1]
    return pl.pallas_call(
        table_kernel,
        in_specs=[VMEM] * len(parts),
        out_specs=VMEM,
        out_shape=jax.ShapeDtypeStruct((nodes, LANES), jnp.bfloat16),
        compiler_params=pltpu.CompilerParams(vmem_limit_bytes=4 * MIB),
        cost_estimate=pl.CostEstimate(flops=1, bytes_accessed=1, transcendentals=0),
        name="table",
    )(*parts)


def product_kernel(trash, group, n_tables, words_ref, blocks_ref, *refs):
    tables, outs = refs[:n_tables], refs[n_tables:]
    pending, acc = outs[-1], outs[-2]
    bounds = words_ref.shape[1] - 8 + group
    start, end = words_ref[0, bounds], words_ref[0, bounds + 1]
    low = lax.broadcasted_iota(jnp.int32, (BLK, LANES), 1) < BLK
    acc[...] = jnp.zeros_like(acc)

    def add(first):
        for u in range(UNROLL):
            i = first + u
            word = words_ref[0, jnp.maximum(i, 0)]
            place = jnp.where((i >= start) & (i < end), word & ((1 << SOURCE_AT) - 1), trash)
            rows = pl.ds(pl.multiple_of(place * PAIR, PAIR), PAIR)
            acc[rows, :] = acc[rows, :] + pending[u * PAIR : (u + 1) * PAIR, :]

    def step(g, carry):
        first = start + g * UNROLL
        products = []
        for u in range(UNROLL):
            word = words_ref[0, first + u]
            block = blocks_ref[pl.ds(pl.multiple_of((word >> SLOT_AT) * PAIR, PAIR), PAIR), :]
            source = (word >> SOURCE_AT) & ((1 << (SLOT_AT - SOURCE_AT)) - 1)
            right = []
            for table in tables:
                part = table[pl.ds(pl.multiple_of(source * BLK, BLK), BLK), :]
                zero = jnp.zeros_like(part)
                right.append(jnp.concatenate([jnp.where(low, part, zero), jnp.where(low, zero, part)], axis=0))
            products.append(jnp.dot(block, jnp.concatenate(right, axis=1), preferred_element_type=jnp.float32))
        add(first - UNROLL)
        for u in range(UNROLL):
            pending[u * PAIR : (u + 1) * PAIR, :] = products[u]
        return carry

    groups = (end - start + (UNROLL - 1)) // UNROLL
    lax.fori_loop(0, groups, step, 0)
    add(start + (groups - 1) * UNROLL)
    if len(outs) > 2:
        outs[0][...] = acc[: trash * PAIR, :].astype(outs[0].dtype)


def product(group, words, blocks, tables, trash, sent):
    lanes = LANES * len(tables)
    full = jax.ShapeDtypeStruct(((trash + 1) * PAIR, lanes), jnp.float32)
    out = jax.ShapeDtypeStruct((trash * PAIR, lanes), jnp.bfloat16) if sent else full
    sums = [pltpu.VMEM(full.shape, full.dtype)] if sent else []
    return pl.pallas_call(
        functools.partial(product_kernel, trash, group, len(tables)),
        in_specs=[SMEM, VMEM] + [VMEM] * len(tables),
        out_specs=VMEM,
        out_shape=out,
        scratch_shapes=sums + [pltpu.VMEM((UNROLL * PAIR, lanes), jnp.float32)],
        compiler_params=pltpu.CompilerParams(vmem_limit_bytes=8 * MIB),
        cost_estimate=pl.CostEstimate(flops=1, bytes_accessed=1, transcendentals=0),
        name="product_send" if sent else "product_keep",
    )(words, blocks, *tables)


def add_kernel(keep_ref, got_ref, next_ref, send_ref):
    half = next_ref.shape[0]
    next_ref[...] = keep_ref[:half, :] + got_ref[:half, :].astype(jnp.float32)
    send_ref[...] = (keep_ref[half:, :] + got_ref[half:, :].astype(jnp.float32)).astype(send_ref.dtype)


def add_halves(keep, place, got):
    rows, lanes = got.shape
    half = (rows // 2, lanes)
    block = lambda shape, place: pl.BlockSpec(shape, lambda _: place)
    return pl.pallas_call(
        add_kernel,
        grid=(1,),
        in_specs=[block(got.shape, place), block(got.shape, (0, 0))],
        out_specs=(block(half, (0, 0)),) * 2,
        out_shape=(jax.ShapeDtypeStruct(half, jnp.float32), jax.ShapeDtypeStruct(half, jnp.bfloat16)),
        compiler_params=pltpu.CompilerParams(vmem_limit_bytes=8 * MIB),
        cost_estimate=pl.CostEstimate(flops=rows * lanes, bytes_accessed=MIB, transcendentals=0),
        name="add",
    )(keep, got)


def layer_kernel(index, counts, *refs):
    sums, (weight_ref, bias_ref, out_ref, wide, left, right) = list(refs[:-6]), refs[-6:]
    r = lax.axis_index("row")
    wide[...] = weight_ref[...].astype(jnp.float32)
    size = wide.shape[0] // (2 * len(index[0]))
    halves = []
    for pieces in index:
        rows = [wide[pl.ds(pl.multiple_of((r ^ i) * size, size), size), :] for i in pieces]
        halves.append(jnp.concatenate(rows, axis=0).astype(jnp.bfloat16))
    zero = jnp.zeros_like(halves[0])
    even = jnp.concatenate([halves[0], zero, halves[1], zero], axis=0)
    odd = jnp.concatenate([zero, halves[0], zero, halves[1]], axis=0)
    base = 0
    for count in counts:
        pairs = [(sums.pop(0), sums.pop(0)) for _ in range(count // 2)]
        aggregated = [(keep[...] + got[...].astype(jnp.float32)).astype(jnp.bfloat16) for keep, got in pairs]
        aggregated = jnp.concatenate(aggregated, axis=1)
        rows = aggregated.shape[0]
        for h, w in enumerate((even, odd)):
            hidden = jnp.dot(aggregated, w, preferred_element_type=jnp.float32) + bias_ref[...]
            hidden = jnp.maximum(hidden, 0.0)
            left[pl.ds(base + h, rows, stride=2), :] = hidden[:, :LANES]
            right[pl.ds(base + h, rows, stride=2), :] = hidden[:, LANES:]
        base += 2 * rows
    out_ref[:, :LANES] = left[...].astype(out_ref.dtype)
    out_ref[:, LANES:] = right[...].astype(out_ref.dtype)


def layer(index, sums, weight, bias):
    rows = sum(2 * part[0].shape[0] for part in sums)
    return pl.pallas_call(
        functools.partial(layer_kernel, index, [len(part) for part in sums]),
        out_shape=jax.ShapeDtypeStruct((rows, weight.shape[1]), jnp.bfloat16),
        scratch_shapes=[pltpu.VMEM(weight.shape, jnp.float32)] + [pltpu.VMEM((rows, LANES), jnp.float32)] * 2,
        compiler_params=pltpu.CompilerParams(vmem_limit_bytes=8 * MIB),
        name="layer",
    )(*[x for part in sums for x in part], weight, bias)


def exchange(x, axis, size, bit):
    return lax.ppermute(x, axis, [(i, i ^ (1 << bit)) for i in range(size)])


def shards(n_row, n_col, features, block_codes, block_count, block_values, weight, bias):
    top, col_axis_bits = log2(n_row) - 1, list(range(log2(n_col)))
    col_blocks = features.shape[0] // BLK
    row_total = col_blocks * n_col // n_row
    per = row_total // n_col

    z_first, x_first = tuple(col_axis_bits[1:] + col_axis_bits[:1]), tuple(col_axis_bits)
    chunks = ((per // 2, x_first), (per // 4, x_first), (per // 4, z_first))
    halves = [size * n_col // 2 for size, _ in chunks]

    def spread(pieces, index):
        for bit in range(top):
            pieces = pieces + [exchange(p, "row", n_row, bit) for p in pieces]
            index = index + [i ^ (1 << bit) for i in index]
        return pieces, index

    mine = features.T
    other = exchange(mine, "row", n_row, top)
    near, near_index = spread([mine], [0])
    blocks, words = relayout(chunks, log2(col_blocks), block_count, block_codes, block_values[0])

    tables = [make_table(near)]
    first = product(0, words, blocks, tables, halves[0], True)
    other, first = lax.optimization_barrier((other, first))
    far, far_index = spread([other], [1 << top])
    tables.append(make_table(far))
    sends = [(first, product(0, words, blocks, tables[1:], halves[0], True))]
    sends += [(product(k, words, blocks, tables, halves[k], True),) for k in (1, 2)]
    gots = [[exchange(s, "col", n_col, order[0]) for s in send] for send, (_, order) in zip(sends, chunks)]
    words, gots[0][0] = lax.optimization_barrier((words, gots[0][0]))
    kept = product(len(chunks), words, blocks, tables, sum(halves), False)
    kept_at = [sum(halves[:k]) // halves[k] for k in range(len(chunks))]
    parts = [[(kept, (at, f), got) for f, got in enumerate(g)] for at, g in zip(kept_at, gots)]
    for k in range(1, len(col_axis_bits)):
        for i, (_, order) in enumerate(chunks):
            sums = [add_halves(*part) for part in parts[i]]
            parts[i] = [(total, (0, 0), exchange(send, "col", n_col, order[k])) for total, send in sums]
    sums = [[x for keep, _, got in part for x in (keep, got)] for part in parts]
    return layer((near_index, far_index), sums, weight, bias[None, :])


def solution(mesh):
    in_specs = (P("col", "row"), P("row", "col"), P("row", "col"), P("row", "col", None), P(), P())
    out_specs = P(("row", "col"), None)
    body = functools.partial(shards, mesh.shape["row"], mesh.shape["col"])
    return jax.shard_map(body, mesh=mesh, in_specs=in_specs, out_specs=out_specs, check_vma=False)
```

```python
import functools

import jax
import jax.numpy as jnp
from jax import lax
from jax.experimental import pallas as pl
from jax.experimental.pallas import tpu as pltpu
from jax.sharding import PartitionSpec as P

BLK = 64
PAIR = BLK // 2
LANES = 2 * BLK
GROUP = 16
TOGETHER = 2
UNROLL = 16
SLOT_AT, SOURCE_AT = 13, 7
MIB = 1024 * 1024
SMEM = pl.BlockSpec(memory_space=pltpu.SMEM)
VMEM = pl.BlockSpec(memory_space=pltpu.VMEM)


def log2(size):
    return size.bit_length() - 1


def list_width(slots):
    return -(-(slots + 2 * UNROLL + 8) // LANES) * LANES


def make_lists(chunks, col_bits, count, codes, words_ref):
    slots, width = codes.shape[1], words_ref.shape[1]
    per = sum(size for size, _ in chunks)
    row_block, col_block = codes >> col_bits, codes & ((1 << col_bits) - 1)
    owner = (row_block >> log2(per)) ^ lax.axis_index("col")
    sub = row_block & (per - 1)
    number = lax.broadcasted_iota(jnp.int32, (1, slots), 1)
    live = number < count
    group, target = jnp.full_like(codes, len(chunks) + 1), jnp.zeros_like(codes)
    first, base = 0, 0
    for c, (size, order) in enumerate(chunks):
        place = jnp.zeros_like(owner)
        for k, bit in enumerate(order):
            place = place | (((owner >> bit) & 1) << (len(order) - 1 - k))
        place = (place << log2(size)) + (sub - first)
        half = size << (len(order) - 1)
        keep = place < half
        here = live & (sub >= first) & (sub < first + size)
        target = jnp.where(here, jnp.where(keep, place + base, place - half), target)
        group = jnp.where(here, jnp.where(keep, len(chunks), c), group)
        first, base = first + size, base + half
    same = lax.broadcasted_iota(jnp.int32, (slots, slots), 0) == lax.broadcasted_iota(jnp.int32, (slots, slots), 1)
    column = lambda row: jnp.sum(jnp.where(same, row, 0.0), axis=1, keepdims=True)
    spot = lax.broadcasted_iota(jnp.int32, (slots, width), 1).astype(jnp.float32)
    lane = lax.broadcasted_iota(jnp.int32, (1, width), 1)
    key = (group * slots + number).astype(jnp.float32)
    word = ((number << SLOT_AT) | (col_block << SOURCE_AT) | target).astype(jnp.float32)
    rank = jnp.sum(jnp.where(key < column(key), 1.0, 0.0), axis=1, keepdims=True)
    words = jnp.sum(jnp.where(rank == spot, column(word), 0.0), axis=0, keepdims=True).astype(jnp.int32)
    for k in range(len(chunks) + 2):
        before = jnp.sum(jnp.where(group < k, 1.0, 0.0), axis=1, keepdims=True).astype(jnp.int32)
        words = jnp.where(lane == width - 8 + k, before, words)
    words_ref[...] = words


def relayout_kernel(chunks, col_bits, count_ref, codes_hbm, values_hbm, out_ref, words_ref, codes, held, scratch, arrived, codes_arrived):
    codes_copy = pltpu.make_async_copy(codes_hbm, codes, codes_arrived)
    codes_copy.start()
    step = GROUP * TOGETHER

    def copy(k):
        rows = pl.ds(pl.multiple_of(k * step, step), step)
        return pltpu.make_async_copy(values_hbm.at[rows], held.at[rows], arrived.at[k])

    steps = values_hbm.shape[0] // step
    for k in range(steps):
        copy(k).start()
    codes_copy.wait()
    make_lists(chunks, col_bits, count_ref[0, 0], codes[...], words_ref)

    def one(k, carry):
        copy(k).wait()
        for g in range(TOGETHER):
            slots = pl.ds(pl.multiple_of(k * step + g * GROUP, GROUP), GROUP)
            for p in range(PAIR):
                wide = held[slots, p * LANES : (p + 1) * LANES].astype(jnp.float32)
                scratch[(g * PAIR + p) * GROUP : (g * PAIR + p + 1) * GROUP, :] = wide
        for g in range(TOGETHER):
            for s in range(GROUP):
                rows = scratch[pl.ds(g * PAIR * GROUP + s, PAIR, stride=GROUP), :]
                at = pl.multiple_of((k * step + g * GROUP + s) * PAIR, PAIR)
                out_ref[pl.ds(at, PAIR), :] = rows.astype(out_ref.dtype)
        return carry

    lax.fori_loop(0, steps, one, 0)


def relayout(chunks, col_bits, count, codes, values):
    slots = values.shape[0]
    return pl.pallas_call(
        functools.partial(relayout_kernel, chunks, col_bits),
        in_specs=[SMEM] + [pl.BlockSpec(memory_space=pltpu.HBM)] * 2,
        out_specs=(VMEM, VMEM),
        out_shape=(
            jax.ShapeDtypeStruct((slots * PAIR, LANES), values.dtype),
            jax.ShapeDtypeStruct((1, list_width(slots)), jnp.int32),
        ),
        scratch_shapes=[
            pltpu.VMEM(codes.shape, codes.dtype),
            pltpu.VMEM(values.shape, values.dtype),
            pltpu.VMEM((TOGETHER * GROUP * PAIR, LANES), jnp.float32),
            pltpu.SemaphoreType.DMA((slots // (GROUP * TOGETHER),)),
            pltpu.SemaphoreType.DMA,
        ],
        cost_estimate=pl.CostEstimate(flops=0, bytes_accessed=4 * slots * BLK * BLK, transcendentals=0),
        compiler_params=pltpu.CompilerParams(vmem_limit_bytes=48 * MIB),
        name="relayout",
    )(count, codes, values)


def table_kernel(*refs):
    parts, table = refs[:-1], refs[-1]
    kind = table.dtype if parts[0].shape[0] % 16 == 0 else jnp.float32

    def build(q, carry):
        at = pl.ds(pl.multiple_of(q * LANES, LANES), LANES)
        x = [part[:, at].astype(kind) for part in parts]
        table[at, :] = jnp.concatenate(x + x, axis=0).T.astype(table.dtype)
        return carry

    lax.fori_loop(0, table.shape[0] // LANES, build, 0, unroll=4)


def make_table(parts):
    nodes = parts[0].shape[1]
    return pl.pallas_call(
        table_kernel,
        in_specs=[VMEM] * len(parts),
        out_specs=VMEM,
        out_shape=jax.ShapeDtypeStruct((nodes, LANES), jnp.bfloat16),
        compiler_params=pltpu.CompilerParams(vmem_limit_bytes=4 * MIB),
        cost_estimate=pl.CostEstimate(flops=1, bytes_accessed=1, transcendentals=0),
        name="table",
    )(*parts)


def product_kernel(trash, group, n_tables, words_ref, blocks_ref, *refs):
    tables, outs = refs[:n_tables], refs[n_tables:]
    pending, acc = outs[-1], outs[-2]
    bounds = words_ref.shape[1] - 8 + group
    start, end = words_ref[0, bounds], words_ref[0, bounds + 1]
    low = lax.broadcasted_iota(jnp.int32, (BLK, LANES), 1) < BLK
    acc[...] = jnp.zeros_like(acc)

    def add(first):
        for u in range(UNROLL):
            i = first + u
            word = words_ref[0, jnp.maximum(i, 0)]
            place = jnp.where((i >= start) & (i < end), word & ((1 << SOURCE_AT) - 1), trash)
            rows = pl.ds(pl.multiple_of(place * PAIR, PAIR), PAIR)
            acc[rows, :] = acc[rows, :] + pending[u * PAIR : (u + 1) * PAIR, :]

    def step(g, carry):
        first = start + g * UNROLL
        products = []
        for u in range(UNROLL):
            word = words_ref[0, first + u]
            block = blocks_ref[pl.ds(pl.multiple_of((word >> SLOT_AT) * PAIR, PAIR), PAIR), :]
            source = (word >> SOURCE_AT) & ((1 << (SLOT_AT - SOURCE_AT)) - 1)
            right = []
            for table in tables:
                part = table[pl.ds(pl.multiple_of(source * BLK, BLK), BLK), :]
                zero = jnp.zeros_like(part)
                right.append(jnp.concatenate([jnp.where(low, part, zero), jnp.where(low, zero, part)], axis=0))
            products.append(jnp.dot(block, jnp.concatenate(right, axis=1), preferred_element_type=jnp.float32))
        add(first - UNROLL)
        for u in range(UNROLL):
            pending[u * PAIR : (u + 1) * PAIR, :] = products[u]
        return carry

    groups = (end - start + (UNROLL - 1)) // UNROLL
    lax.fori_loop(0, groups, step, 0)
    add(start + (groups - 1) * UNROLL)
    if len(outs) > 2:
        outs[0][...] = acc[: trash * PAIR, :].astype(outs[0].dtype)


def product(group, words, blocks, tables, trash, sent):
    lanes = LANES * len(tables)
    full = jax.ShapeDtypeStruct(((trash + 1) * PAIR, lanes), jnp.float32)
    out = jax.ShapeDtypeStruct((trash * PAIR, lanes), jnp.bfloat16) if sent else full
    sums = [pltpu.VMEM(full.shape, full.dtype)] if sent else []
    return pl.pallas_call(
        functools.partial(product_kernel, trash, group, len(tables)),
        in_specs=[SMEM, VMEM] + [VMEM] * len(tables),
        out_specs=VMEM,
        out_shape=out,
        scratch_shapes=sums + [pltpu.VMEM((UNROLL * PAIR, lanes), jnp.float32)],
        compiler_params=pltpu.CompilerParams(vmem_limit_bytes=8 * MIB),
        cost_estimate=pl.CostEstimate(flops=1, bytes_accessed=1, transcendentals=0),
        name="product_send" if sent else "product_keep",
    )(words, blocks, *tables)


def add_kernel(keep_ref, got_ref, next_ref, send_ref):
    half = next_ref.shape[0]
    next_ref[...] = keep_ref[:half, :] + got_ref[:half, :].astype(jnp.float32)
    send_ref[...] = (keep_ref[half:, :] + got_ref[half:, :].astype(jnp.float32)).astype(send_ref.dtype)


def add_halves(keep, place, got):
    rows, lanes = got.shape
    half = (rows // 2, lanes)
    block = lambda shape, place: pl.BlockSpec(shape, lambda _: place)
    return pl.pallas_call(
        add_kernel,
        grid=(1,),
        in_specs=[block(got.shape, place), block(got.shape, (0, 0))],
        out_specs=(block(half, (0, 0)),) * 2,
        out_shape=(jax.ShapeDtypeStruct(half, jnp.float32), jax.ShapeDtypeStruct(half, jnp.bfloat16)),
        compiler_params=pltpu.CompilerParams(vmem_limit_bytes=8 * MIB),
        cost_estimate=pl.CostEstimate(flops=rows * lanes, bytes_accessed=MIB, transcendentals=0),
        name="add",
    )(keep, got)


def layer_kernel(index, counts, *refs):
    sums, (weight_ref, bias_ref, out_ref, wide, left, right) = list(refs[:-6]), refs[-6:]
    r = lax.axis_index("row")
    wide[...] = weight_ref[...].astype(jnp.float32)
    size = wide.shape[0] // (2 * len(index[0]))
    halves = []
    for pieces in index:
        rows = [wide[pl.ds(pl.multiple_of((r ^ i) * size, size), size), :] for i in pieces]
        halves.append(jnp.concatenate(rows, axis=0).astype(jnp.bfloat16))
    zero = jnp.zeros_like(halves[0])
    even = jnp.concatenate([halves[0], zero, halves[1], zero], axis=0)
    odd = jnp.concatenate([zero, halves[0], zero, halves[1]], axis=0)
    base = 0
    for count in counts:
        pairs = [(sums.pop(0), sums.pop(0)) for _ in range(count // 2)]
        aggregated = [(keep[...] + got[...].astype(jnp.float32)).astype(jnp.bfloat16) for keep, got in pairs]
        aggregated = jnp.concatenate(aggregated, axis=1)
        rows = aggregated.shape[0]
        for h, w in enumerate((even, odd)):
            hidden = jnp.dot(aggregated, w, preferred_element_type=jnp.float32) + bias_ref[...]
            hidden = jnp.maximum(hidden, 0.0)
            left[pl.ds(base + h, rows, stride=2), :] = hidden[:, :LANES]
            right[pl.ds(base + h, rows, stride=2), :] = hidden[:, LANES:]
        base += 2 * rows
    out_ref[:, :LANES] = left[...].astype(out_ref.dtype)
    out_ref[:, LANES:] = right[...].astype(out_ref.dtype)


def layer(index, sums, weight, bias):
    rows = sum(2 * part[0].shape[0] for part in sums)
    return pl.pallas_call(
        functools.partial(layer_kernel, index, [len(part) for part in sums]),
        out_shape=jax.ShapeDtypeStruct((rows, weight.shape[1]), jnp.bfloat16),
        scratch_shapes=[pltpu.VMEM(weight.shape, jnp.float32)] + [pltpu.VMEM((rows, LANES), jnp.float32)] * 2,
        compiler_params=pltpu.CompilerParams(vmem_limit_bytes=8 * MIB),
        name="layer",
    )(*[x for part in sums for x in part], weight, bias)


def exchange(x, axis, size, bit):
    return lax.ppermute(x, axis, [(i, i ^ (1 << bit)) for i in range(size)])


def shards(n_row, n_col, features, block_codes, block_count, block_values, weight, bias):
    top, col_axis_bits = log2(n_row) - 1, list(range(log2(n_col)))
    col_blocks = features.shape[0] // BLK
    row_total = col_blocks * n_col // n_row
    per = row_total // n_col

    z_first, x_first = tuple(col_axis_bits[1:] + col_axis_bits[:1]), tuple(col_axis_bits)
    chunks = ((per // 2, x_first), (per // 4, x_first), (per // 4, z_first))
    halves = [size * n_col // 2 for size, _ in chunks]

    def spread(pieces, index):
        for bit in range(top):
            pieces = pieces + [exchange(p, "row", n_row, bit) for p in pieces]
            index = index + [i ^ (1 << bit) for i in index]
        return pieces, index

    mine = features.T
    other = exchange(mine, "row", n_row, top)
    near, near_index = spread([mine], [0])
    blocks, words = relayout(chunks, log2(col_blocks), block_count, block_codes, block_values[0])

    tables = [make_table(near)]
    first = product(0, words, blocks, tables, halves[0], True)
    other, first = lax.optimization_barrier((other, first))
    far, far_index = spread([other], [1 << top])
    tables.append(make_table(far))
    sends = [(first, product(0, words, blocks, tables[1:], halves[0], True))]
    sends += [(product(k, words, blocks, tables, halves[k], True),) for k in (1, 2)]
    gots = [[exchange(s, "col", n_col, order[0]) for s in send] for send, (_, order) in zip(sends, chunks)]
    words, gots[0][0] = lax.optimization_barrier((words, gots[0][0]))
    kept = product(len(chunks), words, blocks, tables, sum(halves), False)
    kept_at = [sum(halves[:k]) // halves[k] for k in range(len(chunks))]
    parts = [[(kept, (at, f), got) for f, got in enumerate(g)] for at, g in zip(kept_at, gots)]
    for k in range(1, len(col_axis_bits)):
        for i, (_, order) in enumerate(chunks):
            sums = [add_halves(*part) for part in parts[i]]
            parts[i] = [(total, (0, 0), exchange(send, "col", n_col, order[k])) for total, send in sums]
    sums = [[x for keep, _, got in part for x in (keep, got)] for part in parts]
    return layer((near_index, far_index), sums, weight, bias[None, :])


def solution(mesh):
    in_specs = (P("col", "row"), P("row", "col"), P("row", "col"), P("row", "col", None), P(), P())
    out_specs = P(("row", "col"), None)
    body = functools.partial(shards, mesh.shape["row"], mesh.shape["col"])
    return jax.shard_map(body, mesh=mesh, in_specs=in_specs, out_specs=out_specs, check_vma=False)
```
